128 devices in a mesh: gx: 16 (over x, y), gy: 8 (over z, core).
Axes of the slice: x: 4, y: 4, z: 4, core: 2. Of those that a mesh axis runs over, the one named last changes fastest.
Arguments:
- estimate: float32 [64, 1024, 2048], P(None, 'gx', 'gy'), may hold values from 0.1 to 8
- measured: float32 [64, 1024, 2048], P('gy', None, 'gx'), may hold values from 0.1 to 14
- z_interp: float32 [64, 64], replicated, may hold values from 0 to 0.95, as said below
- r_interp: float32 [1024, 1024], replicated, may hold values from 0 to 0.95, as said below
- psf_z: float32 [32], replicated, may hold values from 0.004 to 0.25
- psf_r: float32 [32], replicated, may hold values from 0.004 to 0.25
- psf_u: float32 [32], replicated, may hold values from 0.004 to 0.25
Outputs:
- updated: float32 [64, 1024, 2048], P(None, 'gx', 'gy')
The draws below stay inside these ranges and needn't reach their ends.
Inputs may be any that keep to these rules, and one draw needn't show every extreme that they name: `z_interp`: nonzero only at [i, i], equal to 1 - o_i, and at [i, i + 1], equal to o_i (where i + 1 < 64), with every o_i between 0.05 and 0.95. `r_interp`: nonzero only at [i, i], equal to 1 - o_i, and at [i, i + 1], equal to o_i (where i + 1 < 1024), with every o_i between 0.05 and 0.95.
All inputs are finite; a program needn't handle non-finite values.
Results may differ from the reference program's by a relative error of at most 0.00005.
Values sent between devices are 32-bit elements; how exact they have to be, the bound alone decides.
No kernel may reach another device: no remote copies, remote signals or barrier semaphores. Data moves between devices by JAX's collectives and lax.ppermute only.
A program may use at most 128 MiB of HBM per device.

```python
import math
import jax
import jax.numpy as jnp
from jax import lax

Z = 64
K = 32
R = 1024
C = 2048


def interp_matrix(key, size, lowest, highest):
    offsets = lowest + (highest - lowest) * jax.random.uniform(key, (size,), jnp.float32)
    row_ids = jnp.arange(size)[:, None]
    col_ids = jnp.arange(size)[None, :]
    weights = jnp.where(col_ids == row_ids, 1.0 - offsets[:, None], 0.0)
    weights = weights + jnp.where(col_ids == row_ids + 1, offsets[:, None], 0.0)
    return weights.astype(jnp.float32)


def draw_z_interp(key, part):
    key = jax.random.fold_in(key, 11)
    return interp_matrix(key, Z, 0.2, 0.8)


def draw_r_interp(key, part):
    key = jax.random.fold_in(key, 23)
    return interp_matrix(key, R, 0.2, 0.8)


def wave(coord, period, phase):
    cycle = jnp.remainder(coord, period).astype(jnp.float32) / period.astype(jnp.float32)
    return jnp.cos(2.0 * math.pi * cycle + phase)


def smooth_field(key):
    periods = jax.random.randint(key, (4,), 12, 65)
    phases = jax.random.uniform(jax.random.fold_in(key, 1), (4,), jnp.float32, 0.0, 2.0 * math.pi)
    depth_ids = jnp.arange(Z, dtype=jnp.int32)[:, None, None]
    row_ids = jnp.arange(R, dtype=jnp.int32)[None, :, None]
    col_ids = jnp.arange(C, dtype=jnp.int32)[None, None, :]
    total = wave(depth_ids, periods[0], phases[0]) + wave(row_ids, periods[1], phases[1])
    total = total + wave(col_ids, periods[2], phases[2]) + wave(row_ids + 2 * col_ids, periods[3], phases[3])
    return total


def draw_estimate(key, part):
    common = smooth_field(key)
    key = jax.random.fold_in(key, 5)
    rough = jnp.exp(jax.random.uniform(key, (Z, R, C), jnp.float32, -0.35, 0.35))
    return (jnp.exp(0.35 * common) * rough).astype(jnp.float32)


def draw_measured(key, part):
    common = smooth_field(key)
    key = jax.random.fold_in(key, 7)
    own_part = smooth_field(jax.random.fold_in(key, 2))
    noise_key = jax.random.fold_in(key, 3)
    noise = jnp.exp(jax.random.uniform(noise_key, (Z, R, C), jnp.float32, -0.22, 0.22))
    return (1.5 * jnp.exp(0.25 * common + 0.2 * own_part) * noise).astype(jnp.float32)


def taps(key, width_lo, width_hi, height_lo, height_hi, tail_lo, tail_hi):
    width = jax.random.uniform(jax.random.fold_in(key, 1), (), jnp.float32, width_lo, width_hi)
    height = jax.random.uniform(jax.random.fold_in(key, 2), (), jnp.float32, height_lo, height_hi)
    tail = jnp.exp(jax.random.uniform(jax.random.fold_in(key, 3), (K,), jnp.float32, math.log(tail_lo), math.log(tail_hi)))
    positions = jnp.arange(K, dtype=jnp.float32) - 16.0
    return (height * jnp.exp(-0.5 * positions * positions / (width * width)) + tail).astype(jnp.float32)


def draw_psf_z(key, part):
    key = jax.random.fold_in(key, 31)
    return taps(key, 1.5, 3.0, 0.12, 0.2, 0.006, 0.025)


def draw_psf_r(key, part):
    key = jax.random.fold_in(key, 37)
    return taps(key, 1.5, 3.0, 0.12, 0.2, 0.006, 0.025)


def draw_psf_u(key, part):
    key = jax.random.fold_in(key, 41)
    return taps(key, 1.5, 3.0, 0.12, 0.2, 0.006, 0.025)


def setup_inputs(seed: int = 0) -> dict:
    splits = jax.random.split(jax.random.key(seed), 8)
    estimate = draw_estimate(jax.random.fold_in(splits[7], 71), 0)
    measured = draw_measured(jax.random.fold_in(splits[7], 71), 0)
    z_interp = draw_z_interp(jax.random.fold_in(splits[7], 71), 0)
    r_interp = draw_r_interp(jax.random.fold_in(splits[7], 71), 0)
    psf_z = draw_psf_z(jax.random.fold_in(splits[7], 71), 0)
    psf_r = draw_psf_r(jax.random.fold_in(splits[7], 71), 0)
    psf_u = draw_psf_u(jax.random.fold_in(splits[7], 71), 0)
    return dict(estimate=estimate, measured=measured, z_interp=z_interp, r_interp=r_interp, psf_z=psf_z, psf_r=psf_r, psf_u=psf_u)


background = 0.25
HIGH = lax.Precision.HIGHEST


def band(kernel, size):
    distance = jnp.arange(size)[None, :] - jnp.arange(size)[:, None] + 16
    inside = (distance >= 0) & (distance < kernel.shape[0])
    return jnp.where(inside, kernel[jnp.clip(distance, 0, kernel.shape[0] - 1)], jnp.float32(0.0))


def blur_columns(field, kernel):
    width = field.shape[2]
    padded = jnp.pad(field, ((0, 0), (0, 0), (16, 16)))
    total = jnp.zeros_like(field)
    for k in range(kernel.shape[0]):
        total = total + kernel[k] * padded[:, :, k:k + width]
    return total


def spread_columns(field, kernel):
    width = field.shape[2]
    padded = jnp.pad(field, ((0, 0), (0, 0), (16, 16)))
    total = jnp.zeros_like(field)
    for k in range(kernel.shape[0]):
        total = total + kernel[k] * padded[:, :, 32 - k:32 - k + width]
    return total


def reference(estimate, measured, z_interp, r_interp, psf_z, psf_r, psf_u):
    depth = estimate.shape[0]
    rows = estimate.shape[1]
    blur_z = band(psf_z, depth)
    blur_r = band(psf_r, rows)
    field = jnp.einsum('yz,zrc->yrc', z_interp, estimate, precision=HIGH)
    field = jnp.einsum('sr,yrc->ysc', r_interp, field, precision=HIGH)
    field = jnp.einsum('yz,zrc->yrc', blur_z, field, precision=HIGH)
    field = jnp.einsum('sr,yrc->ysc', blur_r, field, precision=HIGH)
    blurred = blur_columns(field, psf_u)
    ratio = measured / (blurred + background)
    back = spread_columns(ratio, psf_u)
    back = jnp.einsum('sr,ysc->yrc', blur_r, back, precision=HIGH)
    back = jnp.einsum('yz,yrc->zrc', blur_z, back, precision=HIGH)
    back = jnp.einsum('sr,ysc->yrc', r_interp, back, precision=HIGH)
    back = jnp.einsum('yz,yrc->zrc', z_interp, back, precision=HIGH)
    return estimate * back
```

```python
import functools

import jax
import jax.numpy as jnp
from jax import lax
from jax.experimental import pallas as pl
from jax.experimental.pallas import tpu as pltpu
from jax.sharding import PartitionSpec as P

background = 0.25
HIGH = lax.Precision.HIGHEST
F32 = jnp.float32
BF = jnp.bfloat16
AXES = ("gx", "gy")
MIB = 1024 * 1024


def split(x):
    hi = x.astype(BF)
    return hi, (x - hi.astype(F32)).astype(BF)


def split_table(x):
    hi = lax.reduce_precision(x, 8, 7)
    return hi.astype(BF), (x - hi).astype(BF)


def dot(a, b):
    return jnp.dot(a, b, preferred_element_type=F32)


def dot3(ah, al, bh, bl):
    return dot(ah, bh) + dot(ah, bl) + dot(al, bh)


def taps(kernel, distance):
    total = jnp.zeros(distance.shape, F32)
    for k in range(kernel.shape[0]):
        total = total + jnp.where(distance == k, kernel[k], 0.0)
    return total


def grid_of(rows, cols):
    i = lax.broadcasted_iota(jnp.int32, (rows, cols), 0)
    j = lax.broadcasted_iota(jnp.int32, (rows, cols), 1)
    return i, j


def shift_perm(axis_of, d):
    if axis_of == "gx":
        return [(i * 8 + j, (i + d) * 8 + j) for i in range(16) for j in range(8) if 0 <= i + d < 16]
    return [(i * 8 + j, i * 8 + j + d) for i in range(16) for j in range(8) if 0 <= j + d < 8]


def position(x, y, z, c):
    return ((x % 4) * 4 + y % 4) * 8 + (z % 4) * 2 + c % 2


def piece_perm(k):
    k1, k2 = k // 4, k % 4
    pairs = []
    for x in range(4):
        for y in range(4):
            for z in range(4):
                for c in range(2):
                    pairs.append((position(x, y, z, c), position(x + z + 2 * c + k1, y + 2 * c + k2, x, y // 2)))
    return pairs


def row_kernel(ah_ref, al_ref, up_ref, own_ref, down_ref, out_ref):
    ah, al = ah_ref[...], al_ref[...]
    wide = jnp.concatenate([ah, ah], axis=1)
    for z in range(out_ref.shape[0]):
        x = jnp.concatenate([up_ref[z], own_ref[z], down_ref[z]], axis=0)
        xh, xl = split(x)
        out_ref[z] = dot(wide, jnp.concatenate([xh, xl], axis=0)) + dot(al, xh)


def row_mix(table, up, own, down):
    ah, al = split_table(table)
    depth, rows, cols = own.shape
    step = 8
    block = lambda r: pl.BlockSpec((step, r, cols), lambda i: (i, 0, 0))
    whole = pl.BlockSpec(ah.shape, lambda i: (0, 0))
    return pl.pallas_call(
        row_kernel,
        grid=(depth // step,),
        in_specs=[whole, whole, block(16), block(rows), block(16)],
        out_specs=block(rows),
        out_shape=jax.ShapeDtypeStruct(own.shape, F32),
        compiler_params=pltpu.CompilerParams(vmem_limit_bytes=32 * MIB),
    )(ah, al, up, own, down)


def column_part(x, left, right, u, ul, ur):
    rows, depth = x.shape[1], x.shape[0]
    xh, xl = split(x.reshape(depth * rows, x.shape[2]))
    total = dot3(xh, xl, u[0], u[1])
    for edge, table in ((left, ul), (right, ur)):
        eh, el = split(edge.reshape(depth * rows, 16))
        total = total + dot3(eh, el, table[0], table[1])
    return total


def column_depth_kernel(uh_ref, ul_ref, eh_ref, el_ref, kh_ref, kl_ref, left_ref, right_ref, x_ref, out_ref):
    u = (uh_ref[...], ul_ref[...])
    lt = (eh_ref[:16], el_ref[:16])
    rt = (eh_ref[16:], el_ref[16:])
    y = column_part(x_ref[...], left_ref[...], right_ref[...], u, lt, rt)
    yh, yl = split(y)
    out_ref[...] = dot3(kh_ref[...], kl_ref[...], yh, yl).reshape(out_ref.shape)


def column_kernel(uh_ref, ul_ref, eh_ref, el_ref, left_ref, right_ref, x_ref, out_ref):
    u = (uh_ref[...], ul_ref[...])
    lt = (eh_ref[:16], el_ref[:16])
    rt = (eh_ref[16:], el_ref[16:])
    out_ref[...] = column_part(x_ref[...], left_ref[...], right_ref[...], u, lt, rt).reshape(out_ref.shape)


def column_mix(main, edges, depth_table, left, right, x):
    depth, rows, cols = x.shape
    tables = [*split_table(main), *split_table(edges)]
    body = column_kernel
    if depth_table is not None:
        tables += [*split_table(depth_table)]
        body = column_depth_kernel
    block = lambda c: pl.BlockSpec((depth, 8, c), lambda i: (0, i, 0))
    whole = lambda t: pl.BlockSpec(t.shape, lambda i: (0, 0))
    return pl.pallas_call(
        body,
        grid=(rows // 8,),
        in_specs=[whole(t) for t in tables] + [block(16), block(16), block(cols)],
        out_specs=block(cols),
        out_shape=jax.ShapeDtypeStruct(x.shape, F32),
        compiler_params=pltpu.CompilerParams(vmem_limit_bytes=32 * MIB),
    )(*tables, left, right, x)


def ratio_kernel(place_ref, blur_ref, *refs):
    pieces, out_ref = refs[:-1], refs[-1]
    for k, piece in enumerate(pieces):
        planes = pl.ds(pl.multiple_of(place_ref[k, 0] * 8, 8), 8)
        cols = pl.ds(pl.multiple_of(place_ref[k, 1] * 128, 128), 128)
        out_ref[planes, :, cols] = piece[...] / (blur_ref[planes, :, cols] + background)


def ratio_of(place, blurred, pieces):
    vmem = pl.BlockSpec(memory_space=pltpu.VMEM)
    return pl.pallas_call(
        ratio_kernel,
        in_specs=[pl.BlockSpec(memory_space=pltpu.SMEM), vmem] + [vmem] * len(pieces),
        out_specs=vmem,
        out_shape=jax.ShapeDtypeStruct(blurred.shape, F32),
        compiler_params=pltpu.CompilerParams(vmem_limit_bytes=48 * MIB),
    )(place, blurred, *pieces)


def depth_update_kernel(kh_ref, kl_ref, est_ref, x_ref, out_ref):
    xh, xl = split(x_ref[...].reshape(-1, x_ref.shape[2]))
    back = dot3(kh_ref[...], kl_ref[...], xh, xl)
    out_ref[...] = est_ref[...] * back.reshape(out_ref.shape)


def depth_update(table, est, x):
    depth, rows, cols = x.shape
    kh, kl = split_table(table)
    block = pl.BlockSpec((depth, 8, cols), lambda i: (0, i, 0))
    whole = pl.BlockSpec(kh.shape, lambda i: (0, 0))
    return pl.pallas_call(
        depth_update_kernel,
        grid=(rows // 8,),
        in_specs=[whole, whole, block, block],
        out_specs=block,
        out_shape=jax.ShapeDtypeStruct(x.shape, F32),
        compiler_params=pltpu.CompilerParams(vmem_limit_bytes=32 * MIB),
    )(kh, kl, est, x)


def column_edges(x):
    width = x.shape[2]
    send = lambda part, d: jnp.transpose(
        lax.ppermute(jnp.transpose(part, (0, 2, 1)), AXES, shift_perm("gy", d)), (0, 2, 1)
    )
    return send(x[:, :, width - 16 :], 1), send(x[:, :, :16], -1)


def row_edges(x):
    rows = x.shape[1]
    return (
        lax.ppermute(x[:, rows - 16 :], AXES, shift_perm("gx", 1)),
        lax.ppermute(x[:, :16], AXES, shift_perm("gx", -1)),
    )


def shards(estimate, measured, z_interp, r_interp, psf_z, psf_r, psf_u):
    depth, rows, width = estimate.shape
    gx, gy = lax.axis_index("gx"), lax.axis_index("gy")
    x, y, z, c = gx // 4, gx % 4, gy // 2, gy % 2

    up, down = row_edges(estimate)
    pieces, place = [], []
    for k in range(16):
        k1, k2 = k // 4, k % 4
        target = ((x + z + 2 * c + k1) % 4) * 4 + (y + 2 * c + k2) % 4
        part = lax.dynamic_slice(measured, (0, target * rows, 0), (8, rows, 128))
        pieces.append(lax.ppermute(part, AXES, piece_perm(k)))
        q = (y - 2 * c - k2) % 4
        half, core = q % 2, q // 2
        place.append(jnp.stack([((x - z - 2 * core - k1) % 4) * 2 + core, half]))
    place = jnp.stack(place).astype(jnp.int32)

    i, j = grid_of(depth, depth)
    mix_z = jnp.dot(taps(psf_z, j - i + 16), z_interp, precision=HIGH)
    eye = jnp.eye(8, dtype=F32)
    total = r_interp.shape[0]
    first = jnp.clip(gx * rows - 64, 0, total - 192)
    band = lax.dynamic_slice(r_interp, (first, 0), (192, total))
    i, j = grid_of(192, total)
    i = i + first
    main = jnp.sum(jnp.where(i == j, band, 0.0), axis=0)
    upper = jnp.sum(jnp.where(i + 1 == j, band, 0.0), axis=0)
    window = lambda v: lax.dynamic_slice(jnp.pad(v, (16, 16)), (gx * rows,), (rows + 32,))
    main, upper = window(main), window(upper)
    i, j = grid_of(rows, rows + 32)
    rows_out = taps(psf_r, j - i) * main[None] + taps(psf_r, j - 1 - i) * upper[None]
    rows_back = taps(psf_r, i - j + 32) * main[16 : 16 + rows, None]
    rows_back = rows_back + taps(psf_r, i - j + 31) * upper[16 : 16 + rows, None]
    i, j = grid_of(width + 32, width)
    out_u = taps(psf_u, i - j)
    back_u = taps(psf_u, j - i + 32)
    edges_of = lambda t: jnp.concatenate([t[:16], t[width + 16 :]], axis=0)

    mixed = row_mix(rows_out, up, estimate, down)
    left, right = column_edges(mixed)
    blurred = column_mix(out_u[16 : 16 + width], edges_of(out_u), jnp.kron(mix_z, eye), left, right, mixed)
    ratio = ratio_of(place, blurred, pieces)
    left, right = column_edges(ratio)
    spread = column_mix(back_u[16 : 16 + width], edges_of(back_u), None, left, right, ratio)
    up, down = row_edges(spread)
    spread = row_mix(rows_back, up, spread, down)
    return depth_update(jnp.kron(mix_z.T, eye), estimate, spread)


def solution(mesh):
    in_specs = (P(None, "gx", "gy"), P("gy", None, "gx"), P(), P(), P(), P(), P())
    out_specs = P(None, "gx", "gy")
    return jax.shard_map(shards, mesh=mesh, in_specs=in_specs, out_specs=out_specs, check_vma=False)
```

```python
import functools

import jax
import jax.numpy as jnp
from jax import lax
from jax.experimental import pallas as pl
from jax.experimental.pallas import tpu as pltpu
from jax.sharding import PartitionSpec as P

background = 0.25
HIGH = lax.Precision.HIGHEST
F32 = jnp.float32
BF = jnp.bfloat16
AXES = ("gx", "gy")
MIB = 1024 * 1024


def split(x):
    hi = x.astype(BF)
    return hi, (x - hi.astype(F32)).astype(BF)


def dot(a, b):
    return jnp.dot(a, b, preferred_element_type=F32)


def dot3(ah, al, bh, bl):
    return dot(ah, bh) + dot(ah, bl) + dot(al, bh)


def shift_perm(axis_of, d):
    if axis_of == "gx":
        return [(i * 8 + j, (i + d) * 8 + j) for i in range(16) for j in range(8) if 0 <= i + d < 16]
    return [(i * 8 + j, i * 8 + j + d) for i in range(16) for j in range(8) if 0 <= j + d < 8]


def position(x, y, z, c):
    return ((x % 4) * 4 + y % 4) * 8 + (z % 4) * 2 + c % 2


def core_swap():
    return [(d, d ^ 1) for d in range(128)]


def target_of(x, y, z, c, k):
    k1, k2 = k // 2, k % 2
    side, half = y // 2, y % 2
    parity = c ^ (x & 1)
    return (x + z + 2 * c + k1) % 4, 2 * (half ^ k2 ^ side) + parity


def source_of(x, y, z, c, k):
    k1, k2 = k // 2, k % 2
    core = (y & 1) ^ (z & 1)
    return (x - z - 2 * core - k1) % 4, core, (y // 2) ^ k2 ^ c


def piece_perm(k):
    pairs = []
    for x in range(4):
        for y in range(4):
            for z in range(4):
                for c in range(2):
                    tx, ty = target_of(x, y, z, c, k)
                    pairs.append((position(x, y, z, c), position(tx, ty, x, y // 2)))
    return pairs


def table_kernel(pz_ref, pr_ref, pu_ref, zi_ref, main_ref, upper_ref, mcol_ref, ucol_ref, *outs):
    (ro_h, ro_l, rb_h, rb_l, uo_h, uo_l, uoe_h, uoe_l, ub_h, ub_l, ube_h, ube_l, kz_h, kz_l, kt_h, kt_l) = outs

    def grid_of(rows, cols):
        return (
            lax.broadcasted_iota(jnp.int32, (rows, cols), 0),
            lax.broadcasted_iota(jnp.int32, (rows, cols), 1),
        )

    def taps(ref, distance):
        total = jnp.zeros(distance.shape, F32)
        for k in range(32):
            total = jnp.where(distance == k, ref[k], total)
        return total

    def put(value, high, low):
        h, l = split(value)
        high[...] = h
        low[...] = l

    rows, wide = ro_h.shape
    i, j = grid_of(rows, wide)
    put(taps(pr_ref, j - i) * main_ref[...] + taps(pr_ref, j - 1 - i) * upper_ref[...], ro_h, ro_l)
    put(taps(pr_ref, i - j + 32) * mcol_ref[...] + taps(pr_ref, i - j + 31) * ucol_ref[...], rb_h, rb_l)
    width = uo_h.shape[0]
    i, j = grid_of(width, width)
    put(taps(pu_ref, i + 16 - j), uo_h, uo_l)
    put(taps(pu_ref, j - i + 16), ub_h, ub_l)
    i, j = grid_of(16, width)
    for sign, high, low in ((1, uoe_h, uoe_l), (-1, ube_h, ube_l)):
        for side, start in ((0, 0), (1, width + 16)):
            distance = i + start - j if sign > 0 else j - i - start + 32
            h, l = split(taps(pu_ref, distance))
            for q in range(8):
                at = pl.ds(side * 128 + q * 16, 16)
                high[at, :] = h
                low[at, :] = l
    depth = zi_ref.shape[0]
    i, j = grid_of(depth, depth)
    mix = jnp.dot(taps(pz_ref, j - i + 16), zi_ref[...], precision=HIGH, preferred_element_type=F32)
    big = depth * 8
    i, j = grid_of(big, depth)
    spread = (i // 8 == j).astype(BF)
    i, j = grid_of(depth, big)
    gather = (j // 8 == i).astype(BF)
    i, j = grid_of(big, big)
    same = (i % 8) == (j % 8)
    for value, high, low in ((mix, kz_h, kz_l), (mix.T, kt_h, kt_l)):
        for part, ref in zip(split(value), (high, low)):
            grown = dot(dot(spread, part).astype(BF), gather)
            ref[...] = jnp.where(same, grown, 0.0).astype(BF)


def make_tables(psf_z, psf_r, psf_u, z_interp, main, upper, rows, width):
    depth = z_interp.shape[0]
    shapes = [(rows, rows + 32)] * 4 + [(width, width)] * 8 + [(depth * 8, depth * 8)] * 4
    smem = pl.BlockSpec(memory_space=pltpu.SMEM)
    vmem = pl.BlockSpec(memory_space=pltpu.VMEM)
    own = slice(16, 16 + rows)
    return pl.pallas_call(
        table_kernel,
        in_specs=[smem] * 3 + [vmem] * 5,
        out_specs=[vmem] * len(shapes),
        out_shape=[jax.ShapeDtypeStruct(s, BF) for s in shapes],
        compiler_params=pltpu.CompilerParams(vmem_limit_bytes=32 * MIB),
    )(psf_z, psf_r, psf_u, z_interp, main[None], upper[None], main[own, None], upper[own, None])


def packed(planes):
    lane = lax.broadcasted_iota(jnp.int32, planes[0][:, :128].shape, 1) // 16
    left = right = None
    for q, x in enumerate(planes):
        a, b = x[:, :128], x[:, x.shape[1] - 128 :]
        a = pltpu.roll(a, 16 * q, 1) if q else a
        b = pltpu.roll(b, (16 * q + 16) % 128, 1) if q != 7 else b
        left = a if q == 0 else jnp.where(lane == q, a, left)
        right = b if q == 0 else jnp.where(lane == q, b, right)
    return left, right


def row_product(wide, low, up, own, down):
    xh, xl = split(jnp.concatenate([up, own, down], axis=0))
    return dot(wide, jnp.concatenate([xh, xl], axis=0)) + dot(low, xh)


def row_kernel(ah_ref, al_ref, up_ref, own_ref, down_ref, out_ref, left_ref, right_ref):
    ah, al = ah_ref[...], al_ref[...]
    wide = jnp.concatenate([ah, ah], axis=1)
    planes = []
    for z in range(8):
        planes.append(row_product(wide, al, up_ref[z], own_ref[z], down_ref[z]))
        out_ref[z] = planes[-1]
    left_ref[0], right_ref[0] = packed(planes)


def row_mix(table, up, own, down):
    depth, rows, cols = own.shape
    block = lambda r: pl.BlockSpec((8, r, cols), lambda i: (i, 0, 0))
    edge = pl.BlockSpec((1, rows, 128), lambda i: (i, 0, 0))
    whole = pl.BlockSpec(table[0].shape, lambda i: (0, 0))
    edge_shape = jax.ShapeDtypeStruct((depth // 8, rows, 128), F32)
    return pl.pallas_call(
        row_kernel,
        grid=(depth // 8,),
        in_specs=[whole, whole, block(16), block(rows), block(16)],
        out_specs=[block(rows), edge, edge],
        out_shape=[jax.ShapeDtypeStruct(own.shape, F32), edge_shape, edge_shape],
        compiler_params=pltpu.CompilerParams(vmem_limit_bytes=32 * MIB),
    )(*table, up, own, down)


def column_part(x, left, right, main, edges):
    depth, rows, cols = x.shape
    xh, xl = split(x.reshape(depth * rows, cols))
    total = dot3(xh, xl, main[0], main[1])
    both = jnp.concatenate([left, right], axis=2)
    lane = (lax.broadcasted_iota(jnp.int32, (8, rows, 256), 2) % 128) // 16
    spaced = jnp.stack([jnp.where(lane == q, both, 0.0) for q in range(8)], axis=1)
    eh, el = split(spaced.reshape(depth * rows, 256))
    return total + dot3(eh, el, edges[0], edges[1])


def column_depth_kernel(uh_ref, ul_ref, eh_ref, el_ref, kh_ref, kl_ref, left_ref, right_ref, x_ref, out_ref):
    tables = ((uh_ref[...], ul_ref[...]), (eh_ref[...], el_ref[...]))
    yh, yl = split(column_part(x_ref[...], left_ref[...], right_ref[...], *tables))
    out_ref[...] = dot3(kh_ref[...], kl_ref[...], yh, yl).reshape(out_ref.shape)


def column_kernel(uh_ref, ul_ref, eh_ref, el_ref, left_ref, right_ref, x_ref, out_ref):
    tables = ((uh_ref[...], ul_ref[...]), (eh_ref[...], el_ref[...]))
    out_ref[...] = column_part(x_ref[...], left_ref[...], right_ref[...], *tables).reshape(out_ref.shape)


def column_mix(body, tables, left, right, x):
    depth, rows, cols = x.shape
    block = lambda d, c: pl.BlockSpec((d, 8, c), lambda i: (0, i, 0))
    whole = lambda t: pl.BlockSpec(t.shape, lambda i: (0, 0))
    return pl.pallas_call(
        body,
        grid=(rows // 8,),
        in_specs=[whole(t) for t in tables] + [block(depth // 8, 128), block(depth // 8, 128), block(depth, cols)],
        out_specs=block(depth, cols),
        out_shape=jax.ShapeDtypeStruct(x.shape, F32),
        compiler_params=pltpu.CompilerParams(vmem_limit_bytes=32 * MIB),
    )(*tables, left, right, x)


def ratio_kernel(place_ref, blur_ref, *refs):
    pieces, (out_ref, left_ref, right_ref) = refs[:-3], refs[-3:]
    for k, piece in enumerate(pieces):
        cols = pl.ds(pl.multiple_of(place_ref[k, 2] * 128, 128), 128)
        for part in range(2):
            planes = pl.ds(pl.multiple_of(place_ref[k, part] * 8, 8), 8)
            out_ref[planes, :, cols] = piece[part] / (blur_ref[planes, :, cols] + background)
    for g in range(left_ref.shape[0]):
        left_ref[g], right_ref[g] = packed([out_ref[8 * g + q] for q in range(8)])


def ratio_of(place, blurred, pieces):
    depth, rows, cols = blurred.shape
    vmem = pl.BlockSpec(memory_space=pltpu.VMEM)
    edge_shape = jax.ShapeDtypeStruct((depth // 8, rows, 128), F32)
    return pl.pallas_call(
        ratio_kernel,
        in_specs=[pl.BlockSpec(memory_space=pltpu.SMEM), vmem] + [vmem] * len(pieces),
        out_specs=[vmem] * 3,
        out_shape=[jax.ShapeDtypeStruct(blurred.shape, F32), edge_shape, edge_shape],
        compiler_params=pltpu.CompilerParams(vmem_limit_bytes=48 * MIB),
    )(place, blurred, *pieces)


def final_kernel(ah_ref, al_ref, kh_ref, kl_ref, up_ref, own_ref, down_ref, est_ref, out_ref, mixed):
    step = pl.program_id(0)
    half = pl.num_programs(0) // 2

    @pl.when(step < half)
    def _():
        ah, al = ah_ref[...], al_ref[...]
        wide = jnp.concatenate([ah, ah], axis=1)
        first = pl.multiple_of(step * 8, 8)
        for z in range(8):
            mixed[first + z] = row_product(wide, al, up_ref[z], own_ref[z], down_ref[z])

    @pl.when(step >= half)
    def _():
        rows = pl.ds(pl.multiple_of((step - half) * 8, 8), 8)
        xh, xl = split(mixed[:, rows, :].reshape(-1, mixed.shape[2]))
        back = dot3(kh_ref[...], kl_ref[...], xh, xl)
        out_ref[...] = est_ref[...] * back.reshape(out_ref.shape)


def final_update(row_table, depth_table, up, own, down, est):
    depth, rows, cols = own.shape
    half = depth // 8
    block = lambda r: pl.BlockSpec((8, r, cols), lambda i: (jnp.minimum(i, half - 1), 0, 0))
    tile = pl.BlockSpec((depth, 8, cols), lambda i: (0, jnp.maximum(i - half, 0), 0))
    whole = lambda t: pl.BlockSpec(t.shape, lambda i: (0, 0))
    return pl.pallas_call(
        final_kernel,
        grid=(half + rows // 8,),
        in_specs=[whole(t) for t in (*row_table, *depth_table)] + [block(16), block(rows), block(16), tile],
        out_specs=tile,
        out_shape=jax.ShapeDtypeStruct(own.shape, F32),
        scratch_shapes=[pltpu.VMEM(own.shape, F32)],
        compiler_params=pltpu.CompilerParams(vmem_limit_bytes=40 * MIB),
    )(*row_table, *depth_table, up, own, down, est)


def column_edges(left, right):
    return lax.ppermute(right, AXES, shift_perm("gy", 1)), lax.ppermute(left, AXES, shift_perm("gy", -1))


def row_edges(x):
    rows = x.shape[1]
    return (
        lax.ppermute(x[:, rows - 16 :], AXES, shift_perm("gx", 1)),
        lax.ppermute(x[:, :16], AXES, shift_perm("gx", -1)),
    )


def shards(estimate, measured, z_interp, r_interp, psf_z, psf_r, psf_u):
    depth, rows, width = estimate.shape
    gx, gy = lax.axis_index("gx"), lax.axis_index("gy")
    x, y, z, c = gx // 4, gx % 4, gy // 2, gy % 2

    up, down = row_edges(estimate)
    blocks = measured.reshape(8, 8, 2, rows, 128)
    parity = c ^ (x & 1)
    take = lambda side: lax.dynamic_index_in_dim(blocks, side, axis=2, keepdims=False)
    kept, swapped = take(parity), lax.ppermute(take(1 - parity), AXES, core_swap())
    pieces, place = [], []
    for k in range(8):
        tx, ty = target_of(x, y, z, c, k)
        slot = tx * 2 + ty // 2
        part = jnp.stack([lax.dynamic_index_in_dim(p, slot, axis=1, keepdims=False) for p in (kept, swapped)])
        pieces.append(lax.ppermute(part, AXES, piece_perm(k)))
        pair, core, half = source_of(x, y, z, c, k)
        place.append(jnp.stack([pair * 2 + core, pair * 2 + 1 - core, half]))
    place = jnp.stack(place).astype(jnp.int32)

    total = r_interp.shape[0]
    first = jnp.clip(gx * rows - 64, 0, total - 192)
    band = lax.dynamic_slice(r_interp, (first, 0), (192, total))
    i = lax.broadcasted_iota(jnp.int32, (192, total), 0) + first
    j = lax.broadcasted_iota(jnp.int32, (192, total), 1)
    main = jnp.sum(jnp.where(i == j, band, 0.0), axis=0)
    upper = jnp.sum(jnp.where(i + 1 == j, band, 0.0), axis=0)
    window = lambda v: lax.dynamic_slice(jnp.pad(v, (16, 16)), (gx * rows,), (rows + 32,))
    tables = make_tables(psf_z, psf_r, psf_u, z_interp, window(main), window(upper), rows, width)
    rows_out, rows_back, cols_out, cols_back = tables[:2], tables[2:4], tables[4:8], tables[8:12]
    depth_out, depth_back = tables[12:14], tables[14:16]

    mixed, left, right = row_mix(rows_out, up, estimate, down)
    left, right = column_edges(left, right)
    blurred = column_mix(column_depth_kernel, (*cols_out, *depth_out), left, right, mixed)
    ratio, left, right = ratio_of(place, blurred, pieces)
    left, right = column_edges(left, right)
    spread = column_mix(column_kernel, cols_back, left, right, ratio)
    up, down = row_edges(spread)
    return final_update(rows_back, depth_back, up, spread, down, estimate)


def solution(mesh):
    in_specs = (P(None, "gx", "gy"), P("gy", None, "gx"), P(), P(), P(), P(), P())
    out_specs = P(None, "gx", "gy")
    return jax.shard_map(shards, mesh=mesh, in_specs=in_specs, out_specs=out_specs, check_vma=False)
```

```python
import functools

import jax
import jax.numpy as jnp
from jax import lax
from jax.experimental import pallas as pl
from jax.experimental.pallas import tpu as pltpu
from jax.sharding import PartitionSpec as P

background = 0.25
HIGH = lax.Precision.HIGHEST
F32 = jnp.float32
BF = jnp.bfloat16
AXES = ("gx", "gy")
MIB = 1024 * 1024


def split(x):
    hi = x.astype(BF)
    return hi, (x - hi.astype(F32)).astype(BF)


def dot(a, b):
    return jnp.dot(a, b, preferred_element_type=F32)


def thrice(a, b):
    (ah, al), (bh, bl) = a, b
    return dot(jnp.concatenate([ah, ah, al], axis=1), jnp.concatenate([bh, bl, bh], axis=0))


def shift_perm(axis_of, d):
    if axis_of == "gx":
        return [(i * 8 + j, (i + d) * 8 + j) for i in range(16) for j in range(8) if 0 <= i + d < 16]
    return [(i * 8 + j, i * 8 + j + d) for i in range(16) for j in range(8) if 0 <= j + d < 8]


def position(x, y, z, c):
    return ((x % 4) * 4 + y % 4) * 8 + (z % 4) * 2 + c % 2


def core_swap():
    return [(d, d ^ 1) for d in range(128)]


def target_of(x, y, z, c, k):
    k1, k2 = k // 2, k % 2
    side, half = y >> 1, y & 1
    parity = c ^ (x & 1)
    return (x + z + 2 * c + k1) & 3, 2 * (half ^ k2 ^ side) + parity


def source_of(x, y, z, c, k):
    k1, k2 = k // 2, k % 2
    core = (y & 1) ^ (z & 1)
    return (x - z - 2 * core - k1) & 3, core, (y >> 1) ^ k2 ^ c


def piece_perm(k):
    pairs = []
    for x in range(4):
        for y in range(4):
            for z in range(4):
                for c in range(2):
                    tx, ty = target_of(x, y, z, c, k)
                    pairs.append((position(x, y, z, c), position(tx, ty, x, y // 2)))
    return pairs


def table_kernel(pz_ref, pr_ref, pu_ref, zi_ref, main_ref, upper_ref, mcol_ref, ucol_ref, *outs):
    ro_ref, rb_ref, re_ref, uo_ref, uoe_ref, ub_ref, ube_ref, zo_ref, zb_ref = outs

    def grid_of(rows, cols):
        return (
            lax.broadcasted_iota(jnp.int32, (rows, cols), 0),
            lax.broadcasted_iota(jnp.int32, (rows, cols), 1),
        )

    def taps(ref, distance):
        total = jnp.zeros(distance.shape, F32)
        for k in range(32):
            total = jnp.where(distance == k, ref[k], total)
        return total

    def left_table(value):
        h, l = split(value)
        return jnp.concatenate([h, h, l], axis=1)

    def right_table(value):
        h, l = split(value)
        return jnp.concatenate([h, l, h], axis=0)

    rows = rb_ref.shape[0]
    i, j = grid_of(rows, rows + 32)
    ro_ref[...] = left_table(taps(pr_ref, j - i) * main_ref[...] + taps(pr_ref, j - 1 - i) * upper_ref[...])
    back = taps(pr_ref, i - j + 32) * mcol_ref[...] + taps(pr_ref, i - j + 31) * ucol_ref[...]
    rb_ref[...] = left_table(back[:, 16 : 16 + rows])
    re_ref[0] = left_table(back[:16, :16])
    re_ref[1] = left_table(back[rows - 16 :, rows + 16 :])

    width = uo_ref.shape[1]
    i, j = grid_of(width, width)
    uo_ref[...] = right_table(taps(pu_ref, i + 16 - j))
    ub_ref[...] = right_table(taps(pu_ref, j - i + 16))
    a, b = i % 16, j % 16
    same = i // 16 == j // 16
    left = i < 128
    uoe_ref[...] = right_table(jnp.where(same, taps(pu_ref, jnp.where(left, a - b, a - b + 32)), 0.0))
    ube_ref[...] = right_table(jnp.where(same, taps(pu_ref, jnp.where(left, b - a + 32, b - a)), 0.0))

    depth = zi_ref.shape[0]
    i, j = grid_of(depth, depth)
    mix = jnp.dot(taps(pz_ref, j - i + 16), zi_ref[...], precision=HIGH, preferred_element_type=F32)
    zo_ref[...] = left_table(mix)
    zb_ref[...] = left_table(mix.T)


def make_tables(psf_z, psf_r, psf_u, z_interp, main, upper, rows, width):
    depth = z_interp.shape[0]
    shapes = [(rows, 3 * (rows + 32)), (rows, 3 * rows), (2, 16, 48)] + [(3 * width, width)] * 4
    shapes += [(depth, 3 * depth)] * 2
    smem = pl.BlockSpec(memory_space=pltpu.SMEM)
    vmem = pl.BlockSpec(memory_space=pltpu.VMEM)
    own = slice(16, 16 + rows)
    return pl.pallas_call(
        table_kernel,
        in_specs=[smem] * 3 + [vmem] * 5,
        out_specs=[vmem] * len(shapes),
        out_shape=[jax.ShapeDtypeStruct(s, BF) for s in shapes],
        **params(32, 3),
    )(psf_z, psf_r, psf_u, z_interp, main[None], upper[None], main[own, None], upper[own, None])


def packed(planes):
    lane = lax.broadcasted_iota(jnp.int32, planes[0][:, :128].shape, 1) // 16
    left = right = None
    for q, x in enumerate(planes):
        a, b = x[:, :128], x[:, x.shape[1] - 128 :]
        a = pltpu.roll(a, 16 * q, 1) if q else a
        b = pltpu.roll(b, (16 * q + 16) % 128, 1) if q != 7 else b
        left = a if q == 0 else jnp.where(lane == q, a, left)
        right = b if q == 0 else jnp.where(lane == q, b, right)
    return left, right


def edge_sums(left, right, table):
    h, l = split(jnp.concatenate([left, right], axis=1))
    total = dot(jnp.concatenate([h, h, l], axis=1), table)
    return total[:, :128], total[:, 128:]


def unpacked(left, right, q):
    lane = lax.broadcasted_iota(jnp.int32, left.shape, 1)
    a = pltpu.roll(left, (128 - 16 * q) % 128, 1) if q else left
    b = pltpu.roll(right, 112 - 16 * q, 1) if q != 7 else right
    return jnp.concatenate([jnp.where(lane < 16, a, 0.0), jnp.where(lane >= 112, b, 0.0)], axis=1)


def across(x, table):
    h, l = split(x)
    return dot(jnp.concatenate([h, h, l], axis=1), table)


def along(table, x):
    h, l = split(x)
    return dot(table, jnp.concatenate([h, l, h], axis=0))


def row_kernel(table_ref, up_ref, own_ref, down_ref, after_ref, out_ref, left_ref, right_ref):
    table = table_ref[...]
    planes = []
    for z in range(8):
        planes.append(along(table, jnp.concatenate([up_ref[z], own_ref[z], down_ref[z]], axis=0)))
        out_ref[z] = planes[-1]
    left_ref[0], right_ref[0] = packed(planes)


def params(mib, us):
    return dict(
        compiler_params=pltpu.CompilerParams(vmem_limit_bytes=mib * MIB),
        cost_estimate=pl.CostEstimate(flops=0, transcendentals=0, bytes_accessed=us * 3_000_000),
    )


def whole(t):
    return pl.BlockSpec(t.shape, lambda i: (0,) * t.ndim)


def row_mix(table, up, own, down, after):
    depth, rows, cols = own.shape
    block = lambda r: pl.BlockSpec((8, r, cols), lambda i: (i, 0, 0))
    edge = pl.BlockSpec((1, rows, 128), lambda i: (i, 0, 0))
    edge_shape = jax.ShapeDtypeStruct((depth // 8, rows, 128), F32)
    return pl.pallas_call(
        row_kernel,
        grid=(depth // 8,),
        in_specs=[whole(table), block(16), block(rows), block(16), ANY],
        out_specs=[block(rows), edge, edge],
        out_shape=[jax.ShapeDtypeStruct(own.shape, F32), edge_shape, edge_shape],
        **params(32, 4),
    )(table, up, own, down, after)


def blur_kernel(u_ref, e_ref, m_ref, left_ref, right_ref, x_ref, out_ref):
    depth, rows, cols = x_ref.shape
    total = across(x_ref[...].reshape(depth * rows, cols), u_ref[...]).reshape(depth, rows, cols)
    groups = depth // 8
    left, right = edge_sums(
        left_ref[...].reshape(groups * rows, 128), right_ref[...].reshape(groups * rows, 128), e_ref[...]
    )
    left, right = left.reshape(groups, rows, 128), right.reshape(groups, rows, 128)
    extra = [unpacked(left[g], right[g], q) for g in range(groups) for q in range(8)]
    total = jnp.transpose(total + jnp.stack(extra), (1, 0, 2))
    table = m_ref[...]
    for r in range(rows):
        out_ref[r] = along(table, total[r])


def blur(u, e, m, left, right, x):
    depth, rows, cols = x.shape
    block = lambda d, c: pl.BlockSpec((d, 8, c), lambda i: (0, i, 0))
    return pl.pallas_call(
        blur_kernel,
        grid=(rows // 8,),
        in_specs=[whole(u), whole(e), whole(m), block(depth // 8, 128), block(depth // 8, 128), block(depth, cols)],
        out_specs=pl.BlockSpec((8, depth, cols), lambda i: (i, 0, 0)),
        out_shape=jax.ShapeDtypeStruct((rows, depth, cols), F32),
        **params(32, 8),
    )(u, e, m, left, right, x)


def ratio_kernel(place_ref, blur_ref, *refs):
    pieces, (out_ref, top_ref, bottom_ref, left_ref, right_ref) = refs[:-5], refs[-5:]
    rows = out_ref.shape[0]
    for k, piece in enumerate(pieces):
        pair, core, half = source_of(*(place_ref[a] for a in range(4)), k)
        cols = pl.ds(pl.multiple_of(half * 128, 128), 128)
        for part in range(2):
            planes = pl.ds(pl.multiple_of((pair * 2 + (core ^ part)) * 8, 8), 8)
            seen = jnp.transpose(piece[part], (1, 0, 2))
            out_ref[:, planes, cols] = seen / (blur_ref[:, planes, cols] + background)
    top_ref[...] = out_ref[:16]
    bottom_ref[...] = out_ref[rows - 16 :]
    for g in range(left_ref.shape[0]):
        left_ref[g], right_ref[g] = packed([out_ref[8 * g + q] for q in range(8)])


def ratio_of(place, blurred, pieces):
    rows, depth, cols = blurred.shape
    vmem = pl.BlockSpec(memory_space=pltpu.VMEM)
    shapes = [blurred.shape] + [(16, depth, cols)] * 2 + [(rows // 8, depth, 128)] * 2
    return pl.pallas_call(
        ratio_kernel,
        in_specs=[pl.BlockSpec(memory_space=pltpu.SMEM), vmem] + [vmem] * len(pieces),
        out_specs=[vmem] * 5,
        out_shape=[jax.ShapeDtypeStruct(s, F32) for s in shapes],
        **params(48, 7),
    )(place, blurred, *pieces)


def spread_tile(ratio, left, right, u, e, m):
    rows, depth, cols = ratio.shape
    total = across(ratio.reshape(rows * depth, cols), u).reshape(rows, depth, cols)
    left, right = edge_sums(left, right, e)
    planes = [along(m, total[q] + unpacked(left, right, q)) for q in range(rows)]
    return jnp.transpose(jnp.stack(planes), (1, 0, 2))


def own_kernel(u_ref, e_ref, m_ref, a_ref, left_ref, right_ref, x_ref, est_ref, out_ref, kept):
    step = pl.program_id(0)
    half = pl.num_programs(0) // 2

    @pl.when(step < half)
    def _():
        rows = pl.ds(pl.multiple_of(step * 8, 8), 8)
        kept[:, rows, :] = spread_tile(x_ref[...], left_ref[0], right_ref[0], u_ref[...], e_ref[...], m_ref[...])

    @pl.when(step >= half)
    def _():
        first = pl.multiple_of((step - half) * 8, 8)
        table = a_ref[...]
        for z in range(8):
            out_ref[z] = est_ref[z] * along(table, kept[first + z])


def own_update(u, e, m, a, left, right, ratio, est):
    rows, depth, cols = ratio.shape
    half = rows // 8
    early = lambda i: (jnp.minimum(i, half - 1), 0, 0)
    late = lambda i: (jnp.maximum(i - half, 0), 0, 0)
    return pl.pallas_call(
        own_kernel,
        grid=(half + depth // 8,),
        in_specs=[whole(u), whole(e), whole(m), whole(a)]
        + [pl.BlockSpec((1, depth, 128), early)] * 2
        + [pl.BlockSpec((8, depth, cols), early), pl.BlockSpec((8, rows, cols), late)],
        out_specs=pl.BlockSpec((8, rows, cols), late),
        out_shape=jax.ShapeDtypeStruct(est.shape, F32),
        scratch_shapes=[pltpu.VMEM(est.shape, F32)],
        **params(40, 11),
    )(u, e, m, a, left, right, ratio, est)


def edge_kernel(u_ref, e_ref, m_ref, a_ref, above_ref, below_ref, up_ref, down_ref, est_ref, part_ref, out_ref, kept):
    side, step = pl.program_id(0), pl.program_id(1)
    rows = pl.ds(pl.multiple_of(step * 8, 8), 8)
    for s, x_ref, c_ref in ((0, up_ref, above_ref), (1, down_ref, below_ref)):

        @pl.when(side == s)
        def _(x_ref=x_ref, c_ref=c_ref):
            kept[:, rows, :] = spread_tile(x_ref[...], c_ref[0, 0], c_ref[1, 0], u_ref[...], e_ref[...], m_ref[...])

    @pl.when(step == 1)
    def _():
        table = a_ref[0]
        for z in range(est_ref.shape[0]):
            out_ref[z] = part_ref[z] + est_ref[z] * along(table, kept[z])


def edge_update(u, e, m, a, above, below, up, down, est, part):
    depth, rows, cols = est.shape
    step = rows // 16 - 1
    tile = pl.BlockSpec((depth, 16, cols), lambda s, i: (0, s * step, 0))
    fixed = lambda t: pl.BlockSpec(t.shape, lambda s, i: (0,) * t.ndim)
    first, second = lambda s, i: jnp.maximum(i, s), lambda s, i: i * s
    return pl.pallas_call(
        edge_kernel,
        grid=(2, 2),
        in_specs=[fixed(u), fixed(e), fixed(m), pl.BlockSpec((1, 16, 48), lambda s, i: (s, 0, 0))]
        + [pl.BlockSpec((2, 1, depth, 128), lambda s, i, at=at: (0, at(s, i), 0, 0)) for at in (first, second)]
        + [pl.BlockSpec((8, depth, cols), lambda s, i, at=at: (at(s, i), 0, 0)) for at in (first, second)]
        + [tile, tile],
        out_specs=tile,
        out_shape=jax.ShapeDtypeStruct(est.shape, F32),
        scratch_shapes=[pltpu.VMEM((depth, 16, cols), F32)],
        input_output_aliases={9: 0},
        **params(40, 6),
    )(u, e, m, a, above, below, up, down, est, part)


def send(x, axis, d):
    return lax.ppermute(x, AXES, shift_perm(axis, d))


def column_edges(left, right):
    return send(right, "gy", 1), send(left, "gy", -1)


ANY = pl.BlockSpec(memory_space=pl.ANY)
SMEM = pl.BlockSpec(memory_space=pltpu.SMEM)


def run_copies(pairs, sems):
    copies = [pltpu.make_async_copy(src, dst, sems.at[n]) for n, (src, dst) in enumerate(pairs)]
    for copy in copies:
        copy.start()
    for copy in copies:
        copy.wait()


def copy_call(body, count, shapes, inputs, us):
    return pl.pallas_call(
        body,
        in_specs=[SMEM] + [ANY] * (len(inputs) - 1),
        out_specs=[ANY] * len(shapes),
        out_shape=[jax.ShapeDtypeStruct(s, F32) for s in shapes],
        scratch_shapes=[pltpu.SemaphoreType.DMA((count,))],
        **params(56, us),
    )(*inputs)


def row_ends(place, est):
    def body(place_ref, est_ref, top_ref, bottom_ref, sems):
        rows = est_ref.shape[1]
        pairs = [(est_ref.at[:, :16], top_ref), (est_ref.at[:, rows - 16 :], bottom_ref)]
        run_copies(pairs, sems)

    depth, _, cols = est.shape
    return copy_call(body, 2, [(depth, 16, cols)] * 2, (place, est), 2)


def far_half(place, measured, rows):
    def body(place_ref, measured_ref, out_ref, sems):
        other = 1 - (place_ref[3] ^ (place_ref[0] & 1))
        run_copies([(measured_ref.at[:, :, other], out_ref)], sems)

    return copy_call(body, 1, [(8, 8, rows, 128)], (place, measured.reshape(8, 8, 2, rows, 128)), 2)[0]


def pieces_of(place, measured, far, rows, steps, after):
    def body(place_ref, measured_ref, far_ref, *refs):
        outs, sems = refs[len(after) : -1], refs[-1]
        pairs = []
        for k, out in zip(steps, outs):
            tx, ty = target_of(*(place_ref[a] for a in range(4)), k)
            pairs.append((measured_ref.at[:, tx * 4 + ty], out.at[0]))
            pairs.append((far_ref.at[:, tx * 2 + (ty >> 1)], out.at[1]))
        run_copies(pairs, sems)

    inputs = (place, measured.reshape(8, 16, rows, 128), far, *after)
    return copy_call(body, 2 * len(steps), [(2, 8, rows, 128)] * len(steps), inputs, 3)


def diagonal_windows(r_interp, gx, rows):
    total = r_interp.shape[0]
    first = jnp.clip(gx * rows - 64, 0, total - 192)
    band = lax.dynamic_slice(r_interp, (first, 0), (192, total))
    i = lax.broadcasted_iota(jnp.int32, (192, total), 0) + first
    j = lax.broadcasted_iota(jnp.int32, (192, total), 1)
    main = jnp.sum(jnp.where(i == j, band, 0.0), axis=0)
    upper = jnp.sum(jnp.where(i + 1 == j, band, 0.0), axis=0)
    window = lambda v: lax.dynamic_slice(jnp.pad(v, (16, 16)), (gx * rows,), (rows + 32,))
    return window(main), window(upper)


def forward(tables, up, estimate, down, column_edges, after):
    mixed, left, right = row_mix(tables[0], up, estimate, down, after)
    return blur(tables[3], tables[4], tables[7], *column_edges(left, right), mixed)


def backward(tables, ratio, top, bottom, left, right, estimate, column_edges, row_edges):
    rb, re, ub, ube, zb = tables[1], tables[2], tables[5], tables[6], tables[8]
    up, down = row_edges(top, bottom)
    left, right = column_edges(left, right)
    groups = left.shape[0]
    both = jnp.stack([left, right])
    above, below = row_edges(both[:, :2], both[:, groups - 2 :])
    part = own_update(ub, ube, zb, rb, left, right, ratio, estimate)
    return edge_update(ub, ube, zb, re, above, below, up, down, estimate, part)


def shards(estimate, measured, z_interp, r_interp, psf_z, psf_r, psf_u):
    depth, rows, width = estimate.shape
    gx, gy = lax.axis_index("gx"), lax.axis_index("gy")
    place = jnp.stack([gx // 4, gx % 4, gy // 2, gy % 2]).astype(jnp.int32)
    row_edges = lambda top, bottom: (send(bottom, "gx", 1), send(top, "gx", -1))
    up, down = row_edges(*row_ends(place, estimate))
    far = lax.ppermute(far_half(place, measured, rows), AXES, core_swap())
    main, upper = diagonal_windows(r_interp, gx, rows)
    tables = make_tables(psf_z, psf_r, psf_u, z_interp, main, upper, rows, width)
    ship = lambda parts, steps: [lax.ppermute(p, AXES, piece_perm(k)) for p, k in zip(parts, steps)]
    early, late = range(6), range(6, 8)
    pieces = ship(pieces_of(place, measured, far, rows, early, ()), early)
    blurred = forward(tables, up, estimate, down, column_edges, pieces[0])
    pieces += ship(pieces_of(place, measured, far, rows, late, (blurred,)), late)
    ratio, top, bottom, left, right = ratio_of(place, blurred, pieces)
    return backward(tables, ratio, top, bottom, left, right, estimate, column_edges, row_edges)


def solution(mesh):
    in_specs = (P(None, "gx", "gy"), P("gy", None, "gx"), P(), P(), P(), P(), P())
    out_specs = P(None, "gx", "gy")
    return jax.shard_map(shards, mesh=mesh, in_specs=in_specs, out_specs=out_specs, check_vma=False)
```

```python
import functools

import jax
import jax.numpy as jnp
from jax import lax
from jax.experimental import pallas as pl
from jax.experimental.pallas import tpu as pltpu
from jax.sharding import PartitionSpec as P

background = 0.25
HIGH = lax.Precision.HIGHEST
F32 = jnp.float32
BF = jnp.bfloat16
AXES = ("gx", "gy")
MIB = 1024 * 1024


def split(x):
    hi = x.astype(BF)
    return hi, (x - hi.astype(F32)).astype(BF)


def dot(a, b):
    return jnp.dot(a, b, preferred_element_type=F32)


def thrice(a, b):
    (ah, al), (bh, bl) = a, b
    return dot(jnp.concatenate([ah, ah, al], axis=1), jnp.concatenate([bh, bl, bh], axis=0))


def shift_perm(axis_of, d):
    if axis_of == "gx":
        return [(i * 8 + j, (i + d) * 8 + j) for i in range(16) for j in range(8) if 0 <= i + d < 16]
    return [(i * 8 + j, i * 8 + j + d) for i in range(16) for j in range(8) if 0 <= j + d < 8]


def position(x, y, z, c):
    return ((x % 4) * 4 + y % 4) * 8 + (z % 4) * 2 + c % 2


def core_swap():
    return [(d, d ^ 1) for d in range(128)]


def target_of(x, y, z, c, k):
    k1, k2 = k // 2, k % 2
    side, half = y >> 1, y & 1
    parity = c ^ (x & 1)
    return (x + z + 2 * c + k1) & 3, 2 * (half ^ k2 ^ side) + parity


def source_of(x, y, z, c, k):
    k1, k2 = k // 2, k % 2
    core = (y & 1) ^ (z & 1)
    return (x - z - 2 * core - k1) & 3, core, (y >> 1) ^ k2 ^ c


def piece_perm(k):
    pairs = []
    for x in range(4):
        for y in range(4):
            for z in range(4):
                for c in range(2):
                    tx, ty = target_of(x, y, z, c, k)
                    pairs.append((position(x, y, z, c), position(tx, ty, x, y // 2)))
    return pairs


def table_kernel(pz_ref, pr_ref, pu_ref, zi_ref, main_ref, upper_ref, mcol_ref, ucol_ref, *outs):
    ro_ref, rb_ref, re_ref, uo_ref, uoe_ref, ub_ref, ube_ref, zo_ref, zb_ref = outs

    def grid_of(rows, cols):
        return (
            lax.broadcasted_iota(jnp.int32, (rows, cols), 0),
            lax.broadcasted_iota(jnp.int32, (rows, cols), 1),
        )

    def taps(ref, distance):
        total = jnp.zeros(distance.shape, F32)
        for k in range(32):
            total = jnp.where(distance == k, ref[k], total)
        return total

    def left_table(value):
        h, l = split(value)
        return jnp.concatenate([h, h, l], axis=1)

    def right_table(value):
        h, l = split(value)
        return jnp.concatenate([h, l, h], axis=0)

    rows = rb_ref.shape[0]
    i, j = grid_of(rows, rows + 32)
    ro_ref[...] = left_table(taps(pr_ref, j - i) * main_ref[...] + taps(pr_ref, j - 1 - i) * upper_ref[...])
    back = taps(pr_ref, i - j + 32) * mcol_ref[...] + taps(pr_ref, i - j + 31) * ucol_ref[...]
    rb_ref[...] = left_table(back[:, 16 : 16 + rows])
    re_ref[0] = left_table(back[:16, :16])
    re_ref[1] = left_table(back[rows - 16 :, rows + 16 :])

    width = uo_ref.shape[1]
    i, j = grid_of(width, width)
    uo_ref[...] = right_table(taps(pu_ref, i + 16 - j))
    ub_ref[...] = right_table(taps(pu_ref, j - i + 16))
    a, b = i % 16, j % 16
    same = i // 16 == j // 16
    left = i < 128
    uoe_ref[...] = right_table(jnp.where(same, taps(pu_ref, jnp.where(left, a - b, a - b + 32)), 0.0))
    ube_ref[...] = right_table(jnp.where(same, taps(pu_ref, jnp.where(left, b - a + 32, b - a)), 0.0))

    depth = zi_ref.shape[0]
    i, j = grid_of(depth, depth)
    mix = jnp.dot(taps(pz_ref, j - i + 16), zi_ref[...], precision=HIGH, preferred_element_type=F32)
    zo_ref[...] = left_table(mix)
    zb_ref[...] = left_table(mix.T)


def make_tables(psf_z, psf_r, psf_u, z_interp, main, upper, rows, width):
    depth = z_interp.shape[0]
    shapes = [(rows, 3 * (rows + 32)), (rows, 3 * rows), (2, 16, 48)] + [(3 * width, width)] * 4
    shapes += [(depth, 3 * depth)] * 2
    smem = pl.BlockSpec(memory_space=pltpu.SMEM)
    vmem = pl.BlockSpec(memory_space=pltpu.VMEM)
    own = slice(16, 16 + rows)
    return pl.pallas_call(
        table_kernel,
        in_specs=[smem] * 3 + [vmem] * 5,
        out_specs=[vmem] * len(shapes),
        out_shape=[jax.ShapeDtypeStruct(s, BF) for s in shapes],
        **params(32, 3),
    )(psf_z, psf_r, psf_u, z_interp, main[None], upper[None], main[own, None], upper[own, None])


def packed(planes):
    lane = lax.broadcasted_iota(jnp.int32, planes[0][:, :128].shape, 1) // 16
    left = right = None
    for q, x in enumerate(planes):
        a, b = x[:, :128], x[:, x.shape[1] - 128 :]
        a = pltpu.roll(a, 16 * q, 1) if q else a
        b = pltpu.roll(b, (16 * q + 16) % 128, 1) if q != 7 else b
        left = a if q == 0 else jnp.where(lane == q, a, left)
        right = b if q == 0 else jnp.where(lane == q, b, right)
    return left, right


def edge_sums(left, right, table):
    h, l = split(jnp.concatenate([left, right], axis=1))
    total = dot(jnp.concatenate([h, h, l], axis=1), table)
    return total[:, :128], total[:, 128:]


def unpacked(left, right, q):
    lane = lax.broadcasted_iota(jnp.int32, left.shape, 1)
    a = pltpu.roll(left, (128 - 16 * q) % 128, 1) if q else left
    b = pltpu.roll(right, 112 - 16 * q, 1) if q != 7 else right
    return jnp.concatenate([jnp.where(lane < 16, a, 0.0), jnp.where(lane >= 112, b, 0.0)], axis=1)


def across(x, table):
    h, l = split(x)
    return dot(jnp.concatenate([h, h, l], axis=1), table)


def along(table, x):
    h, l = split(x)
    return dot(table, jnp.concatenate([h, l, h], axis=0))


def row_kernel(table_ref, up_ref, own_ref, down_ref, after_ref, out_ref, left_ref, right_ref):
    table = table_ref[...]
    planes = []
    for z in range(8):
        planes.append(along(table, jnp.concatenate([up_ref[z], own_ref[z], down_ref[z]], axis=0)))
        out_ref[z] = planes[-1]
    left_ref[0], right_ref[0] = packed(planes)


def params(mib, us):
    return dict(
        compiler_params=pltpu.CompilerParams(vmem_limit_bytes=mib * MIB),
        cost_estimate=pl.CostEstimate(flops=0, transcendentals=0, bytes_accessed=us * 3_000_000),
    )


def whole(t):
    return pl.BlockSpec(t.shape, lambda i: (0,) * t.ndim)


def row_mix(table, up, own, down, after):
    depth, rows, cols = own.shape
    block = lambda r: pl.BlockSpec((8, r, cols), lambda i: (i, 0, 0))
    edge = pl.BlockSpec((1, rows, 128), lambda i: (i, 0, 0))
    edge_shape = jax.ShapeDtypeStruct((depth // 8, rows, 128), F32)
    return pl.pallas_call(
        row_kernel,
        grid=(depth // 8,),
        in_specs=[whole(table), block(16), block(rows), block(16), ANY],
        out_specs=[block(rows), edge, edge],
        out_shape=[jax.ShapeDtypeStruct(own.shape, F32), edge_shape, edge_shape],
        **params(32, 4),
    )(table, up, own, down, after)


def blur_kernel(u_ref, e_ref, m_ref, left_ref, right_ref, x_ref, out_ref):
    depth, rows, cols = x_ref.shape
    total = across(x_ref[...].reshape(depth * rows, cols), u_ref[...]).reshape(depth, rows, cols)
    groups = depth // 8
    left, right = edge_sums(
        left_ref[...].reshape(groups * rows, 128), right_ref[...].reshape(groups * rows, 128), e_ref[...]
    )
    left, right = left.reshape(groups, rows, 128), right.reshape(groups, rows, 128)
    extra = [unpacked(left[g], right[g], q) for g in range(groups) for q in range(8)]
    total = jnp.transpose(total + jnp.stack(extra), (1, 0, 2))
    table = m_ref[...]
    for r in range(rows):
        out_ref[r] = along(table, total[r])


def blur(u, e, m, left, right, x):
    depth, rows, cols = x.shape
    block = lambda d, c: pl.BlockSpec((d, 8, c), lambda i: (0, i, 0))
    return pl.pallas_call(
        blur_kernel,
        grid=(rows // 8,),
        in_specs=[whole(u), whole(e), whole(m), block(depth // 8, 128), block(depth // 8, 128), block(depth, cols)],
        out_specs=pl.BlockSpec((8, depth, cols), lambda i: (i, 0, 0)),
        out_shape=jax.ShapeDtypeStruct((rows, depth, cols), F32),
        **params(32, 8),
    )(u, e, m, left, right, x)


def ratio_kernel(place_ref, blur_ref, *refs):
    pieces, (out_ref, left_ref, right_ref) = refs[:-3], refs[-3:]
    for k, piece in enumerate(pieces):
        pair, core, half = source_of(*(place_ref[a] for a in range(4)), k)
        cols = pl.ds(pl.multiple_of(half * 128, 128), 128)
        for part in range(2):
            planes = pl.ds(pl.multiple_of((pair * 2 + (core ^ part)) * 8, 8), 8)
            seen = jnp.transpose(piece[part], (1, 0, 2))
            out_ref[:, planes, cols] = seen / (blur_ref[:, planes, cols] + background)
    for g in range(left_ref.shape[0]):
        left_ref[g], right_ref[g] = packed([out_ref[8 * g + q] for q in range(8)])


def ratio_of(place, blurred, pieces):
    rows, depth, cols = blurred.shape
    vmem = pl.BlockSpec(memory_space=pltpu.VMEM)
    shapes = [blurred.shape] + [(rows // 8, depth, 128)] * 2
    return pl.pallas_call(
        ratio_kernel,
        in_specs=[pl.BlockSpec(memory_space=pltpu.SMEM), vmem] + [vmem] * len(pieces),
        out_specs=[vmem] * 3,
        out_shape=[jax.ShapeDtypeStruct(s, F32) for s in shapes],
        **params(48, 7),
    )(place, blurred, *pieces)


def spread_tile(ratio, left, right, u, e, m):
    rows, depth, cols = ratio.shape
    total = across(ratio.reshape(rows * depth, cols), u).reshape(rows, depth, cols)
    left, right = edge_sums(left, right, e)
    planes = [along(m, total[q] + unpacked(left, right, q)) for q in range(rows)]
    return jnp.transpose(jnp.stack(planes), (1, 0, 2))


def ends_kernel(u_ref, e_ref, m_ref, left_ref, right_ref, x_ref, top_ref, bottom_ref):
    step = pl.program_id(0)
    tile = spread_tile(x_ref[...], left_ref[0], right_ref[0], u_ref[...], e_ref[...], m_ref[...])
    for s, ref in ((0, top_ref), (2, bottom_ref)):
        for t in range(2):

            @pl.when(step == s + t)
            def _(ref=ref, t=t):
                ref[:, 8 * t : 8 * t + 8, :] = tile


def spread_ends(u, e, m, left, right, ratio):
    rows, depth, cols = ratio.shape
    at = lambda i: (jnp.where(i < 2, i, rows // 8 - 4 + i), 0, 0)
    end = pl.BlockSpec((depth, 16, cols), lambda i: (0, 0, 0))
    return pl.pallas_call(
        ends_kernel,
        grid=(4,),
        in_specs=[whole(u), whole(e), whole(m)]
        + [pl.BlockSpec((1, depth, 128), at)] * 2
        + [pl.BlockSpec((8, depth, cols), at)],
        out_specs=[end, end],
        out_shape=[jax.ShapeDtypeStruct((depth, 16, cols), F32)] * 2,
        **params(40, 4),
    )(u, e, m, left, right, ratio)


def own_kernel(u_ref, e_ref, m_ref, a_ref, left_ref, right_ref, x_ref, top_ref, bottom_ref, est_ref, out_ref, kept):
    step = pl.program_id(0)
    inner = kept.shape[1] // 8

    @pl.when(step < inner)
    def _():
        rows = pl.ds(pl.multiple_of(step * 8, 8), 8)
        kept[:, rows, :] = spread_tile(x_ref[...], left_ref[0], right_ref[0], u_ref[...], e_ref[...], m_ref[...])

    @pl.when(step >= inner)
    def _():
        first = pl.multiple_of((step - inner) * 8, 8)
        table = a_ref[...]
        for z in range(8):
            x = jnp.concatenate([top_ref[z], kept[first + z], bottom_ref[z]], axis=0)
            out_ref[z] = est_ref[z] * along(table, x)


def own_update(u, e, m, a, left, right, ratio, top, bottom, est):
    rows, depth, cols = ratio.shape
    inner = rows // 8 - 4
    early = lambda i: (jnp.minimum(i, inner - 1) + 2, 0, 0)
    late = lambda i: (jnp.maximum(i - inner, 0), 0, 0)
    return pl.pallas_call(
        own_kernel,
        grid=(inner + depth // 8,),
        in_specs=[whole(u), whole(e), whole(m), whole(a)]
        + [pl.BlockSpec((1, depth, 128), early)] * 2
        + [pl.BlockSpec((8, depth, cols), early)]
        + [pl.BlockSpec((8, 16, cols), late)] * 2
        + [pl.BlockSpec((8, rows, cols), late)],
        out_specs=pl.BlockSpec((8, rows, cols), late),
        out_shape=jax.ShapeDtypeStruct(est.shape, F32),
        scratch_shapes=[pltpu.VMEM((depth, rows - 32, cols), F32)],
        **params(40, 8),
    )(u, e, m, a, left, right, ratio, top, bottom, est)


def edge_kernel(a_ref, up_ref, down_ref, est_ref, part_ref, out_ref):
    side = pl.program_id(0)
    for s, x_ref in ((0, up_ref), (1, down_ref)):

        @pl.when(side == s)
        def _(x_ref=x_ref):
            table = a_ref[0]
            for z in range(est_ref.shape[0]):
                out_ref[z] = part_ref[z] + est_ref[z] * along(table, x_ref[z])


def edge_update(a, up, down, est, part):
    depth, rows, cols = est.shape
    step, chunk = rows // 16 - 1, 16
    last = depth // chunk - 1
    tile = pl.BlockSpec((chunk, 16, cols), lambda s, i: (i, s * step, 0))
    return pl.pallas_call(
        edge_kernel,
        grid=(2, depth // chunk),
        in_specs=[pl.BlockSpec((1, 16, 48), lambda s, i: (s, 0, 0))]
        + [pl.BlockSpec((chunk, 16, cols), lambda s, i: (i + (last - i) * s, 0, 0))]
        + [pl.BlockSpec((chunk, 16, cols), lambda s, i: (i * s, 0, 0))]
        + [tile, tile],
        out_specs=tile,
        out_shape=jax.ShapeDtypeStruct(est.shape, F32),
        input_output_aliases={4: 0},
        **params(40, 3),
    )(a, up, down, est, part)


def send(x, axis, d):
    return lax.ppermute(x, AXES, shift_perm(axis, d))


def column_edges(left, right):
    return send(right, "gy", 1), send(left, "gy", -1)


ANY = pl.BlockSpec(memory_space=pl.ANY)
SMEM = pl.BlockSpec(memory_space=pltpu.SMEM)


def run_copies(pairs, sems):
    copies = [pltpu.make_async_copy(src, dst, sems.at[n]) for n, (src, dst) in enumerate(pairs)]
    for copy in copies:
        copy.start()
    for copy in copies:
        copy.wait()


def copy_call(body, count, shapes, inputs, us):
    return pl.pallas_call(
        body,
        in_specs=[SMEM] + [ANY] * (len(inputs) - 1),
        out_specs=[pl.BlockSpec(memory_space=pltpu.VMEM)] * len(shapes),
        out_shape=[jax.ShapeDtypeStruct(s, F32) for s in shapes],
        scratch_shapes=[pltpu.SemaphoreType.DMA((count,))],
        **params(56, us),
    )(*inputs)


def row_ends(place, est):
    def body(place_ref, est_ref, top_ref, bottom_ref, sems):
        rows = est_ref.shape[1]
        pairs = [(est_ref.at[:, :16], top_ref), (est_ref.at[:, rows - 16 :], bottom_ref)]
        run_copies(pairs, sems)

    depth, _, cols = est.shape
    return copy_call(body, 2, [(depth, 16, cols)] * 2, (place, est), 2)


def far_half(place, measured, rows):
    def body(place_ref, measured_ref, out_ref, sems):
        other = 1 - (place_ref[3] ^ (place_ref[0] & 1))
        run_copies([(measured_ref.at[:, :, other], out_ref)], sems)

    return copy_call(body, 1, [(8, 8, rows, 128)], (place, measured.reshape(8, 8, 2, rows, 128)), 2)[0]


def pieces_of(place, measured, far, rows, steps, after):
    def body(place_ref, measured_ref, far_ref, *refs):
        outs, sems = refs[len(after) : -1], refs[-1]
        pairs = []
        for k, out in zip(steps, outs):
            tx, ty = target_of(*(place_ref[a] for a in range(4)), k)
            pairs.append((measured_ref.at[:, tx * 4 + ty], out.at[0]))
            pairs.append((far_ref.at[:, tx * 2 + (ty >> 1)], out.at[1]))
        run_copies(pairs, sems)

    inputs = (place, measured.reshape(8, 16, rows, 128), far, *after)
    return copy_call(body, 2 * len(steps), [(2, 8, rows, 128)] * len(steps), inputs, 3)


def diagonal_windows(r_interp, gx, rows):
    total = r_interp.shape[0]
    first = jnp.clip(gx * rows - 64, 0, total - 192)
    band = lax.dynamic_slice(r_interp, (first, 0), (192, total))
    i = lax.broadcasted_iota(jnp.int32, (192, total), 0) + first
    j = lax.broadcasted_iota(jnp.int32, (192, total), 1)
    main = jnp.sum(jnp.where(i == j, band, 0.0), axis=0)
    upper = jnp.sum(jnp.where(i + 1 == j, band, 0.0), axis=0)
    window = lambda v: lax.dynamic_slice(jnp.pad(v, (16, 16)), (gx * rows,), (rows + 32,))
    return window(main), window(upper)


def forward(tables, up, estimate, down, column_edges, after):
    mixed, left, right = row_mix(tables[0], up, estimate, down, after)
    return blur(tables[3], tables[4], tables[7], *column_edges(left, right), mixed)


def backward(tables, ratio, left, right, estimate, column_edges, row_edges):
    rb, re, ub, ube, zb = tables[1], tables[2], tables[5], tables[6], tables[8]
    left, right = column_edges(left, right)
    top, bottom = spread_ends(ub, ube, zb, left, right, ratio)
    up, down = row_edges(top, bottom)
    part = own_update(ub, ube, zb, rb, left, right, ratio, top, bottom, estimate)
    return edge_update(re, up, down, estimate, part)


def shards(estimate, measured, z_interp, r_interp, psf_z, psf_r, psf_u):
    depth, rows, width = estimate.shape
    gx, gy = lax.axis_index("gx"), lax.axis_index("gy")
    place = jnp.stack([gx // 4, gx % 4, gy // 2, gy % 2]).astype(jnp.int32)
    row_edges = lambda top, bottom: (send(bottom, "gx", 1), send(top, "gx", -1))
    up, down = row_edges(*row_ends(place, estimate))
    far = lax.ppermute(far_half(place, measured, rows), AXES, core_swap())
    main, upper = diagonal_windows(r_interp, gx, rows)
    tables = make_tables(psf_z, psf_r, psf_u, z_interp, main, upper, rows, width)
    ship = lambda parts, steps: [lax.ppermute(p, AXES, piece_perm(k)) for p, k in zip(parts, steps)]
    early, late = range(6), range(6, 8)
    pieces = ship(pieces_of(place, measured, far, rows, early, ()), early)
    blurred = forward(tables, up, estimate, down, column_edges, pieces[0])
    pieces += ship(pieces_of(place, measured, far, rows, late, (blurred,)), late)
    ratio, left, right = ratio_of(place, blurred, pieces)
    return backward(tables, ratio, left, right, estimate, column_edges, row_edges)


def solution(mesh):
    in_specs = (P(None, "gx", "gy"), P("gy", None, "gx"), P(), P(), P(), P(), P())
    out_specs = P(None, "gx", "gy")
    return jax.shard_map(shards, mesh=mesh, in_specs=in_specs, out_specs=out_specs, check_vma=False)
```

```python
import functools

import jax
import jax.numpy as jnp
from jax import lax
from jax.experimental import pallas as pl
from jax.experimental.pallas import tpu as pltpu
from jax.sharding import PartitionSpec as P

background = 0.25
HIGH = lax.Precision.HIGHEST
F32 = jnp.float32
BF = jnp.bfloat16
AXES = ("gx", "gy")
MIB = 1024 * 1024


def split(x):
    hi = x.astype(BF)
    return hi, (x - hi.astype(F32)).astype(BF)


def dot(a, b):
    return jnp.dot(a, b, preferred_element_type=F32)


def thrice(a, b):
    (ah, al), (bh, bl) = a, b
    return dot(jnp.concatenate([ah, ah, al], axis=1), jnp.concatenate([bh, bl, bh], axis=0))


def shift_perm(axis_of, d):
    if axis_of == "gx":
        return [(i * 8 + j, (i + d) * 8 + j) for i in range(16) for j in range(8) if 0 <= i + d < 16]
    return [(i * 8 + j, i * 8 + j + d) for i in range(16) for j in range(8) if 0 <= j + d < 8]


def position(x, y, z, c):
    return ((x % 4) * 4 + y % 4) * 8 + (z % 4) * 2 + c % 2


def core_swap():
    return [(d, d ^ 1) for d in range(128)]


def target_of(x, y, z, c, k):
    k1, k2 = k // 2, k % 2
    side, half = y >> 1, y & 1
    return (x + z + 2 * c + 2 * side + k1) & 3, 2 * (half ^ k2) + c


def source_of(x, y, z, c, k):
    k1, k2 = k // 2, k % 2
    core = y & 1
    return (x - z - 2 * core - 2 * c - k1) & 3, core, (y >> 1) ^ k2


def piece_perm(k):
    pairs = []
    for x in range(4):
        for y in range(4):
            for z in range(4):
                for c in range(2):
                    tx, ty = target_of(x, y, z, c, k)
                    pairs.append((position(x, y, z, c), position(tx, ty, x, y // 2)))
    return pairs


def table_kernel(pz_ref, pr_ref, pu_ref, zi_ref, main_ref, upper_ref, mcol_ref, ucol_ref, *outs):
    ro_ref, rb_ref, re_ref, uo_ref, uoe_ref, ub_ref, ube_ref, zo_ref, zb_ref = outs

    def grid_of(rows, cols):
        return (
            lax.broadcasted_iota(jnp.int32, (rows, cols), 0),
            lax.broadcasted_iota(jnp.int32, (rows, cols), 1),
        )

    def taps(ref, distance):
        total = jnp.zeros(distance.shape, F32)
        for k in range(32):
            total = jnp.where(distance == k, ref[k], total)
        return total

    def left_table(value):
        h, l = split(value)
        return jnp.concatenate([h, h, l], axis=1)

    def right_table(value):
        h, l = split(value)
        return jnp.concatenate([h, l, h], axis=0)

    rows = rb_ref.shape[0]
    i, j = grid_of(rows, rows + 32)
    ro_ref[...] = left_table(taps(pr_ref, j - i) * main_ref[...] + taps(pr_ref, j - 1 - i) * upper_ref[...])
    back = taps(pr_ref, i - j + 32) * mcol_ref[...] + taps(pr_ref, i - j + 31) * ucol_ref[...]
    rb_ref[...] = left_table(back[:, 16 : 16 + rows])
    re_ref[0] = left_table(back[:16, :16])
    re_ref[1] = left_table(back[rows - 16 :, rows + 16 :])

    width = uo_ref.shape[1]
    i, j = grid_of(width, width)
    uo_ref[...] = right_table(taps(pu_ref, i + 16 - j))
    ub_ref[...] = right_table(taps(pu_ref, j - i + 16))
    a, b = i % 16, j % 16
    same = i // 16 == j // 16
    left = i < 128
    uoe_ref[...] = right_table(jnp.where(same, taps(pu_ref, jnp.where(left, a - b, a - b + 32)), 0.0))
    ube_ref[...] = right_table(jnp.where(same, taps(pu_ref, jnp.where(left, b - a + 32, b - a)), 0.0))

    depth = zi_ref.shape[0]
    i, j = grid_of(depth, depth)
    mix = jnp.dot(taps(pz_ref, j - i + 16), zi_ref[...], precision=HIGH, preferred_element_type=F32)
    zo_ref[...] = left_table(mix)
    zb_ref[...] = left_table(mix.T)


def make_tables(psf_z, psf_r, psf_u, z_interp, main, upper, rows, width):
    depth = z_interp.shape[0]
    shapes = [(rows, 3 * (rows + 32)), (rows, 3 * rows), (2, 16, 48)] + [(3 * width, width)] * 4
    shapes += [(depth, 3 * depth)] * 2
    smem = pl.BlockSpec(memory_space=pltpu.SMEM)
    vmem = pl.BlockSpec(memory_space=pltpu.VMEM)
    own = slice(16, 16 + rows)
    return pl.pallas_call(
        table_kernel,
        in_specs=[smem] * 3 + [vmem] * 5,
        out_specs=[vmem] * len(shapes),
        out_shape=[jax.ShapeDtypeStruct(s, BF) for s in shapes],
        **params(8, 3),
    )(psf_z, psf_r, psf_u, z_interp, main[None], upper[None], main[own, None], upper[own, None])


def packed(planes):
    lane = lax.broadcasted_iota(jnp.int32, planes[0][:, :128].shape, 1) // 16
    left = right = None
    for q, x in enumerate(planes):
        a, b = x[:, :128], x[:, x.shape[1] - 128 :]
        a = pltpu.roll(a, 16 * q, 1) if q else a
        b = pltpu.roll(b, (16 * q + 16) % 128, 1) if q != 7 else b
        left = a if q == 0 else jnp.where(lane == q, a, left)
        right = b if q == 0 else jnp.where(lane == q, b, right)
    return left, right


def edge_sums(left, right, table):
    h, l = split(jnp.concatenate([left, right], axis=1))
    total = dot(jnp.concatenate([h, h, l], axis=1), table)
    return total[:, :128], total[:, 128:]


def unpacked(left, right, q):
    lane = lax.broadcasted_iota(jnp.int32, left.shape, 1)
    a = pltpu.roll(left, (128 - 16 * q) % 128, 1) if q else left
    b = pltpu.roll(right, 112 - 16 * q, 1) if q != 7 else right
    return jnp.concatenate([jnp.where(lane < 16, a, 0.0), jnp.where(lane >= 112, b, 0.0)], axis=1)


def across(x, table):
    h, l = split(x)
    return dot(jnp.concatenate([h, h, l], axis=1), table)


def along(table, x):
    h, l = split(x)
    return dot(table, jnp.concatenate([h, l, h], axis=0))


def row_kernel(table_ref, up_ref, own_ref, down_ref, *refs):
    out_ref, left_ref, right_ref = refs[-3:]
    table = table_ref[...]
    planes = []
    for z in range(8):
        planes.append(along(table, jnp.concatenate([up_ref[z], own_ref[z], down_ref[z]], axis=0)))
        out_ref[z] = planes[-1]
    left_ref[0], right_ref[0] = packed(planes)


def params(mib, us):
    return dict(
        compiler_params=pltpu.CompilerParams(vmem_limit_bytes=mib * MIB),
        cost_estimate=pl.CostEstimate(flops=0, transcendentals=0, bytes_accessed=us * 3_000_000),
    )


def whole(t):
    return pl.BlockSpec(t.shape, lambda i: (0,) * t.ndim)


def row_mix(table, up, own, down, after):
    depth, rows, cols = own.shape
    block = lambda r: pl.BlockSpec((8, r, cols), lambda i: (i, 0, 0))
    edge = pl.BlockSpec((1, rows, 128), lambda i: (i, 0, 0))
    edge_shape = jax.ShapeDtypeStruct((depth // 8, rows, 128), F32)
    return pl.pallas_call(
        row_kernel,
        grid=(depth // 8,),
        in_specs=[whole(table), block(16), block(rows), block(16)] + [ANY] * len(after),
        out_specs=[block(rows), edge, edge],
        out_shape=[jax.ShapeDtypeStruct(own.shape, F32), edge_shape, edge_shape],
        **params(10, 4),
    )(table, up, own, down, *after)


def blur_kernel(u_ref, e_ref, m_ref, left_ref, right_ref, x_ref, out_ref):
    depth, rows, cols = x_ref.shape
    total = across(x_ref[...].reshape(depth * rows, cols), u_ref[...]).reshape(depth, rows, cols)
    groups = depth // 8
    left, right = edge_sums(
        left_ref[...].reshape(groups * rows, 128), right_ref[...].reshape(groups * rows, 128), e_ref[...]
    )
    left, right = left.reshape(groups, rows, 128), right.reshape(groups, rows, 128)
    extra = [unpacked(left[g], right[g], q) for g in range(groups) for q in range(8)]
    total = jnp.transpose(total + jnp.stack(extra), (1, 0, 2))
    table = m_ref[...]
    for r in range(rows):
        out_ref[r] = along(table, total[r])


def blur(u, e, m, left, right, x):
    depth, rows, cols = x.shape
    block = lambda d, c: pl.BlockSpec((d, 8, c), lambda i: (0, i, 0))
    return pl.pallas_call(
        blur_kernel,
        grid=(rows // 8,),
        in_specs=[whole(u), whole(e), whole(m), block(depth // 8, 128), block(depth // 8, 128), block(depth, cols)],
        out_specs=pl.BlockSpec((8, depth, cols), lambda i: (i, 0, 0)),
        out_shape=jax.ShapeDtypeStruct((rows, depth, cols), F32),
        **params(14, 8),
    )(u, e, m, left, right, x)


def ratio_kernel(blur_ref, *refs):
    pieces, (out_ref, left_ref, right_ref) = refs[:-3], refs[-3:]
    for k, piece in enumerate(pieces):
        pair, core, half = source_of(*place(), k)
        cols = pl.ds(pl.multiple_of(half * 128, 128), 128)
        for part in range(2):
            planes = pl.ds(pl.multiple_of((pair * 2 + (core ^ part)) * 8, 8), 8)
            seen = jnp.transpose(piece[part], (1, 0, 2))
            out_ref[:, planes, cols] = seen / (blur_ref[:, planes, cols] + background)
    for g in range(left_ref.shape[0]):
        left_ref[g], right_ref[g] = packed([out_ref[8 * g + q] for q in range(8)])


def ratio_of(blurred, pieces):
    rows, depth, cols = blurred.shape
    vmem = pl.BlockSpec(memory_space=pltpu.VMEM)
    shapes = [blurred.shape] + [(rows // 8, depth, 128)] * 2
    return pl.pallas_call(
        ratio_kernel,
        in_specs=[vmem] * (1 + len(pieces)),
        out_specs=[vmem] * 3,
        out_shape=[jax.ShapeDtypeStruct(s, F32) for s in shapes],
        **params(20, 7),
    )(blurred, *pieces)


def spread_tile(ratio, left, right, u, e, m):
    rows, depth, cols = ratio.shape
    total = across(ratio.reshape(rows * depth, cols), u).reshape(rows, depth, cols)
    left, right = edge_sums(left, right, e)
    planes = [along(m, total[q] + unpacked(left, right, q)) for q in range(rows)]
    return jnp.transpose(jnp.stack(planes), (1, 0, 2))


def ends_kernel(u_ref, e_ref, m_ref, left_ref, right_ref, x_ref, top_ref, bottom_ref):
    step = pl.program_id(0)
    tile = spread_tile(x_ref[...], left_ref[0], right_ref[0], u_ref[...], e_ref[...], m_ref[...])
    for s, ref in ((0, top_ref), (2, bottom_ref)):
        for t in range(2):

            @pl.when(step == s + t)
            def _(ref=ref, t=t):
                ref[:, 8 * t : 8 * t + 8, :] = tile


def spread_ends(u, e, m, left, right, ratio):
    rows, depth, cols = ratio.shape
    at = lambda i: (jnp.where(i < 2, i, rows // 8 - 4 + i), 0, 0)
    end = pl.BlockSpec((depth, 16, cols), lambda i: (0, 0, 0))
    return pl.pallas_call(
        ends_kernel,
        grid=(4,),
        in_specs=[whole(u), whole(e), whole(m)]
        + [pl.BlockSpec((1, depth, 128), at)] * 2
        + [pl.BlockSpec((8, depth, cols), at)],
        out_specs=[end, end],
        out_shape=[jax.ShapeDtypeStruct((depth, 16, cols), F32)] * 2,
        **params(14, 4),
    )(u, e, m, left, right, ratio)


def own_kernel(u_ref, e_ref, m_ref, a_ref, left_ref, right_ref, x_ref, top_ref, bottom_ref, est_ref, out_ref, kept):
    step = pl.program_id(0)
    inner = kept.shape[1] // 8

    @pl.when(step < inner)
    def _():
        rows = pl.ds(pl.multiple_of(step * 8, 8), 8)
        kept[:, rows, :] = spread_tile(x_ref[...], left_ref[0], right_ref[0], u_ref[...], e_ref[...], m_ref[...])

    @pl.when(step >= inner)
    def _():
        first = pl.multiple_of((step - inner) * 8, 8)
        table = a_ref[...]
        for z in range(8):
            x = jnp.concatenate([top_ref[z], kept[first + z], bottom_ref[z]], axis=0)
            out_ref[z] = est_ref[z] * along(table, x)


def own_update(u, e, m, a, left, right, ratio, top, bottom, est):
    rows, depth, cols = ratio.shape
    inner = rows // 8 - 4
    early = lambda i: (jnp.minimum(i, inner - 1) + 2, 0, 0)
    late = lambda i: (jnp.maximum(i - inner, 0), 0, 0)
    return pl.pallas_call(
        own_kernel,
        grid=(inner + depth // 8,),
        in_specs=[whole(u), whole(e), whole(m), whole(a)]
        + [pl.BlockSpec((1, depth, 128), early)] * 2
        + [pl.BlockSpec((8, depth, cols), early)]
        + [pl.BlockSpec((8, 16, cols), late)] * 2
        + [pl.BlockSpec((8, rows, cols), late)],
        out_specs=pl.BlockSpec((8, rows, cols), late),
        out_shape=jax.ShapeDtypeStruct(est.shape, F32),
        scratch_shapes=[pltpu.VMEM((depth, rows - 32, cols), F32)],
        **params(16, 8),
    )(u, e, m, a, left, right, ratio, top, bottom, est)


def edge_kernel(a_ref, up_ref, down_ref, est_ref, part_ref, out_ref):
    side = pl.program_id(0)
    for s, x_ref in ((0, up_ref), (1, down_ref)):

        @pl.when(side == s)
        def _(x_ref=x_ref):
            table = a_ref[0]
            for z in range(est_ref.shape[0]):
                out_ref[z] = part_ref[z] + est_ref[z] * along(table, x_ref[z])


def edge_update(a, up, down, est, part):
    depth, rows, cols = est.shape
    step, chunk = rows // 16 - 1, depth
    last = depth // chunk - 1
    tile = pl.BlockSpec((chunk, 16, cols), lambda s, i: (i, s * step, 0))
    return pl.pallas_call(
        edge_kernel,
        grid=(2, depth // chunk),
        in_specs=[pl.BlockSpec((1, 16, 48), lambda s, i: (s, 0, 0))]
        + [pl.BlockSpec((chunk, 16, cols), lambda s, i: (i + (last - i) * s, 0, 0))]
        + [pl.BlockSpec((chunk, 16, cols), lambda s, i: (i * s, 0, 0))]
        + [tile, tile],
        out_specs=tile,
        out_shape=jax.ShapeDtypeStruct(est.shape, F32),
        input_output_aliases={4: 0},
        **params(20, 3),
    )(a, up, down, est, part)


def send(x, axis, d):
    return lax.ppermute(x, AXES, shift_perm(axis, d))


def column_edges(left, right):
    return send(right, "gy", 1), send(left, "gy", -1)


def place():
    gx, gy = lax.axis_index("gx"), lax.axis_index("gy")
    return gx >> 2, gx & 3, gy >> 1, gy & 1


HBM = pl.BlockSpec(memory_space=pltpu.HBM)
ANY = pl.BlockSpec(memory_space=pl.ANY)


def run_copies(pairs, sems):
    copies = [pltpu.make_async_copy(src, dst, sems.at[n]) for n, (src, dst) in enumerate(pairs)]
    for copy in copies:
        copy.start()
    for copy in copies:
        copy.wait()


def copy_call(body, count, shapes, inputs, us):
    return pl.pallas_call(
        body,
        in_specs=[HBM] * len(inputs),
        out_specs=[pl.BlockSpec(memory_space=pltpu.VMEM)] * len(shapes),
        out_shape=[jax.ShapeDtypeStruct(s, F32) for s in shapes],
        scratch_shapes=[pltpu.SemaphoreType.DMA((count,))],
        **params(16, us),
    )(*inputs)


def row_ends(est):
    def body(est_ref, top_ref, bottom_ref, sems):
        depth, rows, _ = est_ref.shape
        pairs = []
        for d in range(0, depth, 16):
            at = pl.ds(d, 16)
            pairs.append((est_ref.at[at, :16], top_ref.at[at]))
            pairs.append((est_ref.at[at, rows - 16 :], bottom_ref.at[at]))
        run_copies(pairs, sems)

    depth, _, cols = est.shape
    return copy_call(body, depth // 8, [(depth, 16, cols)] * 2, (est,), 2)


def far_half(measured, rows):
    def body(measured_ref, out_ref, sems):
        _, _, _, c = place()
        run_copies([(measured_ref.at[p, :, 1 - c], out_ref.at[p]) for p in range(8)], sems)

    return copy_call(body, 8, [(8, 8, rows, 128)], (measured.reshape(8, 8, 2, rows, 128),), 2)[0]


def pieces_of(measured, far, rows):
    def body(measured_ref, far_ref, *refs):
        outs, sems = refs[:-1], refs[-1]
        pairs = []
        for k, out in enumerate(outs):
            tx, ty = target_of(*place(), k)
            pairs.append((measured_ref.at[:, tx * 4 + ty], out.at[0]))
            pairs.append((far_ref.at[:, tx * 2 + (ty >> 1)], out.at[1]))
        run_copies(pairs, sems)

    inputs = (measured.reshape(8, 16, rows, 128), far)
    return copy_call(body, 16, [(2, 8, rows, 128)] * 8, inputs, 3)


def diagonal_windows(r_interp, gx, rows):
    total = r_interp.shape[0]
    first = jnp.clip(gx * rows - 64, 0, total - 192)
    band = lax.dynamic_slice(r_interp, (first, 0), (192, total))
    i = lax.broadcasted_iota(jnp.int32, (192, total), 0) + first
    j = lax.broadcasted_iota(jnp.int32, (192, total), 1)
    main = jnp.sum(jnp.where(i == j, band, 0.0), axis=0)
    upper = jnp.sum(jnp.where(i + 1 == j, band, 0.0), axis=0)
    window = lambda v: lax.dynamic_slice(jnp.pad(v, (16, 16)), (gx * rows,), (rows + 32,))
    return window(main), window(upper)


def forward(tables, up, estimate, down, column_edges, after):
    mixed, left, right = row_mix(tables[0], up, estimate, down, after)
    return blur(tables[3], tables[4], tables[7], *column_edges(left, right), mixed)


def backward(tables, ratio, left, right, estimate, column_edges, row_edges):
    rb, re, ub, ube, zb = tables[1], tables[2], tables[5], tables[6], tables[8]
    left, right = column_edges(left, right)
    top, bottom = spread_ends(ub, ube, zb, left, right, ratio)
    up, down = row_edges(top, bottom)
    part = own_update(ub, ube, zb, rb, left, right, ratio, top, bottom, estimate)
    return edge_update(re, up, down, estimate, part)


def shards(estimate, measured, z_interp, r_interp, psf_z, psf_r, psf_u):
    depth, rows, width = estimate.shape
    gx = lax.axis_index("gx")
    row_edges = lambda top, bottom: (send(bottom, "gx", 1), send(top, "gx", -1))
    up, down = row_edges(*row_ends(estimate))
    far = lax.ppermute(far_half(measured, rows), AXES, core_swap())
    main, upper = diagonal_windows(r_interp, gx, rows)
    tables = make_tables(psf_z, psf_r, psf_u, z_interp, main, upper, rows, width)
    pieces = [lax.ppermute(p, AXES, piece_perm(k)) for k, p in enumerate(pieces_of(measured, far, rows))]
    blurred = forward(tables, up, estimate, down, column_edges, pieces[:4])
    ratio, left, right = ratio_of(blurred, pieces)
    return backward(tables, ratio, left, right, estimate, column_edges, row_edges)


def solution(mesh):
    in_specs = (P(None, "gx", "gy"), P("gy", None, "gx"), P(), P(), P(), P(), P())
    out_specs = P(None, "gx", "gy")
    return jax.shard_map(shards, mesh=mesh, in_specs=in_specs, out_specs=out_specs, check_vma=False)
```

```python
import functools

import jax
import jax.numpy as jnp
from jax import lax
from jax.experimental import pallas as pl
from jax.experimental.pallas import tpu as pltpu
from jax.sharding import PartitionSpec as P

background = 0.25
HIGH = lax.Precision.HIGHEST
F32 = jnp.float32
BF = jnp.bfloat16
AXES = ("gx", "gy")
MIB = 1024 * 1024


def split(x):
    hi = x.astype(BF)
    return hi, (x - hi.astype(F32)).astype(BF)


def dot(a, b):
    return jnp.dot(a, b, preferred_element_type=F32)


def thrice(a, b):
    (ah, al), (bh, bl) = a, b
    return dot(jnp.concatenate([ah, ah, al], axis=1), jnp.concatenate([bh, bl, bh], axis=0))


def shift_perm(axis_of, d):
    if axis_of == "gx":
        return [(i * 8 + j, (i + d) * 8 + j) for i in range(16) for j in range(8) if 0 <= i + d < 16]
    return [(i * 8 + j, i * 8 + j + d) for i in range(16) for j in range(8) if 0 <= j + d < 8]


def position(x, y, z, c):
    return ((x % 4) * 4 + y % 4) * 8 + (z % 4) * 2 + c % 2


def core_swap():
    return [(d, d ^ 1) for d in range(128)]


def target_of(x, y, z, c, k):
    k1, k2 = k // 2, k % 2
    side, half = y >> 1, y & 1
    return (x + z + 2 * c + 2 * side + k1) & 3, 2 * (half ^ k2) + c


def source_of(x, y, z, c, k):
    k1, k2 = k // 2, k % 2
    core = y & 1
    return (x - z - 2 * core - 2 * c - k1) & 3, core, (y >> 1) ^ k2


def piece_perm(k):
    pairs = []
    for x in range(4):
        for y in range(4):
            for z in range(4):
                for c in range(2):
                    tx, ty = target_of(x, y, z, c, k)
                    pairs.append((position(x, y, z, c), position(tx, ty, x, y // 2)))
    return pairs


def params(mib, us):
    return dict(
        compiler_params=pltpu.CompilerParams(vmem_limit_bytes=mib * MIB),
        cost_estimate=pl.CostEstimate(flops=0, transcendentals=0, bytes_accessed=us * 3_000_000),
    )


def table_kernel(pz_ref, pr_ref, pu_ref, zi_ref, main_ref, upper_ref, mcol_ref, ucol_ref, *outs):
    ro_ref, rb_ref, re_ref, uo_ref, uoe_ref, ub_ref, ube_ref, zo_ref, zb_ref = outs

    def grid_of(rows, cols):
        return (
            lax.broadcasted_iota(jnp.int32, (rows, cols), 0),
            lax.broadcasted_iota(jnp.int32, (rows, cols), 1),
        )

    def taps(ref, distance):
        total = jnp.zeros(distance.shape, F32)
        for k in range(32):
            total = jnp.where(distance == k, ref[k], total)
        return total

    def left_table(value):
        h, l = split(value)
        return jnp.concatenate([h, h, l], axis=1)

    def right_table(value):
        h, l = split(value)
        return jnp.concatenate([h, l, h], axis=0)

    rows = rb_ref.shape[0]
    i, j = grid_of(rows, rows + 32)
    ro_ref[...] = left_table(taps(pr_ref, j - i) * main_ref[...] + taps(pr_ref, j - 1 - i) * upper_ref[...])
    back = taps(pr_ref, i - j + 32) * mcol_ref[...] + taps(pr_ref, i - j + 31) * ucol_ref[...]
    rb_ref[...] = left_table(back[:, 16 : 16 + rows])
    re_ref[0] = left_table(back[:16, :16])
    re_ref[1] = left_table(back[rows - 16 :, rows + 16 :])

    width = uo_ref.shape[1]
    i, j = grid_of(width, width)
    uo_ref[...] = right_table(taps(pu_ref, i + 16 - j))
    ub_ref[...] = right_table(taps(pu_ref, j - i + 16))
    a, b = i % 16, j % 16
    same = i // 16 == j // 16
    left = i < 128
    uoe_ref[...] = right_table(jnp.where(same, taps(pu_ref, jnp.where(left, a - b, a - b + 32)), 0.0))
    ube_ref[...] = right_table(jnp.where(same, taps(pu_ref, jnp.where(left, b - a + 32, b - a)), 0.0))

    depth = zi_ref.shape[0]
    i, j = grid_of(depth, depth)
    mix = jnp.dot(taps(pz_ref, j - i + 16), zi_ref[...], precision=HIGH, preferred_element_type=F32)
    zo_ref[...] = left_table(mix)
    zb_ref[...] = left_table(mix.T)


def make_tables(psf_z, psf_r, psf_u, z_interp, main, upper, rows, width):
    depth = z_interp.shape[0]
    shapes = [(rows, 3 * (rows + 32)), (rows, 3 * rows), (2, 16, 48)] + [(3 * width, width)] * 4
    shapes += [(depth, 3 * depth)] * 2
    smem = pl.BlockSpec(memory_space=pltpu.SMEM)
    vmem = pl.BlockSpec(memory_space=pltpu.VMEM)
    own = slice(16, 16 + rows)
    return pl.pallas_call(
        table_kernel,
        in_specs=[smem] * 3 + [vmem] * 5,
        out_specs=[vmem] * len(shapes),
        out_shape=[jax.ShapeDtypeStruct(s, BF) for s in shapes],
        **params(8, 3),
    )(psf_z, psf_r, psf_u, z_interp, main[None], upper[None], main[own, None], upper[own, None])


def packed(planes):
    lane = lax.broadcasted_iota(jnp.int32, planes[0][:, :128].shape, 1) // 16
    left = right = None
    for q, x in enumerate(planes):
        a, b = x[:, :128], x[:, x.shape[1] - 128 :]
        a = pltpu.roll(a, 16 * q, 1) if q else a
        b = pltpu.roll(b, (16 * q + 16) % 128, 1) if q != 7 else b
        left = a if q == 0 else jnp.where(lane == q, a, left)
        right = b if q == 0 else jnp.where(lane == q, b, right)
    return left, right


def edge_sums(both, table):
    total = across(both, table)
    return total[:, :128], total[:, 128:]


def unpacked(left, right, q):
    lane = lax.broadcasted_iota(jnp.int32, left.shape, 1)
    a = pltpu.roll(left, (128 - 16 * q) % 128, 1) if q else left
    b = pltpu.roll(right, 112 - 16 * q, 1) if q != 7 else right
    return jnp.concatenate([jnp.where(lane < 16, a, 0.0), jnp.where(lane >= 112, b, 0.0)], axis=1)


def across(x, table):
    h, l = split(x)
    return dot(jnp.concatenate([h, h, l], axis=1), table)


def along(table, x):
    h, l = split(x)
    return dot(table, jnp.concatenate([h, l, h], axis=0))


def whole(t):
    return pl.BlockSpec(t.shape, lambda i: (0,) * t.ndim)


def row_kernel(table_ref, own_ref, left_ref, right_ref, *refs):
    up_ref, down_ref, up_edge_ref, down_edge_ref = refs[:4]
    out_ref, edge_ref = refs[-2:]
    table = table_ref[...]
    for z in range(8):
        out_ref[z] = along(table, jnp.concatenate([up_ref[z], own_ref[z], down_ref[z]], axis=0))
    both = jnp.concatenate([left_ref[0], right_ref[0]], axis=1)
    edge_ref[0] = along(table, jnp.concatenate([up_edge_ref[0], both, down_edge_ref[0]], axis=0))


def row_mix(table, up, own, down, left, right, after):
    depth, rows, cols = own.shape
    groups = depth // 8
    block = lambda r: pl.BlockSpec((8, r, cols), lambda i: (i, 0, 0))
    packs = pl.BlockSpec((1, rows, 128), lambda i: (i, 0, 0))
    extra = pl.BlockSpec((1, 16, cols), lambda i: (depth + i, 0, 0))
    return pl.pallas_call(
        row_kernel,
        grid=(groups,),
        in_specs=[whole(table), block(rows), packs, packs, block(16), block(16), extra, extra] + [ANY] * len(after),
        out_specs=[block(rows), pl.BlockSpec((1, rows, cols), lambda i: (i, 0, 0))],
        out_shape=[jax.ShapeDtypeStruct(own.shape, F32), jax.ShapeDtypeStruct((groups, rows, cols), F32)],
        **params(10, 4),
    )(table, own, left, right, up, down, up, down, *after)


def blur_kernel(u_ref, e_ref, m_ref, edge_ref, x_ref, out_ref):
    depth, rows, cols = x_ref.shape
    total = across(x_ref[...].reshape(depth * rows, cols), u_ref[...]).reshape(depth, rows, cols)
    groups = depth // 8
    left, right = edge_sums(edge_ref[...].reshape(groups * rows, cols), e_ref[...])
    left, right = left.reshape(groups, rows, 128), right.reshape(groups, rows, 128)
    extra = [unpacked(left[g], right[g], q) for g in range(groups) for q in range(8)]
    total = jnp.transpose(total + jnp.stack(extra), (1, 0, 2))
    table = m_ref[...]
    for r in range(rows):
        out_ref[r] = along(table, total[r])


def blur(u, e, m, edge, x):
    depth, rows, cols = x.shape
    block = lambda d, c: pl.BlockSpec((d, 8, c), lambda i: (0, i, 0))
    return pl.pallas_call(
        blur_kernel,
        grid=(rows // 8,),
        in_specs=[whole(u), whole(e), whole(m), block(depth // 8, cols), block(depth, cols)],
        out_specs=pl.BlockSpec((8, depth, cols), lambda i: (i, 0, 0)),
        out_shape=jax.ShapeDtypeStruct((rows, depth, cols), F32),
        **params(14, 8),
    )(u, e, m, edge, x)


def ratio_kernel(blur_ref, *refs):
    pieces, (out_ref, left_ref, right_ref) = refs[:-3], refs[-3:]
    for k, piece in enumerate(pieces):
        pair, core, half = source_of(*place(), k)
        cols = pl.ds(pl.multiple_of(half * 128, 128), 128)
        for part in range(2):
            planes = pl.ds(pl.multiple_of((pair * 2 + (core ^ part)) * 8, 8), 8)
            seen = jnp.transpose(piece[part], (1, 0, 2))
            out_ref[:, planes, cols] = seen / (blur_ref[:, planes, cols] + background)
    for g in range(left_ref.shape[0]):
        left_ref[g], right_ref[g] = packed([out_ref[8 * g + q] for q in range(8)])


def ratio_of(blurred, pieces):
    rows, depth, cols = blurred.shape
    vmem = pl.BlockSpec(memory_space=pltpu.VMEM)
    shapes = [blurred.shape] + [(rows // 8, depth, 128)] * 2
    return pl.pallas_call(
        ratio_kernel,
        in_specs=[vmem] * (1 + len(pieces)),
        out_specs=[vmem] * 3,
        out_shape=[jax.ShapeDtypeStruct(s, F32) for s in shapes],
        **params(20, 7),
    )(blurred, *pieces)


def spread_tile(ratio, left, right, u, e, m):
    rows, depth, cols = ratio.shape
    total = across(ratio.reshape(rows * depth, cols), u).reshape(rows, depth, cols)
    left, right = edge_sums(jnp.concatenate([left, right], axis=1), e)
    planes = [along(m, total[q] + unpacked(left, right, q)) for q in range(rows)]
    return jnp.transpose(jnp.stack(planes), (1, 0, 2))


def ends_kernel(u_ref, e_ref, m_ref, left_ref, right_ref, x_ref, top_ref, bottom_ref):
    step = pl.program_id(0)
    tile = spread_tile(x_ref[...], left_ref[0], right_ref[0], u_ref[...], e_ref[...], m_ref[...])
    for s, ref in ((0, top_ref), (2, bottom_ref)):
        for t in range(2):

            @pl.when(step == s + t)
            def _(ref=ref, t=t):
                ref[:, 8 * t : 8 * t + 8, :] = tile


def spread_ends(u, e, m, left, right, ratio):
    rows, depth, cols = ratio.shape
    at = lambda i: (jnp.where(i < 2, i, rows // 8 - 4 + i), 0, 0)
    end = pl.BlockSpec((depth, 16, cols), lambda i: (0, 0, 0))
    return pl.pallas_call(
        ends_kernel,
        grid=(4,),
        in_specs=[whole(u), whole(e), whole(m)]
        + [pl.BlockSpec((1, depth, 128), at)] * 2
        + [pl.BlockSpec((8, depth, cols), at)],
        out_specs=[end, end],
        out_shape=[jax.ShapeDtypeStruct((depth, 16, cols), F32)] * 2,
        **params(14, 4),
    )(u, e, m, left, right, ratio)


def own_kernel(u_ref, e_ref, m_ref, a_ref, left_ref, right_ref, x_ref, top_ref, bottom_ref, est_ref, out_ref, kept):
    step = pl.program_id(0)
    inner = kept.shape[1] // 8

    @pl.when(step < inner)
    def _():
        rows = pl.ds(pl.multiple_of(step * 8, 8), 8)
        kept[:, rows, :] = spread_tile(x_ref[...], left_ref[0], right_ref[0], u_ref[...], e_ref[...], m_ref[...])

    @pl.when(step >= inner)
    def _():
        first = pl.multiple_of((step - inner) * 8, 8)
        table = a_ref[...]
        for z in range(8):
            x = jnp.concatenate([top_ref[z], kept[first + z], bottom_ref[z]], axis=0)
            out_ref[z] = est_ref[z] * along(table, x)


def own_update(u, e, m, a, left, right, ratio, top, bottom, est):
    rows, depth, cols = ratio.shape
    inner = rows // 8 - 4
    early = lambda i: (jnp.minimum(i, inner - 1) + 2, 0, 0)
    late = lambda i: (jnp.maximum(i - inner, 0), 0, 0)
    return pl.pallas_call(
        own_kernel,
        grid=(inner + depth // 8,),
        in_specs=[whole(u), whole(e), whole(m), whole(a)]
        + [pl.BlockSpec((1, depth, 128), early)] * 2
        + [pl.BlockSpec((8, depth, cols), early)]
        + [pl.BlockSpec((8, 16, cols), late)] * 2
        + [pl.BlockSpec((8, rows, cols), late)],
        out_specs=pl.BlockSpec((8, rows, cols), late),
        out_shape=jax.ShapeDtypeStruct(est.shape, F32),
        scratch_shapes=[pltpu.VMEM((depth, rows - 32, cols), F32)],
        **params(16, 8),
    )(u, e, m, a, left, right, ratio, top, bottom, est)


def edge_kernel(a_ref, up_ref, down_ref, est_ref, part_ref, out_ref):
    side = pl.program_id(0)
    for s, x_ref in ((0, up_ref), (1, down_ref)):

        @pl.when(side == s)
        def _(x_ref=x_ref):
            table = a_ref[0]
            for z in range(est_ref.shape[0]):
                out_ref[z] = part_ref[z] + est_ref[z] * along(table, x_ref[z])


def edge_update(a, up, down, est, part):
    depth, rows, cols = est.shape
    step, chunk = rows // 16 - 1, depth
    last = depth // chunk - 1
    tile = pl.BlockSpec((chunk, 16, cols), lambda s, i: (i, s * step, 0))
    return pl.pallas_call(
        edge_kernel,
        grid=(2, depth // chunk),
        in_specs=[pl.BlockSpec((1, 16, 48), lambda s, i: (s, 0, 0))]
        + [pl.BlockSpec((chunk, 16, cols), lambda s, i: (i + (last - i) * s, 0, 0))]
        + [pl.BlockSpec((chunk, 16, cols), lambda s, i: (i * s, 0, 0))]
        + [tile, tile],
        out_specs=tile,
        out_shape=jax.ShapeDtypeStruct(est.shape, F32),
        input_output_aliases={4: 0},
        **params(20, 3),
    )(a, up, down, est, part)


def send(x, axis, d):
    return lax.ppermute(x, AXES, shift_perm(axis, d))


def column_edges(left, right):
    return send(right, "gy", 1), send(left, "gy", -1)


def place():
    gx, gy = lax.axis_index("gx"), lax.axis_index("gy")
    return gx >> 2, gx & 3, gy >> 1, gy & 1


HBM = pl.BlockSpec(memory_space=pltpu.HBM)
ANY = pl.BlockSpec(memory_space=pl.ANY)


def run_copies(pairs, sems):
    copies = [pltpu.make_async_copy(src, dst, sems.at[n]) for n, (src, dst) in enumerate(pairs)]
    for copy in copies:
        copy.start()
    for copy in copies:
        copy.wait()


def copy_call(body, count, shapes, inputs, us):
    return pl.pallas_call(
        body,
        in_specs=[HBM] * len(inputs),
        out_specs=[pl.BlockSpec(memory_space=pltpu.VMEM)] * len(shapes),
        out_shape=[jax.ShapeDtypeStruct(s, F32) for s in shapes],
        scratch_shapes=[pltpu.SemaphoreType.DMA((count,))],
        **params(16, us),
    )(*inputs)


def column_ends(est):
    def body(est_ref, left_ref, right_ref):
        for g in range(left_ref.shape[0]):
            left_ref[g], right_ref[g] = packed([est_ref[8 * g + q] for q in range(8)])

    depth, rows, _ = est.shape
    vmem = pl.BlockSpec(memory_space=pltpu.VMEM)
    return pl.pallas_call(
        body,
        in_specs=[vmem],
        out_specs=[vmem] * 2,
        out_shape=[jax.ShapeDtypeStruct((depth // 8, rows, 128), F32)] * 2,
        **params(14, 2),
    )(est)


def row_ends(est, left, right):
    def body(est_ref, left_ref, right_ref, top_ref, bottom_ref, sems):
        depth, rows, _ = est_ref.shape
        pairs = []
        for out, r in ((top_ref, 0), (bottom_ref, rows - 16)):
            at = pl.ds(r, 16)
            for d in range(0, depth, 16):
                pairs.append((est_ref.at[pl.ds(d, 16), at], out.at[pl.ds(d, 16)]))
            tail = pl.ds(depth, depth // 8)
            pairs.append((left_ref.at[:, at], out.at[tail, :, pl.ds(0, 128)]))
            pairs.append((right_ref.at[:, at], out.at[tail, :, pl.ds(128, 128)]))
        run_copies(pairs, sems)

    depth, _, cols = est.shape
    return copy_call(body, depth // 8 + 4, [(depth + depth // 8, 16, cols)] * 2, (est, left, right), 2)


def halves_of(measured, rows):
    def body(measured_ref, near_ref, far_ref, sems):
        x, y, z, c = place()
        pairs = []
        for out, core in ((near_ref, c), (far_ref, 1 - c)):
            for k in range(8):
                tx, ty = target_of(x, y, z, core, k)
                pairs.append((measured_ref.at[:, tx * 4 + ty], out.at[k]))
        run_copies(pairs, sems)

    return copy_call(body, 16, [(8, 8, rows, 128)] * 2, (measured.reshape(8, 16, rows, 128),), 2)


def pieces_of(near, far):
    def body(near_ref, far_ref, *refs):
        outs, sems = refs[:-1], refs[-1]
        pairs = []
        for k, out in enumerate(outs):
            pairs.append((near_ref.at[k], out.at[0]))
            pairs.append((far_ref.at[k], out.at[1]))
        run_copies(pairs, sems)

    return copy_call(body, 16, [(2, *near.shape[1:])] * 8, (near, far), 2)


def diagonal_windows(r_interp, gx, rows):
    total = r_interp.shape[0]
    first = jnp.clip(gx * rows - 64, 0, total - 192)
    band = lax.dynamic_slice(r_interp, (first, 0), (192, total))
    i = lax.broadcasted_iota(jnp.int32, (192, total), 0) + first
    j = lax.broadcasted_iota(jnp.int32, (192, total), 1)
    main = jnp.sum(jnp.where(i == j, band, 0.0), axis=0)
    upper = jnp.sum(jnp.where(i + 1 == j, band, 0.0), axis=0)
    window = lambda v: lax.dynamic_slice(jnp.pad(v, (16, 16)), (gx * rows,), (rows + 32,))
    return window(main), window(upper)


def forward(tables, up, estimate, down, left, right, after):
    mixed, edge = row_mix(tables[0], up, estimate, down, left, right, after)
    return blur(tables[3], tables[4], tables[7], edge, mixed)


def backward(tables, ratio, left, right, estimate, column_edges, row_edges):
    rb, re, ub, ube, zb = tables[1], tables[2], tables[5], tables[6], tables[8]
    left, right = column_edges(left, right)
    top, bottom = spread_ends(ub, ube, zb, left, right, ratio)
    up, down = row_edges(top, bottom)
    part = own_update(ub, ube, zb, rb, left, right, ratio, top, bottom, estimate)
    return edge_update(re, up, down, estimate, part)


def shards(estimate, measured, z_interp, r_interp, psf_z, psf_r, psf_u):
    depth, rows, width = estimate.shape
    gx = lax.axis_index("gx")
    row_edges = lambda top, bottom: (send(bottom, "gx", 1), send(top, "gx", -1))
    left, right = column_edges(*column_ends(estimate))
    near, far = halves_of(measured, rows)
    far = lax.ppermute(far, AXES, core_swap())
    up, down = row_edges(*row_ends(estimate, left, right))
    main, upper = diagonal_windows(r_interp, gx, rows)
    tables = make_tables(psf_z, psf_r, psf_u, z_interp, main, upper, rows, width)
    pieces = [lax.ppermute(p, AXES, piece_perm(k)) for k, p in enumerate(pieces_of(near, far))]
    blurred = forward(tables, up, estimate, down, left, right, pieces[:3])
    ratio, left, right = ratio_of(blurred, pieces)
    return backward(tables, ratio, left, right, estimate, column_edges, row_edges)


def solution(mesh):
    in_specs = (P(None, "gx", "gy"), P("gy", None, "gx"), P(), P(), P(), P(), P())
    out_specs = P(None, "gx", "gy")
    return jax.shard_map(shards, mesh=mesh, in_specs=in_specs, out_specs=out_specs, check_vma=False)
```

```python
import functools

import jax
import jax.numpy as jnp
from jax import lax
from jax.experimental import pallas as pl
from jax.experimental.pallas import tpu as pltpu
from jax.sharding import PartitionSpec as P

background = 0.25
HIGH = lax.Precision.HIGHEST
F32 = jnp.float32
BF = jnp.bfloat16
AXES = ("gx", "gy")
MIB = 1024 * 1024


def split(x):
    hi = x.astype(BF)
    return hi, (x - hi.astype(F32)).astype(BF)


def dot(a, b):
    return jnp.dot(a, b, preferred_element_type=F32)


def thrice(a, b):
    (ah, al), (bh, bl) = a, b
    return dot(jnp.concatenate([ah, ah, al], axis=1), jnp.concatenate([bh, bl, bh], axis=0))


def shift_perm(axis_of, d):
    if axis_of == "gx":
        return [(i * 8 + j, (i + d) * 8 + j) for i in range(16) for j in range(8) if 0 <= i + d < 16]
    return [(i * 8 + j, i * 8 + j + d) for i in range(16) for j in range(8) if 0 <= j + d < 8]


def position(x, y, z, c):
    return ((x % 4) * 4 + y % 4) * 8 + (z % 4) * 2 + c % 2


def core_swap():
    return [(d, d ^ 1) for d in range(128)]


def target_of(x, y, z, c, k):
    k1, k2 = k // 2, k % 2
    side, half = y >> 1, y & 1
    return (x + z + 2 * c + 2 * side + k1) & 3, 2 * (half ^ k2) + c


def source_of(x, y, z, c, k):
    k1, k2 = k // 2, k % 2
    core = y & 1
    return (x - z - 2 * core - 2 * c - k1) & 3, core, (y >> 1) ^ k2


def piece_perm(k):
    pairs = []
    for x in range(4):
        for y in range(4):
            for z in range(4):
                for c in range(2):
                    tx, ty = target_of(x, y, z, c, k)
                    pairs.append((position(x, y, z, c), position(tx, ty, x, y // 2)))
    return pairs


def params(mib, us):
    return dict(
        compiler_params=pltpu.CompilerParams(vmem_limit_bytes=mib * MIB),
        cost_estimate=pl.CostEstimate(flops=0, transcendentals=0, bytes_accessed=us * 3_000_000),
    )


def table_kernel(pz_ref, pr_ref, pu_ref, zi_ref, main_ref, upper_ref, mcol_ref, ucol_ref, *outs):
    ro_ref, rb_ref, re_ref, uo_ref, uoe_ref, ub_ref, ube_ref, zo_ref, zb_ref = outs

    def grid_of(rows, cols):
        return (
            lax.broadcasted_iota(jnp.int32, (rows, cols), 0),
            lax.broadcasted_iota(jnp.int32, (rows, cols), 1),
        )

    def taps(ref, distance):
        total = jnp.zeros(distance.shape, F32)
        for k in range(32):
            total = jnp.where(distance == k, ref[k], total)
        return total

    def left_table(value):
        h, l = split(value)
        return jnp.concatenate([h, h, l], axis=1)

    def right_table(value):
        h, l = split(value)
        return jnp.concatenate([h, l, h], axis=0)

    rows = rb_ref.shape[0]
    i, j = grid_of(rows, rows + 32)
    ro_ref[...] = left_table(taps(pr_ref, j - i) * main_ref[...] + taps(pr_ref, j - 1 - i) * upper_ref[...])
    back = taps(pr_ref, i - j + 32) * mcol_ref[...] + taps(pr_ref, i - j + 31) * ucol_ref[...]
    rb_ref[...] = left_table(back[:, 16 : 16 + rows])
    re_ref[0] = left_table(back[:16, :16])
    re_ref[1] = left_table(back[rows - 16 :, rows + 16 :])

    width = uo_ref.shape[1]
    i, j = grid_of(width, width)
    uo_ref[...] = right_table(taps(pu_ref, i + 16 - j))
    ub_ref[...] = right_table(taps(pu_ref, j - i + 16))
    a, b = i % 16, j % 16
    same = i // 16 == j // 16
    left = i < 128
    uoe_ref[...] = right_table(jnp.where(same, taps(pu_ref, jnp.where(left, a - b, a - b + 32)), 0.0))
    ube_ref[...] = right_table(jnp.where(same, taps(pu_ref, jnp.where(left, b - a + 32, b - a)), 0.0))

    depth = zi_ref.shape[0]
    i, j = grid_of(depth, depth)
    mix = jnp.dot(taps(pz_ref, j - i + 16), zi_ref[...], precision=HIGH, preferred_element_type=F32)
    zo_ref[...] = left_table(mix)
    zb_ref[...] = left_table(mix.T)


def make_tables(psf_z, psf_r, psf_u, z_interp, main, upper, rows, width):
    depth = z_interp.shape[0]
    shapes = [(rows, 3 * (rows + 32)), (rows, 3 * rows), (2, 16, 48)] + [(3 * width, width)] * 4
    shapes += [(depth, 3 * depth)] * 2
    smem = pl.BlockSpec(memory_space=pltpu.SMEM)
    vmem = pl.BlockSpec(memory_space=pltpu.VMEM)
    own = slice(16, 16 + rows)
    return pl.pallas_call(
        table_kernel,
        in_specs=[smem] * 3 + [vmem] * 5,
        out_specs=[vmem] * len(shapes),
        out_shape=[jax.ShapeDtypeStruct(s, BF) for s in shapes],
        **params(8, 3),
    )(psf_z, psf_r, psf_u, z_interp, main[None], upper[None], main[own, None], upper[own, None])


def packed(planes):
    lane = lax.broadcasted_iota(jnp.int32, planes[0][:, :128].shape, 1) // 16
    left = right = None
    for q, x in enumerate(planes):
        a, b = x[:, :128], x[:, x.shape[1] - 128 :]
        a = pltpu.roll(a, 16 * q, 1) if q else a
        b = pltpu.roll(b, (16 * q + 16) % 128, 1) if q != 7 else b
        left = a if q == 0 else jnp.where(lane == q, a, left)
        right = b if q == 0 else jnp.where(lane == q, b, right)
    return left, right


def edge_sums(both, table):
    total = across(both, table)
    return total[:, :128], total[:, 128:]


def unpacked(left, right, q):
    lane = lax.broadcasted_iota(jnp.int32, left.shape, 1)
    a = pltpu.roll(left, (128 - 16 * q) % 128, 1) if q else left
    b = pltpu.roll(right, 112 - 16 * q, 1) if q != 7 else right
    return jnp.concatenate([jnp.where(lane < 16, a, 0.0), jnp.where(lane >= 112, b, 0.0)], axis=1)


def across(x, table):
    h, l = split(x)
    return dot(jnp.concatenate([h, h, l], axis=1), table)


def along(table, x):
    h, l = split(x)
    return dot(table, jnp.concatenate([h, l, h], axis=0))


def whole(t):
    return pl.BlockSpec(t.shape, lambda i: (0,) * t.ndim)


def row_kernel(*refs):
    (table_ref, own_ref, left_ref, right_ref, up_ref, down_ref, up_edge_ref, down_edge_ref, out_ref, edge_ref) = refs[-10:]
    table = table_ref[...]
    for z in range(8):
        out_ref[z] = along(table, jnp.concatenate([up_ref[z], own_ref[z], down_ref[z]], axis=0))
    both = jnp.concatenate([left_ref[0], right_ref[0]], axis=1)
    edge_ref[0] = along(table, jnp.concatenate([up_edge_ref[0], both, down_edge_ref[0]], axis=0))


def row_mix(table, up, own, down, left, right, after):
    depth, rows, cols = own.shape
    groups = depth // 8
    block = lambda r: pl.BlockSpec((8, r, cols), lambda i: (i, 0, 0))
    packs = pl.BlockSpec((1, rows, 128), lambda i: (i, 0, 0))
    extra = pl.BlockSpec((1, 16, cols), lambda i: (depth + i, 0, 0))
    return pl.pallas_call(
        row_kernel,
        grid=(groups,),
        in_specs=[ANY] * len(after) + [whole(table), block(rows), packs, packs, block(16), block(16), extra, extra],
        out_specs=[block(rows), pl.BlockSpec((1, rows, cols), lambda i: (i, 0, 0))],
        out_shape=[jax.ShapeDtypeStruct(own.shape, F32), jax.ShapeDtypeStruct((groups, rows, cols), F32)],
        **params(10, 4),
    )(*after, table, own, left, right, up, down, up, down)


def blur_kernel(u_ref, e_ref, m_ref, edge_ref, x_ref, out_ref):
    depth, rows, cols = x_ref.shape
    total = across(x_ref[...].reshape(depth * rows, cols), u_ref[...]).reshape(depth, rows, cols)
    groups = depth // 8
    left, right = edge_sums(edge_ref[...].reshape(groups * rows, cols), e_ref[...])
    left, right = left.reshape(groups, rows, 128), right.reshape(groups, rows, 128)
    extra = [unpacked(left[g], right[g], q) for g in range(groups) for q in range(8)]
    total = jnp.transpose(total + jnp.stack(extra), (1, 0, 2))
    table = m_ref[...]
    for r in range(rows):
        out_ref[r] = along(table, total[r])


def blur(u, e, m, edge, x):
    depth, rows, cols = x.shape
    block = lambda d, c: pl.BlockSpec((d, 8, c), lambda i: (0, i, 0))
    return pl.pallas_call(
        blur_kernel,
        grid=(rows // 8,),
        in_specs=[whole(u), whole(e), whole(m), block(depth // 8, cols), block(depth, cols)],
        out_specs=pl.BlockSpec((8, depth, cols), lambda i: (i, 0, 0)),
        out_shape=jax.ShapeDtypeStruct((rows, depth, cols), F32),
        **params(14, 8),
    )(u, e, m, edge, x)


def ratio_kernel(blur_ref, *refs):
    pieces, (out_ref, left_ref, right_ref) = refs[:-3], refs[-3:]
    for k, piece in enumerate(pieces):
        pair, core, half = source_of(*place(), k)
        cols = pl.ds(pl.multiple_of(half * 128, 128), 128)
        for part in range(2):
            planes = pl.ds(pl.multiple_of((pair * 2 + (core ^ part)) * 8, 8), 8)
            seen = jnp.transpose(piece[part], (1, 0, 2))
            out_ref[:, planes, cols] = seen / (blur_ref[:, planes, cols] + background)
    for g in range(left_ref.shape[0]):
        left_ref[g], right_ref[g] = packed([out_ref[8 * g + q] for q in range(8)])


def ratio_of(blurred, pieces):
    rows, depth, cols = blurred.shape
    vmem = pl.BlockSpec(memory_space=pltpu.VMEM)
    shapes = [blurred.shape] + [(rows // 8, depth, 128)] * 2
    return pl.pallas_call(
        ratio_kernel,
        in_specs=[vmem] * (1 + len(pieces)),
        out_specs=[vmem] * 3,
        out_shape=[jax.ShapeDtypeStruct(s, F32) for s in shapes],
        **params(20, 7),
    )(blurred, *pieces)


def spread_tile(ratio, left, right, u, e, m):
    rows, depth, cols = ratio.shape
    total = across(ratio.reshape(rows * depth, cols), u).reshape(rows, depth, cols)
    left, right = edge_sums(jnp.concatenate([left, right], axis=1), e)
    planes = [along(m, total[q] + unpacked(left, right, q)) for q in range(rows)]
    return jnp.transpose(jnp.stack(planes), (1, 0, 2))


def ends_kernel(u_ref, e_ref, m_ref, left_ref, right_ref, x_ref, top_ref, bottom_ref):
    step = pl.program_id(0)
    tile = spread_tile(x_ref[...], left_ref[0], right_ref[0], u_ref[...], e_ref[...], m_ref[...])
    for s, ref in ((0, top_ref), (2, bottom_ref)):
        for t in range(2):

            @pl.when(step == s + t)
            def _(ref=ref, t=t):
                ref[:, 8 * t : 8 * t + 8, :] = tile


def spread_ends(u, e, m, left, right, ratio):
    rows, depth, cols = ratio.shape
    at = lambda i: (jnp.where(i < 2, i, rows // 8 - 4 + i), 0, 0)
    end = pl.BlockSpec((depth, 16, cols), lambda i: (0, 0, 0))
    return pl.pallas_call(
        ends_kernel,
        grid=(4,),
        in_specs=[whole(u), whole(e), whole(m)]
        + [pl.BlockSpec((1, depth, 128), at)] * 2
        + [pl.BlockSpec((8, depth, cols), at)],
        out_specs=[end, end],
        out_shape=[jax.ShapeDtypeStruct((depth, 16, cols), F32)] * 2,
        **params(14, 4),
    )(u, e, m, left, right, ratio)


def own_kernel(u_ref, e_ref, m_ref, a_ref, left_ref, right_ref, x_ref, top_ref, bottom_ref, est_ref, out_ref, kept):
    step = pl.program_id(0)
    inner = kept.shape[1] // 8

    @pl.when(step < inner)
    def _():
        rows = pl.ds(pl.multiple_of(step * 8, 8), 8)
        kept[:, rows, :] = spread_tile(x_ref[...], left_ref[0], right_ref[0], u_ref[...], e_ref[...], m_ref[...])

    @pl.when(step >= inner)
    def _():
        first = pl.multiple_of((step - inner) * 8, 8)
        table = a_ref[...]
        for z in range(8):
            x = jnp.concatenate([top_ref[z], kept[first + z], bottom_ref[z]], axis=0)
            out_ref[z] = est_ref[z] * along(table, x)


def own_update(u, e, m, a, left, right, ratio, top, bottom, est):
    rows, depth, cols = ratio.shape
    inner = rows // 8 - 4
    early = lambda i: (jnp.minimum(i, inner - 1) + 2, 0, 0)
    late = lambda i: (jnp.maximum(i - inner, 0), 0, 0)
    return pl.pallas_call(
        own_kernel,
        grid=(inner + depth // 8,),
        in_specs=[whole(u), whole(e), whole(m), whole(a)]
        + [pl.BlockSpec((1, depth, 128), early)] * 2
        + [pl.BlockSpec((8, depth, cols), early)]
        + [pl.BlockSpec((8, 16, cols), late)] * 2
        + [pl.BlockSpec((8, rows, cols), late)],
        out_specs=pl.BlockSpec((8, rows, cols), late),
        out_shape=jax.ShapeDtypeStruct(est.shape, F32),
        scratch_shapes=[pltpu.VMEM((depth, rows - 32, cols), F32)],
        **params(16, 8),
    )(u, e, m, a, left, right, ratio, top, bottom, est)


def edge_kernel(a_ref, up_ref, down_ref, est_ref, part_ref, out_ref):
    side = pl.program_id(0)
    for s, x_ref in ((0, up_ref), (1, down_ref)):

        @pl.when(side == s)
        def _(x_ref=x_ref):
            table = a_ref[0]
            for z in range(est_ref.shape[0]):
                out_ref[z] = part_ref[z] + est_ref[z] * along(table, x_ref[z])


def edge_update(a, up, down, est, part):
    depth, rows, cols = est.shape
    step, chunk = rows // 16 - 1, depth
    last = depth // chunk - 1
    tile = pl.BlockSpec((chunk, 16, cols), lambda s, i: (i, s * step, 0))
    return pl.pallas_call(
        edge_kernel,
        grid=(2, depth // chunk),
        in_specs=[pl.BlockSpec((1, 16, 48), lambda s, i: (s, 0, 0))]
        + [pl.BlockSpec((chunk, 16, cols), lambda s, i: (i + (last - i) * s, 0, 0))]
        + [pl.BlockSpec((chunk, 16, cols), lambda s, i: (i * s, 0, 0))]
        + [tile, tile],
        out_specs=tile,
        out_shape=jax.ShapeDtypeStruct(est.shape, F32),
        input_output_aliases={4: 0},
        **params(20, 3),
    )(a, up, down, est, part)


def send(x, axis, d):
    return lax.ppermute(x, AXES, shift_perm(axis, d))


def column_edges(left, right):
    return send(right, "gy", 1), send(left, "gy", -1)


def place():
    gx, gy = lax.axis_index("gx"), lax.axis_index("gy")
    return gx >> 2, gx & 3, gy >> 1, gy & 1


HBM = pl.BlockSpec(memory_space=pltpu.HBM)
ANY = pl.BlockSpec(memory_space=pl.ANY)


def run_copies(pairs, sems):
    copies = [pltpu.make_async_copy(src, dst, sems.at[n]) for n, (src, dst) in enumerate(pairs)]
    for copy in copies:
        copy.start()
    for copy in copies:
        copy.wait()


def copy_call(body, count, shapes, inputs, us):
    return pl.pallas_call(
        body,
        in_specs=[HBM] * len(inputs),
        out_specs=[pl.BlockSpec(memory_space=pltpu.VMEM)] * len(shapes),
        out_shape=[jax.ShapeDtypeStruct(s, F32) for s in shapes],
        scratch_shapes=[pltpu.SemaphoreType.DMA((count,))],
        **params(16, us),
    )(*inputs)


def column_ends(est):
    def body(est_ref, left_ref, right_ref):
        for g in range(left_ref.shape[0]):
            left_ref[g], right_ref[g] = packed([est_ref[8 * g + q] for q in range(8)])

    depth, rows, _ = est.shape
    vmem = pl.BlockSpec(memory_space=pltpu.VMEM)
    return pl.pallas_call(
        body,
        in_specs=[vmem],
        out_specs=[vmem] * 2,
        out_shape=[jax.ShapeDtypeStruct((depth // 8, rows, 128), F32)] * 2,
        **params(14, 2),
    )(est)


def row_ends(est, left, right, after):
    def body(*refs):
        est_ref, left_ref, right_ref, top_ref, bottom_ref, sems = refs[-6:]
        depth, rows, _ = est_ref.shape
        pairs = []
        for out, r in ((top_ref, 0), (bottom_ref, rows - 16)):
            at = pl.ds(r, 16)
            for d in range(0, depth, 16):
                pairs.append((est_ref.at[pl.ds(d, 16), at], out.at[pl.ds(d, 16)]))
            tail = pl.ds(depth, depth // 8)
            pairs.append((left_ref.at[:, at], out.at[tail, :, pl.ds(0, 128)]))
            pairs.append((right_ref.at[:, at], out.at[tail, :, pl.ds(128, 128)]))
        run_copies(pairs, sems)

    depth, _, cols = est.shape
    return copy_call(body, depth // 8 + 4, [(depth + depth // 8, 16, cols)] * 2, (*after, est, left, right), 2)


def halves_of(measured, rows):
    def body(measured_ref, near_ref, far_ref, sems):
        x, y, z, c = place()
        pairs = []
        for out, core in ((near_ref, c), (far_ref, 1 - c)):
            for k in range(8):
                tx, ty = target_of(x, y, z, core, k)
                pairs.append((measured_ref.at[:, tx * 4 + ty], out.at[k]))
        run_copies(pairs, sems)

    return copy_call(body, 16, [(8, 8, rows, 128)] * 2, (measured.reshape(8, 16, rows, 128),), 2)


def pieces_of(near, far, steps, after):
    def body(*refs):
        near_ref, far_ref, *outs = refs[len(after) : -1]
        sems = refs[-1]
        pairs = []
        for k, out in zip(steps, outs):
            pairs.append((near_ref.at[k], out.at[0]))
            pairs.append((far_ref.at[k], out.at[1]))
        run_copies(pairs, sems)

    shapes = [(2, *near.shape[1:])] * len(steps)
    return copy_call(body, 2 * len(steps), shapes, (*after, near, far), 2)


def diagonal_windows(r_interp, gx, rows):
    total = r_interp.shape[0]
    first = jnp.clip(gx * rows - 64, 0, total - 192)
    band = lax.dynamic_slice(r_interp, (first, 0), (192, total))
    i = lax.broadcasted_iota(jnp.int32, (192, total), 0) + first
    j = lax.broadcasted_iota(jnp.int32, (192, total), 1)
    main = jnp.sum(jnp.where(i == j, band, 0.0), axis=0)
    upper = jnp.sum(jnp.where(i + 1 == j, band, 0.0), axis=0)
    window = lambda v: lax.dynamic_slice(jnp.pad(v, (16, 16)), (gx * rows,), (rows + 32,))
    return window(main), window(upper)


def forward(tables, up, estimate, down, left, right, after):
    mixed, edge = row_mix(tables[0], up, estimate, down, left, right, after)
    return blur(tables[3], tables[4], tables[7], edge, mixed)


def backward(tables, ratio, left, right, estimate, column_edges, row_edges):
    rb, re, ub, ube, zb = tables[1], tables[2], tables[5], tables[6], tables[8]
    left, right = column_edges(left, right)
    top, bottom = spread_ends(ub, ube, zb, left, right, ratio)
    up, down = row_edges(top, bottom)
    part = own_update(ub, ube, zb, rb, left, right, ratio, top, bottom, estimate)
    return edge_update(re, up, down, estimate, part)


def shards(estimate, measured, z_interp, r_interp, psf_z, psf_r, psf_u):
    depth, rows, width = estimate.shape
    gx = lax.axis_index("gx")
    row_edges = lambda top, bottom: (send(bottom, "gx", 1), send(top, "gx", -1))
    left, right = column_edges(*column_ends(estimate))
    near, far = halves_of(measured, rows)
    far = lax.ppermute(far, AXES, core_swap())
    ship = lambda parts, steps: [lax.ppermute(p, AXES, piece_perm(k)) for p, k in zip(parts, steps)]
    parts = pieces_of(near, far, range(3), ())
    pieces = ship(parts, range(3))
    top, bottom = row_ends(estimate, left, right, parts[:1])
    up, down = row_edges(top, bottom)
    main, upper = diagonal_windows(r_interp, gx, rows)
    tables = make_tables(psf_z, psf_r, psf_u, z_interp, main, upper, rows, width)
    pieces += ship(pieces_of(near, far, range(3, 8), (top, tables[0])), range(3, 8))
    blurred = forward(tables, up, estimate, down, left, right, pieces[:3])
    ratio, left, right = ratio_of(blurred, pieces)
    return backward(tables, ratio, left, right, estimate, column_edges, row_edges)


def solution(mesh):
    in_specs = (P(None, "gx", "gy"), P("gy", None, "gx"), P(), P(), P(), P(), P())
    out_specs = P(None, "gx", "gy")
    return jax.shard_map(shards, mesh=mesh, in_specs=in_specs, out_specs=out_specs, check_vma=False)
```

```python
import functools

import jax
import jax.numpy as jnp
from jax import lax
from jax.experimental import pallas as pl
from jax.experimental.pallas import tpu as pltpu
from jax.sharding import PartitionSpec as P

background = 0.25
HIGH = lax.Precision.HIGHEST
F32 = jnp.float32
BF = jnp.bfloat16
AXES = ("gx", "gy")
MIB = 1024 * 1024


def split(x):
    hi = x.astype(BF)
    return hi, (x - hi.astype(F32)).astype(BF)


def dot(a, b):
    return jnp.dot(a, b, preferred_element_type=F32)


def thrice(a, b):
    (ah, al), (bh, bl) = a, b
    return dot(jnp.concatenate([ah, ah, al], axis=1), jnp.concatenate([bh, bl, bh], axis=0))


def shift_perm(axis_of, d):
    if axis_of == "gx":
        return [(i * 8 + j, (i + d) * 8 + j) for i in range(16) for j in range(8) if 0 <= i + d < 16]
    return [(i * 8 + j, i * 8 + j + d) for i in range(16) for j in range(8) if 0 <= j + d < 8]


def position(x, y, z, c):
    return ((x % 4) * 4 + y % 4) * 8 + (z % 4) * 2 + c % 2


def core_swap():
    return [(d, d ^ 1) for d in range(128)]


def target_of(x, y, z, c, k):
    k1, k2 = k // 2, k % 2
    side, half = y >> 1, y & 1
    return (x + z + 2 * c + 2 * side + k1) & 3, 2 * (half ^ k2) + c


def source_of(x, y, z, c, k):
    k1, k2 = k // 2, k % 2
    core = y & 1
    return (x - z - 2 * core - 2 * c - k1) & 3, core, (y >> 1) ^ k2


def piece_perm(k):
    pairs = []
    for x in range(4):
        for y in range(4):
            for z in range(4):
                for c in range(2):
                    tx, ty = target_of(x, y, z, c, k)
                    pairs.append((position(x, y, z, c), position(tx, ty, x, y // 2)))
    return pairs


def params(mib, us):
    return dict(
        compiler_params=pltpu.CompilerParams(vmem_limit_bytes=mib * MIB),
        cost_estimate=pl.CostEstimate(flops=0, transcendentals=0, bytes_accessed=us * 3_000_000),
    )


def table_kernel(pz_ref, pr_ref, pu_ref, zi_ref, main_ref, upper_ref, mcol_ref, ucol_ref, *outs):
    ro_ref, rb_ref, re_ref, uo_ref, uoe_ref, ub_ref, ube_ref, zo_ref, zb_ref = outs

    def grid_of(rows, cols):
        return (
            lax.broadcasted_iota(jnp.int32, (rows, cols), 0),
            lax.broadcasted_iota(jnp.int32, (rows, cols), 1),
        )

    def taps(ref, distance):
        total = jnp.zeros(distance.shape, F32)
        for k in range(32):
            total = jnp.where(distance == k, ref[k], total)
        return total

    def left_table(value):
        h, l = split(value)
        return jnp.concatenate([h, h, l], axis=1)

    def right_table(value):
        h, l = split(value)
        return jnp.concatenate([h, l, h], axis=0)

    rows = rb_ref.shape[0]
    i, j = grid_of(rows, rows + 32)
    ro_ref[...] = left_table(taps(pr_ref, j - i) * main_ref[...] + taps(pr_ref, j - 1 - i) * upper_ref[...])
    back = taps(pr_ref, i - j + 32) * mcol_ref[...] + taps(pr_ref, i - j + 31) * ucol_ref[...]
    rb_ref[...] = left_table(back[:, 16 : 16 + rows])
    re_ref[0] = left_table(back[:16, :16])
    re_ref[1] = left_table(back[rows - 16 :, rows + 16 :])

    width = uo_ref.shape[1]
    i, j = grid_of(width, width)
    uo_ref[...] = right_table(taps(pu_ref, i + 16 - j))
    ub_ref[...] = right_table(taps(pu_ref, j - i + 16))
    a, b = i % 16, j % 16
    same = i // 16 == j // 16
    left = i < 128
    uoe_ref[...] = right_table(jnp.where(same, taps(pu_ref, jnp.where(left, a - b, a - b + 32)), 0.0))
    ube_ref[...] = right_table(jnp.where(same, taps(pu_ref, jnp.where(left, b - a + 32, b - a)), 0.0))

    depth = zi_ref.shape[0]
    i, j = grid_of(depth, depth)
    mix = jnp.dot(taps(pz_ref, j - i + 16), zi_ref[...], precision=HIGH, preferred_element_type=F32)
    zo_ref[...] = left_table(mix)
    zb_ref[...] = left_table(mix.T)


def make_tables(psf_z, psf_r, psf_u, z_interp, main, upper, rows, width):
    depth = z_interp.shape[0]
    shapes = [(rows, 3 * (rows + 32)), (rows, 3 * rows), (2, 16, 48)] + [(3 * width, width)] * 4
    shapes += [(depth, 3 * depth)] * 2
    smem = pl.BlockSpec(memory_space=pltpu.SMEM)
    vmem = pl.BlockSpec(memory_space=pltpu.VMEM)
    own = slice(16, 16 + rows)
    return pl.pallas_call(
        table_kernel,
        in_specs=[smem] * 3 + [vmem] * 5,
        out_specs=[vmem] * len(shapes),
        out_shape=[jax.ShapeDtypeStruct(s, BF) for s in shapes],
        **params(8, 3),
    )(psf_z, psf_r, psf_u, z_interp, main[None], upper[None], main[own, None], upper[own, None])


def packed(planes):
    lane = lax.broadcasted_iota(jnp.int32, planes[0][:, :128].shape, 1) // 16
    left = right = None
    for q, x in enumerate(planes):
        a, b = x[:, :128], x[:, x.shape[1] - 128 :]
        a = pltpu.roll(a, 16 * q, 1) if q else a
        b = pltpu.roll(b, (16 * q + 16) % 128, 1) if q != 7 else b
        left = a if q == 0 else jnp.where(lane == q, a, left)
        right = b if q == 0 else jnp.where(lane == q, b, right)
    return left, right


def edge_sums(both, table):
    total = across(both, table)
    return total[:, :128], total[:, 128:]


def unpacked(left, right, q):
    lane = lax.broadcasted_iota(jnp.int32, left.shape, 1)
    a = pltpu.roll(left, (128 - 16 * q) % 128, 1) if q else left
    b = pltpu.roll(right, 112 - 16 * q, 1) if q != 7 else right
    return jnp.concatenate([jnp.where(lane < 16, a, 0.0), jnp.where(lane >= 112, b, 0.0)], axis=1)


def across(x, table):
    h, l = split(x)
    return dot(jnp.concatenate([h, h, l], axis=1), table)


def along(table, x):
    h, l = split(x)
    return dot(table, jnp.concatenate([h, l, h], axis=0))


def whole(t):
    return pl.BlockSpec(t.shape, lambda i: (0,) * t.ndim)


def row_kernel(table_ref, own_ref, left_ref, right_ref, *refs):
    up_ref, down_ref, up_edge_ref, down_edge_ref = refs[:4]
    out_ref, edge_ref = refs[-2:]
    table = table_ref[...]
    for z in range(8):
        out_ref[z] = along(table, jnp.concatenate([up_ref[z], own_ref[z], down_ref[z]], axis=0))
    both = jnp.concatenate([left_ref[0], right_ref[0]], axis=1)
    edge_ref[0] = along(table, jnp.concatenate([up_edge_ref[0], both, down_edge_ref[0]], axis=0))


def row_mix(table, up, own, down, left, right, after):
    depth, rows, cols = own.shape
    groups = depth // 8
    block = lambda r: pl.BlockSpec((8, r, cols), lambda i: (i, 0, 0))
    packs = pl.BlockSpec((1, rows, 128), lambda i: (i, 0, 0))
    extra = pl.BlockSpec((1, 16, cols), lambda i: (depth + i, 0, 0))
    return pl.pallas_call(
        row_kernel,
        grid=(groups,),
        in_specs=[whole(table), block(rows), packs, packs, block(16), block(16), extra, extra] + [ANY] * len(after),
        out_specs=[block(rows), pl.BlockSpec((1, rows, cols), lambda i: (i, 0, 0))],
        out_shape=[jax.ShapeDtypeStruct(own.shape, F32), jax.ShapeDtypeStruct((groups, rows, cols), F32)],
        **params(10, 4),
    )(table, own, left, right, up, down, up, down, *after)


def blur_kernel(u_ref, e_ref, m_ref, edge_ref, x_ref, out_ref):
    depth, rows, cols = x_ref.shape
    total = across(x_ref[...].reshape(depth * rows, cols), u_ref[...]).reshape(depth, rows, cols)
    groups = depth // 8
    left, right = edge_sums(edge_ref[...].reshape(groups * rows, cols), e_ref[...])
    left, right = left.reshape(groups, rows, 128), right.reshape(groups, rows, 128)
    extra = [unpacked(left[g], right[g], q) for g in range(groups) for q in range(8)]
    total = jnp.transpose(total + jnp.stack(extra), (1, 0, 2))
    table = m_ref[...]
    for r in range(rows):
        out_ref[r] = along(table, total[r])


def blur(u, e, m, edge, x):
    depth, rows, cols = x.shape
    block = lambda d, c: pl.BlockSpec((d, 8, c), lambda i: (0, i, 0))
    return pl.pallas_call(
        blur_kernel,
        grid=(rows // 8,),
        in_specs=[whole(u), whole(e), whole(m), block(depth // 8, cols), block(depth, cols)],
        out_specs=pl.BlockSpec((8, depth, cols), lambda i: (i, 0, 0)),
        out_shape=jax.ShapeDtypeStruct((rows, depth, cols), F32),
        **params(14, 8),
    )(u, e, m, edge, x)


EARLY = 3
ENDS = ((0, 0, 16), (48, 16, 16))
INNER = ((16, 0, 32),)


def ratio_of(blurred, pieces, segments):
    def body(blur_ref, *refs):
        pieces, (out_ref, left_ref, right_ref) = refs[:-3], refs[-3:]
        for k, piece in enumerate(pieces):
            pair, core, half = source_of(*place(), k)
            cols = pl.ds(pl.multiple_of(half * 128, 128), 128)
            for part in range(2):
                planes = pl.ds(pl.multiple_of((pair * 2 + (core ^ part)) * 8, 8), 8)
                seen = jnp.transpose(piece[part], (1, 0, 2))
                for start, here, n in segments:
                    below = blur_ref[start : start + n, planes, cols] + background
                    out_ref[here : here + n, planes, cols] = seen[here : here + n] / below
        for g in range(left_ref.shape[0]):
            left_ref[g], right_ref[g] = packed([out_ref[8 * g + q] for q in range(8)])

    _, depth, cols = blurred.shape
    vmem = pl.BlockSpec(memory_space=pltpu.VMEM)
    shapes = [(32, depth, cols)] + [(4, depth, 128)] * 2
    return pl.pallas_call(
        body,
        in_specs=[vmem] * (1 + len(pieces)),
        out_specs=[vmem] * 3,
        out_shape=[jax.ShapeDtypeStruct(s, F32) for s in shapes],
        **params(14, 3),
    )(blurred, *pieces)


def spread_tile(ratio, left, right, u, e, m):
    rows, depth, cols = ratio.shape
    total = across(ratio.reshape(rows * depth, cols), u).reshape(rows, depth, cols)
    left, right = edge_sums(jnp.concatenate([left, right], axis=1), e)
    planes = [along(m, total[q] + unpacked(left, right, q)) for q in range(rows)]
    return jnp.transpose(jnp.stack(planes), (1, 0, 2))


def ends_kernel(*refs):
    u_ref, e_ref, m_ref, left_ref, right_ref, x_ref, top_ref, bottom_ref = refs[-8:]
    step = pl.program_id(0)
    tile = spread_tile(x_ref[...], left_ref[0], right_ref[0], u_ref[...], e_ref[...], m_ref[...])
    for s, ref in ((0, top_ref), (2, bottom_ref)):
        for t in range(2):

            @pl.when(step == s + t)
            def _(ref=ref, t=t):
                ref[:, 8 * t : 8 * t + 8, :] = tile


def spread_ends(u, e, m, left, right, ratio, after):
    _, depth, cols = ratio.shape
    at = lambda i: (i, 0, 0)
    end = pl.BlockSpec((depth, 16, cols), lambda i: (0, 0, 0))
    return pl.pallas_call(
        ends_kernel,
        grid=(4,),
        in_specs=[ANY] * len(after)
        + [whole(u), whole(e), whole(m)]
        + [pl.BlockSpec((1, depth, 128), at)] * 2
        + [pl.BlockSpec((8, depth, cols), at)],
        out_specs=[end, end],
        out_shape=[jax.ShapeDtypeStruct((depth, 16, cols), F32)] * 2,
        **params(14, 4),
    )(*after, u, e, m, left, right, ratio)


def own_kernel(u_ref, e_ref, m_ref, a_ref, left_ref, right_ref, x_ref, top_ref, bottom_ref, est_ref, out_ref, kept):
    step = pl.program_id(0)
    inner = kept.shape[1] // 8

    @pl.when(step < inner)
    def _():
        rows = pl.ds(pl.multiple_of(step * 8, 8), 8)
        kept[:, rows, :] = spread_tile(x_ref[...], left_ref[0], right_ref[0], u_ref[...], e_ref[...], m_ref[...])

    @pl.when(step >= inner)
    def _():
        first = pl.multiple_of((step - inner) * 8, 8)
        table = a_ref[...]
        for z in range(8):
            x = jnp.concatenate([top_ref[z], kept[first + z], bottom_ref[z]], axis=0)
            out_ref[z] = est_ref[z] * along(table, x)


def own_update(u, e, m, a, left, right, ratio, top, bottom, est):
    (_, depth, cols), rows = ratio.shape, est.shape[1]
    inner = rows // 8 - 4
    early = lambda i: (jnp.minimum(i, inner - 1), 0, 0)
    late = lambda i: (jnp.maximum(i - inner, 0), 0, 0)
    return pl.pallas_call(
        own_kernel,
        grid=(inner + depth // 8,),
        in_specs=[whole(u), whole(e), whole(m), whole(a)]
        + [pl.BlockSpec((1, depth, 128), early)] * 2
        + [pl.BlockSpec((8, depth, cols), early)]
        + [pl.BlockSpec((8, 16, cols), late)] * 2
        + [pl.BlockSpec((8, rows, cols), late)],
        out_specs=pl.BlockSpec((8, rows, cols), late),
        out_shape=jax.ShapeDtypeStruct(est.shape, F32),
        scratch_shapes=[pltpu.VMEM((depth, rows - 32, cols), F32)],
        **params(16, 8),
    )(u, e, m, a, left, right, ratio, top, bottom, est)


def edge_kernel(a_ref, up_ref, down_ref, est_ref, part_ref, out_ref):
    side = pl.program_id(0)
    for s, x_ref in ((0, up_ref), (1, down_ref)):

        @pl.when(side == s)
        def _(x_ref=x_ref):
            table = a_ref[0]
            for z in range(est_ref.shape[0]):
                out_ref[z] = part_ref[z] + est_ref[z] * along(table, x_ref[z])


def edge_update(a, up, down, est, part):
    depth, rows, cols = est.shape
    step, chunk = rows // 16 - 1, depth
    last = depth // chunk - 1
    tile = pl.BlockSpec((chunk, 16, cols), lambda s, i: (i, s * step, 0))
    return pl.pallas_call(
        edge_kernel,
        grid=(2, depth // chunk),
        in_specs=[pl.BlockSpec((1, 16, 48), lambda s, i: (s, 0, 0))]
        + [pl.BlockSpec((chunk, 16, cols), lambda s, i: (i + (last - i) * s, 0, 0))]
        + [pl.BlockSpec((chunk, 16, cols), lambda s, i: (i * s, 0, 0))]
        + [tile, tile],
        out_specs=tile,
        out_shape=jax.ShapeDtypeStruct(est.shape, F32),
        input_output_aliases={4: 0},
        **params(20, 3),
    )(a, up, down, est, part)


def send(x, axis, d):
    return lax.ppermute(x, AXES, shift_perm(axis, d))


def column_edges(left, right):
    return send(right, "gy", 1), send(left, "gy", -1)


def place():
    gx, gy = lax.axis_index("gx"), lax.axis_index("gy")
    return gx >> 2, gx & 3, gy >> 1, gy & 1


HBM = pl.BlockSpec(memory_space=pltpu.HBM)
ANY = pl.BlockSpec(memory_space=pl.ANY)


def run_copies(pairs, sems):
    copies = [pltpu.make_async_copy(src, dst, sems.at[n]) for n, (src, dst) in enumerate(pairs)]
    for copy in copies:
        copy.start()
    for copy in copies:
        copy.wait()


def copy_call(body, count, shapes, inputs, us):
    return pl.pallas_call(
        body,
        in_specs=[HBM] * len(inputs),
        out_specs=[pl.BlockSpec(memory_space=pltpu.VMEM)] * len(shapes),
        out_shape=[jax.ShapeDtypeStruct(s, F32) for s in shapes],
        scratch_shapes=[pltpu.SemaphoreType.DMA((count,))],
        **params(16, us),
    )(*inputs)


def column_ends(est):
    def body(est_ref, left_ref, right_ref):
        for g in range(left_ref.shape[0]):
            left_ref[g], right_ref[g] = packed([est_ref[8 * g + q] for q in range(8)])

    depth, rows, _ = est.shape
    vmem = pl.BlockSpec(memory_space=pltpu.VMEM)
    return pl.pallas_call(
        body,
        in_specs=[vmem],
        out_specs=[vmem] * 2,
        out_shape=[jax.ShapeDtypeStruct((depth // 8, rows, 128), F32)] * 2,
        **params(14, 2),
    )(est)


def row_ends(est, left, right):
    def body(est_ref, left_ref, right_ref, top_ref, bottom_ref, sems):
        depth, rows, _ = est_ref.shape
        pairs = []
        for out, r in ((top_ref, 0), (bottom_ref, rows - 16)):
            at = pl.ds(r, 16)
            for d in range(0, depth, 16):
                pairs.append((est_ref.at[pl.ds(d, 16), at], out.at[pl.ds(d, 16)]))
            tail = pl.ds(depth, depth // 8)
            pairs.append((left_ref.at[:, at], out.at[tail, :, pl.ds(0, 128)]))
            pairs.append((right_ref.at[:, at], out.at[tail, :, pl.ds(128, 128)]))
        run_copies(pairs, sems)

    depth, _, cols = est.shape
    return copy_call(body, depth // 8 + 4, [(depth + depth // 8, 16, cols)] * 2, (est, left, right), 2)


def halves_of(measured, rows):
    def body(measured_ref, near_ref, far_ref, sems):
        x, y, z, c = place()
        pairs = []
        for out, core in ((near_ref, c), (far_ref, 1 - c)):
            for k in range(8):
                tx, ty = target_of(x, y, z, core, k)
                pairs.append((measured_ref.at[:, tx * 4 + ty], out.at[k]))
        run_copies(pairs, sems)

    return copy_call(body, 16, [(8, 8, rows, 128)] * 2, (measured.reshape(8, 16, rows, 128),), 2)


def pieces_of(near, far, steps, segments, after):
    def body(*refs):
        near_ref, far_ref, *outs = refs[len(after) : -1]
        sems = refs[-1]
        pairs = []
        for k, out in zip(steps, outs):
            for part, ref in enumerate((near_ref, far_ref)):
                for start, here, n in segments:
                    pairs.append((ref.at[k, :, pl.ds(start, n)], out.at[part, :, pl.ds(here, n)]))
        run_copies(pairs, sems)

    _, planes, _, cols = near.shape
    shapes = [(2, planes, 32, cols)] * len(steps)
    return copy_call(body, 2 * len(steps) * len(segments), shapes, (*after, near, far), 2)


def diagonal_windows(r_interp, gx, rows):
    total = r_interp.shape[0]
    first = jnp.clip(gx * rows - 64, 0, total - 192)
    band = lax.dynamic_slice(r_interp, (first, 0), (192, total))
    i = lax.broadcasted_iota(jnp.int32, (192, total), 0) + first
    j = lax.broadcasted_iota(jnp.int32, (192, total), 1)
    main = jnp.sum(jnp.where(i == j, band, 0.0), axis=0)
    upper = jnp.sum(jnp.where(i + 1 == j, band, 0.0), axis=0)
    window = lambda v: lax.dynamic_slice(jnp.pad(v, (16, 16)), (gx * rows,), (rows + 32,))
    return window(main), window(upper)


def forward(tables, up, estimate, down, left, right, after):
    mixed, edge = row_mix(tables[0], up, estimate, down, left, right, after)
    return blur(tables[3], tables[4], tables[7], edge, mixed)


def backward(tables, ends, inner, estimate, column_edges, row_edges, after):
    rb, re, ub, ube, zb = tables[1], tables[2], tables[5], tables[6], tables[8]
    ratio, left, right = ends
    left, right = column_edges(left, right)
    top, bottom = spread_ends(ub, ube, zb, left, right, ratio, after)
    up, down = row_edges(top, bottom)
    ratio, left, right = inner(top)
    left, right = column_edges(left, right)
    part = own_update(ub, ube, zb, rb, left, right, ratio, top, bottom, estimate)
    return edge_update(re, up, down, estimate, part)


def shards(estimate, measured, z_interp, r_interp, psf_z, psf_r, psf_u):
    depth, rows, width = estimate.shape
    gx = lax.axis_index("gx")
    row_edges = lambda top, bottom: (send(bottom, "gx", 1), send(top, "gx", -1))
    left, right = column_edges(*column_ends(estimate))
    near, far = halves_of(measured, rows)
    far = lax.ppermute(far, AXES, core_swap())
    up, down = row_edges(*row_ends(estimate, left, right))
    main, upper = diagonal_windows(r_interp, gx, rows)
    tables = make_tables(psf_z, psf_r, psf_u, z_interp, main, upper, rows, width)
    every = range(8)
    ship = lambda parts, steps: [lax.ppermute(p, AXES, piece_perm(k)) for p, k in zip(parts, steps)]
    pieces = ship(pieces_of(near, far, every, ENDS, ()), every)
    blurred = forward(tables, up, estimate, down, left, right, pieces[:3])
    early, late = every[:EARLY], every[EARLY:]
    rest = ship(pieces_of(near, far, early, INNER, (blurred,)), early)
    ends = ratio_of(blurred, pieces, ENDS)

    def inner(after):
        return ratio_of(blurred, rest + ship(pieces_of(near, far, late, INNER, (after,)), late), INNER)

    return backward(tables, ends, inner, estimate, column_edges, row_edges, rest[:1])


def solution(mesh):
    in_specs = (P(None, "gx", "gy"), P("gy", None, "gx"), P(), P(), P(), P(), P())
    out_specs = P(None, "gx", "gy")
    return jax.shard_map(shards, mesh=mesh, in_specs=in_specs, out_specs=out_specs, check_vma=False)
```

```python
import functools

import jax
import jax.numpy as jnp
from jax import lax
from jax.experimental import pallas as pl
from jax.experimental.pallas import tpu as pltpu
from jax.sharding import PartitionSpec as P

background = 0.25
HIGH = lax.Precision.HIGHEST
F32 = jnp.float32
BF = jnp.bfloat16
AXES = ("gx", "gy")
MIB = 1024 * 1024


def split(x):
    hi = x.astype(BF)
    return hi, (x - hi.astype(F32)).astype(BF)


def dot(a, b):
    return jnp.dot(a, b, preferred_element_type=F32)


def thrice(a, b):
    (ah, al), (bh, bl) = a, b
    return dot(jnp.concatenate([ah, ah, al], axis=1), jnp.concatenate([bh, bl, bh], axis=0))


def shift_perm(axis_of, d):
    if axis_of == "gx":
        return [(i * 8 + j, (i + d) * 8 + j) for i in range(16) for j in range(8) if 0 <= i + d < 16]
    return [(i * 8 + j, i * 8 + j + d) for i in range(16) for j in range(8) if 0 <= j + d < 8]


def position(x, y, z, c):
    return ((x % 4) * 4 + y % 4) * 8 + (z % 4) * 2 + c % 2


def core_swap():
    return [(d, d ^ 1) for d in range(128)]


def target_of(x, y, z, c, k):
    k1, k2 = k // 2, k % 2
    side, half = y >> 1, y & 1
    return (x + z + 2 * c + 2 * side + k1) & 3, 2 * (half ^ k2) + c


def source_of(x, y, z, c, k):
    k1, k2 = k // 2, k % 2
    core = y & 1
    return (x - z - 2 * core - 2 * c - k1) & 3, core, (y >> 1) ^ k2


def piece_perm(k):
    pairs = []
    for x in range(4):
        for y in range(4):
            for z in range(4):
                for c in range(2):
                    tx, ty = target_of(x, y, z, c, k)
                    pairs.append((position(x, y, z, c), position(tx, ty, x, y // 2)))
    return pairs


def params(mib, us):
    return dict(
        compiler_params=pltpu.CompilerParams(vmem_limit_bytes=mib * MIB),
        cost_estimate=pl.CostEstimate(flops=0, transcendentals=0, bytes_accessed=us * 3_000_000),
    )


def table_kernel(pz_ref, pr_ref, pu_ref, zi_ref, main_ref, upper_ref, *outs):
    ro_ref, rb_ref, re_ref, uo_ref, uoe_ref, ub_ref, ube_ref, zo_ref, zb_ref = outs

    def grid_of(rows, cols):
        return (
            lax.broadcasted_iota(jnp.int32, (rows, cols), 0),
            lax.broadcasted_iota(jnp.int32, (rows, cols), 1),
        )

    def taps(ref, distance):
        total = jnp.zeros(distance.shape, F32)
        for k in range(32):
            total = jnp.where(distance == k, ref[k], total)
        return total

    def left_table(value):
        h, l = split(value)
        return jnp.concatenate([h, h, l], axis=1)

    def right_table(value):
        h, l = split(value)
        return jnp.concatenate([h, l, h], axis=0)

    rows = rb_ref.shape[0]
    i, j = grid_of(rows, 128)
    main, upper = main_ref[...], upper_ref[...]
    out = taps(pr_ref, j - i) * main + taps(pr_ref, j - 1 - i) * upper
    ro_ref[...] = left_table(out[:, : rows + 32])
    i, j = grid_of(128, 128)
    back = (taps(pr_ref, j - i + 16) * main + taps(pr_ref, j - i + 15) * upper).T[16 : 16 + rows]
    rb_ref[...] = left_table(back[:, 16 : 16 + rows])
    re_ref[0] = left_table(back[:16, :16])
    re_ref[1] = left_table(back[rows - 16 :, rows + 16 : rows + 32])

    width = uo_ref.shape[1]
    i, j = grid_of(width, width)
    uo_ref[...] = right_table(taps(pu_ref, i + 16 - j))
    ub_ref[...] = right_table(taps(pu_ref, j - i + 16))
    a, b = i % 16, j % 16
    same = i // 16 == j // 16
    left = i < 128
    uoe_ref[...] = right_table(jnp.where(same, taps(pu_ref, jnp.where(left, a - b, a - b + 32)), 0.0))
    ube_ref[...] = right_table(jnp.where(same, taps(pu_ref, jnp.where(left, b - a + 32, b - a)), 0.0))

    depth = zi_ref.shape[0]
    i, j = grid_of(depth, depth)
    mix = jnp.dot(taps(pz_ref, j - i + 16), zi_ref[...], precision=HIGH, preferred_element_type=F32)
    zo_ref[...] = left_table(mix)
    zb_ref[...] = left_table(mix.T)


def make_tables(psf_z, psf_r, psf_u, z_interp, main, upper, rows, width):
    depth = z_interp.shape[0]
    shapes = [(rows, 3 * (rows + 32)), (rows, 3 * rows), (2, 16, 48)] + [(3 * width, width)] * 4
    shapes += [(depth, 3 * depth)] * 2
    smem = pl.BlockSpec(memory_space=pltpu.SMEM)
    vmem = pl.BlockSpec(memory_space=pltpu.VMEM)
    return pl.pallas_call(
        table_kernel,
        in_specs=[smem] * 3 + [vmem] * 3,
        out_specs=[vmem] * len(shapes),
        out_shape=[jax.ShapeDtypeStruct(s, BF) for s in shapes],
        **params(8, 3),
    )(psf_z, psf_r, psf_u, z_interp, main[None], upper[None])


def packed(planes):
    lane = lax.broadcasted_iota(jnp.int32, planes[0][:, :128].shape, 1) // 16
    left = right = None
    for q, x in enumerate(planes):
        a, b = x[:, :128], x[:, x.shape[1] - 128 :]
        a = pltpu.roll(a, 16 * q, 1) if q else a
        b = pltpu.roll(b, (16 * q + 16) % 128, 1) if q != 7 else b
        left = a if q == 0 else jnp.where(lane == q, a, left)
        right = b if q == 0 else jnp.where(lane == q, b, right)
    return left, right


def edge_sums(both, table):
    total = across(both, table)
    return total[:, :128], total[:, 128:]


def unpacked(left, right, q):
    lane = lax.broadcasted_iota(jnp.int32, left.shape, 1)
    a = pltpu.roll(left, (128 - 16 * q) % 128, 1) if q else left
    b = pltpu.roll(right, 112 - 16 * q, 1) if q != 7 else right
    return jnp.concatenate([jnp.where(lane < 16, a, 0.0), jnp.where(lane >= 112, b, 0.0)], axis=1)


def across(x, table):
    h, l = split(x)
    return dot(jnp.concatenate([h, h, l], axis=1), table)


def along(table, x):
    h, l = split(x)
    return dot(table, jnp.concatenate([h, l, h], axis=0))


def whole(t):
    return pl.BlockSpec(t.shape, lambda i: (0,) * t.ndim)


def row_kernel(table_ref, own_ref, left_ref, right_ref, *refs):
    up_ref, down_ref, up_edge_ref, down_edge_ref = refs[:4]
    out_ref, edge_ref = refs[-2:]
    table = table_ref[...]
    for z in range(8):
        out_ref[z] = along(table, jnp.concatenate([up_ref[z], own_ref[z], down_ref[z]], axis=0))
    both = jnp.concatenate([left_ref[0], right_ref[0]], axis=1)
    edge_ref[0] = along(table, jnp.concatenate([up_edge_ref[0], both, down_edge_ref[0]], axis=0))


def row_mix(table, up, own, down, left, right, after):
    depth, rows, cols = own.shape
    groups = depth // 8
    block = lambda r: pl.BlockSpec((8, r, cols), lambda i: (i, 0, 0))
    packs = pl.BlockSpec((1, rows, 128), lambda i: (i, 0, 0))
    extra = pl.BlockSpec((1, 16, cols), lambda i: (depth + i, 0, 0))
    return pl.pallas_call(
        row_kernel,
        grid=(groups,),
        in_specs=[whole(table), block(rows), packs, packs, block(16), block(16), extra, extra] + [ANY] * len(after),
        out_specs=[block(rows), pl.BlockSpec((1, rows, cols), lambda i: (i, 0, 0))],
        out_shape=[jax.ShapeDtypeStruct(own.shape, F32), jax.ShapeDtypeStruct((groups, rows, cols), F32)],
        **params(10, 4),
    )(table, own, left, right, up, down, up, down, *after)


def blur_kernel(u_ref, e_ref, m_ref, edge_ref, x_ref, out_ref):
    depth, rows, cols = x_ref.shape
    total = across(x_ref[...].reshape(depth * rows, cols), u_ref[...]).reshape(depth, rows, cols)
    groups = depth // 8
    left, right = edge_sums(edge_ref[...].reshape(groups * rows, cols), e_ref[...])
    left, right = left.reshape(groups, rows, 128), right.reshape(groups, rows, 128)
    extra = [unpacked(left[g], right[g], q) for g in range(groups) for q in range(8)]
    total = jnp.transpose(total + jnp.stack(extra), (1, 0, 2))
    table = m_ref[...]
    for r in range(rows):
        out_ref[r] = along(table, total[r])


def blur(u, e, m, edge, x):
    depth, rows, cols = x.shape
    block = lambda d, c: pl.BlockSpec((d, 8, c), lambda i: (0, i, 0))
    return pl.pallas_call(
        blur_kernel,
        grid=(rows // 8,),
        in_specs=[whole(u), whole(e), whole(m), block(depth // 8, cols), block(depth, cols)],
        out_specs=pl.BlockSpec((8, depth, cols), lambda i: (i, 0, 0)),
        out_shape=jax.ShapeDtypeStruct((rows, depth, cols), F32),
        **params(14, 8),
    )(u, e, m, edge, x)


def ratio_kernel(blur_ref, *refs):
    pieces, (out_ref, left_ref, right_ref) = refs[:-3], refs[-3:]
    for k, piece in enumerate(pieces):
        pair, core, half = source_of(*place(), k)
        cols = pl.ds(pl.multiple_of(half * 128, 128), 128)
        for part in range(2):
            planes = pl.ds(pl.multiple_of((pair * 2 + (core ^ part)) * 8, 8), 8)
            seen = jnp.transpose(piece[part], (1, 0, 2))
            out_ref[:, planes, cols] = seen / (blur_ref[:, planes, cols] + background)
    for g in range(left_ref.shape[0]):
        left_ref[g], right_ref[g] = packed([out_ref[8 * g + q] for q in range(8)])


def ratio_of(blurred, pieces):
    rows, depth, cols = blurred.shape
    vmem = pl.BlockSpec(memory_space=pltpu.VMEM)
    shapes = [blurred.shape] + [(rows // 8, depth, 128)] * 2
    return pl.pallas_call(
        ratio_kernel,
        in_specs=[vmem] * (1 + len(pieces)),
        out_specs=[vmem] * 3,
        out_shape=[jax.ShapeDtypeStruct(s, F32) for s in shapes],
        **params(20, 7),
    )(blurred, *pieces)


def spread_tile(ratio, left, right, u, e, m):
    rows, depth, cols = ratio.shape
    total = across(ratio.reshape(rows * depth, cols), u).reshape(rows, depth, cols)
    left, right = edge_sums(jnp.concatenate([left, right], axis=1), e)
    planes = [along(m, total[q] + unpacked(left, right, q)) for q in range(rows)]
    return jnp.transpose(jnp.stack(planes), (1, 0, 2))


def ends_kernel(u_ref, e_ref, m_ref, left_ref, right_ref, x_ref, top_ref, bottom_ref):
    step = pl.program_id(0)
    tile = spread_tile(x_ref[...], left_ref[0], right_ref[0], u_ref[...], e_ref[...], m_ref[...])
    for s, ref in ((0, top_ref), (2, bottom_ref)):
        for t in range(2):

            @pl.when(step == s + t)
            def _(ref=ref, t=t):
                ref[:, 8 * t : 8 * t + 8, :] = tile


def spread_ends(u, e, m, left, right, ratio):
    rows, depth, cols = ratio.shape
    at = lambda i: (jnp.where(i < 2, i, rows // 8 - 4 + i), 0, 0)
    end = pl.BlockSpec((depth, 16, cols), lambda i: (0, 0, 0))
    return pl.pallas_call(
        ends_kernel,
        grid=(4,),
        in_specs=[whole(u), whole(e), whole(m)]
        + [pl.BlockSpec((1, depth, 128), at)] * 2
        + [pl.BlockSpec((8, depth, cols), at)],
        out_specs=[end, end],
        out_shape=[jax.ShapeDtypeStruct((depth, 16, cols), F32)] * 2,
        **params(14, 4),
    )(u, e, m, left, right, ratio)


def own_kernel(u_ref, e_ref, m_ref, a_ref, left_ref, right_ref, x_ref, top_ref, bottom_ref, est_ref, out_ref, kept):
    step = pl.program_id(0)
    inner = kept.shape[1] // 8

    @pl.when(step < inner)
    def _():
        rows = pl.ds(pl.multiple_of(step * 8, 8), 8)
        kept[:, rows, :] = spread_tile(x_ref[...], left_ref[0], right_ref[0], u_ref[...], e_ref[...], m_ref[...])

    @pl.when(step >= inner)
    def _():
        first = pl.multiple_of((step - inner) * 8, 8)
        table = a_ref[...]
        for z in range(8):
            x = jnp.concatenate([top_ref[z], kept[first + z], bottom_ref[z]], axis=0)
            out_ref[z] = est_ref[z] * along(table, x)


def own_update(u, e, m, a, left, right, ratio, top, bottom, est):
    rows, depth, cols = ratio.shape
    inner = rows // 8 - 4
    early = lambda i: (jnp.minimum(i, inner - 1) + 2, 0, 0)
    late = lambda i: (jnp.maximum(i - inner, 0), 0, 0)
    return pl.pallas_call(
        own_kernel,
        grid=(inner + depth // 8,),
        in_specs=[whole(u), whole(e), whole(m), whole(a)]
        + [pl.BlockSpec((1, depth, 128), early)] * 2
        + [pl.BlockSpec((8, depth, cols), early)]
        + [pl.BlockSpec((8, 16, cols), late)] * 2
        + [pl.BlockSpec((8, rows, cols), late)],
        out_specs=pl.BlockSpec((8, rows, cols), late),
        out_shape=jax.ShapeDtypeStruct(est.shape, F32),
        scratch_shapes=[pltpu.VMEM((depth, rows - 32, cols), F32)],
        **params(16, 8),
    )(u, e, m, a, left, right, ratio, top, bottom, est)


def edge_kernel(a_ref, up_ref, down_ref, est_ref, part_ref, out_ref):
    side = pl.program_id(0)
    for s, x_ref in ((0, up_ref), (1, down_ref)):

        @pl.when(side == s)
        def _(x_ref=x_ref):
            table = a_ref[0]
            for z in range(est_ref.shape[0]):
                out_ref[z] = part_ref[z] + est_ref[z] * along(table, x_ref[z])


def edge_update(a, up, down, est, part):
    depth, rows, cols = est.shape
    step, chunk = rows // 16 - 1, depth
    last = depth // chunk - 1
    tile = pl.BlockSpec((chunk, 16, cols), lambda s, i: (i, s * step, 0))
    return pl.pallas_call(
        edge_kernel,
        grid=(2, depth // chunk),
        in_specs=[pl.BlockSpec((1, 16, 48), lambda s, i: (s, 0, 0))]
        + [pl.BlockSpec((chunk, 16, cols), lambda s, i: (i + (last - i) * s, 0, 0))]
        + [pl.BlockSpec((chunk, 16, cols), lambda s, i: (i * s, 0, 0))]
        + [tile, tile],
        out_specs=tile,
        out_shape=jax.ShapeDtypeStruct(est.shape, F32),
        input_output_aliases={4: 0},
        **params(20, 3),
    )(a, up, down, est, part)


def send(x, axis, d):
    return lax.ppermute(x, AXES, shift_perm(axis, d))


def column_edges(left, right):
    return send(right, "gy", 1), send(left, "gy", -1)


def place():
    gx, gy = lax.axis_index("gx"), lax.axis_index("gy")
    return gx >> 2, gx & 3, gy >> 1, gy & 1


HBM = pl.BlockSpec(memory_space=pltpu.HBM)
ANY = pl.BlockSpec(memory_space=pl.ANY)


def run_copies(pairs, sems):
    copies = [pltpu.make_async_copy(src, dst, sems.at[n]) for n, (src, dst) in enumerate(pairs)]
    for copy in copies:
        copy.start()
    for copy in copies:
        copy.wait()


def copy_call(body, count, shapes, inputs, us):
    return pl.pallas_call(
        body,
        in_specs=[HBM] * len(inputs),
        out_specs=[pl.BlockSpec(memory_space=pltpu.VMEM)] * len(shapes),
        out_shape=[jax.ShapeDtypeStruct(s, F32) for s in shapes],
        scratch_shapes=[pltpu.SemaphoreType.DMA((count,))],
        **params(16, us),
    )(*inputs)


def column_ends(est):
    def body(est_ref, left_ref, right_ref):
        for g in range(left_ref.shape[0]):
            left_ref[g], right_ref[g] = packed([est_ref[8 * g + q] for q in range(8)])

    depth, rows, _ = est.shape
    vmem = pl.BlockSpec(memory_space=pltpu.VMEM)
    return pl.pallas_call(
        body,
        in_specs=[vmem],
        out_specs=[vmem] * 2,
        out_shape=[jax.ShapeDtypeStruct((depth // 8, rows, 128), F32)] * 2,
        **params(14, 2),
    )(est)


def row_ends(est, left, right):
    def body(est_ref, left_ref, right_ref, top_ref, bottom_ref, sems):
        depth, rows, _ = est_ref.shape
        pairs = []
        for out, r in ((top_ref, 0), (bottom_ref, rows - 16)):
            at = pl.ds(r, 16)
            for d in range(0, depth, 16):
                pairs.append((est_ref.at[pl.ds(d, 16), at], out.at[pl.ds(d, 16)]))
            tail = pl.ds(depth, depth // 8)
            pairs.append((left_ref.at[:, at], out.at[tail, :, pl.ds(0, 128)]))
            pairs.append((right_ref.at[:, at], out.at[tail, :, pl.ds(128, 128)]))
        run_copies(pairs, sems)

    depth, _, cols = est.shape
    return copy_call(body, depth // 8 + 4, [(depth + depth // 8, 16, cols)] * 2, (est, left, right), 2)


def halves_of(measured, rows):
    def body(measured_ref, near_ref, far_ref, sems):
        x, y, z, c = place()
        pairs = []
        for out, core in ((near_ref, c), (far_ref, 1 - c)):
            for k in range(8):
                tx, ty = target_of(x, y, z, core, k)
                pairs.append((measured_ref.at[:, tx * 4 + ty], out.at[k]))
        run_copies(pairs, sems)

    return copy_call(body, 16, [(8, 8, rows, 128)] * 2, (measured.reshape(8, 16, rows, 128),), 2)


def pieces_of(near, far, steps, after):
    def body(*refs):
        near_ref, far_ref, *outs = refs[len(after) : -1]
        sems = refs[-1]
        pairs = []
        for k, out in zip(steps, outs):
            pairs.append((near_ref.at[k], out.at[0]))
            pairs.append((far_ref.at[k], out.at[1]))
        run_copies(pairs, sems)

    shapes = [(2, *near.shape[1:])] * len(steps)
    return copy_call(body, 2 * len(steps), shapes, (*after, near, far), 2)


def diagonal_windows(r_interp, gx, rows):
    total = r_interp.shape[0]
    first = jnp.clip(gx * rows - 64, 0, total - 192)
    band = lax.dynamic_slice(r_interp, (first, 0), (192, total))
    i = lax.broadcasted_iota(jnp.int32, (192, total), 0) + first
    j = lax.broadcasted_iota(jnp.int32, (192, total), 1)
    main = jnp.sum(jnp.where(i == j, band, 0.0), axis=0)
    upper = jnp.sum(jnp.where(i + 1 == j, band, 0.0), axis=0)
    window = lambda v: lax.dynamic_slice(jnp.pad(v, (16, 48)), (gx * rows,), (128,))
    return window(main), window(upper)


def forward(tables, up, estimate, down, left, right, after):
    mixed, edge = row_mix(tables[0], up, estimate, down, left, right, after)
    return blur(tables[3], tables[4], tables[7], edge, mixed)


def backward(tables, ratio, left, right, estimate, column_edges, row_edges):
    rb, re, ub, ube, zb = tables[1], tables[2], tables[5], tables[6], tables[8]
    left, right = column_edges(left, right)
    top, bottom = spread_ends(ub, ube, zb, left, right, ratio)
    up, down = row_edges(top, bottom)
    part = own_update(ub, ube, zb, rb, left, right, ratio, top, bottom, estimate)
    return edge_update(re, up, down, estimate, part)


def shards(estimate, measured, z_interp, r_interp, psf_z, psf_r, psf_u):
    depth, rows, width = estimate.shape
    gx = lax.axis_index("gx")
    row_edges = lambda top, bottom: (send(bottom, "gx", 1), send(top, "gx", -1))
    left, right = column_edges(*column_ends(estimate))
    near, far = halves_of(measured, rows)
    far = lax.ppermute(far, AXES, core_swap())
    up, down = row_edges(*row_ends(estimate, left, right))
    main, upper = diagonal_windows(r_interp, gx, rows)
    tables = make_tables(psf_z, psf_r, psf_u, z_interp, main, upper, rows, width)
    first, second = range(3), range(3, 8)
    ship = lambda parts, steps: [lax.ppermute(p, AXES, piece_perm(k)) for p, k in zip(parts, steps)]
    pieces = ship(pieces_of(near, far, first, ()), first)
    pieces += ship(pieces_of(near, far, second, (tables[0],)), second)
    blurred = forward(tables, up, estimate, down, left, right, pieces[:3])
    ratio, left, right = ratio_of(blurred, pieces)
    return backward(tables, ratio, left, right, estimate, column_edges, row_edges)


def solution(mesh):
    in_specs = (P(None, "gx", "gy"), P("gy", None, "gx"), P(), P(), P(), P(), P())
    out_specs = P(None, "gx", "gy")
    return jax.shard_map(shards, mesh=mesh, in_specs=in_specs, out_specs=out_specs, check_vma=False)
```

```python
import functools

import jax
import jax.numpy as jnp
from jax import lax
from jax.experimental import pallas as pl
from jax.experimental.pallas import tpu as pltpu
from jax.sharding import PartitionSpec as P

background = 0.25
HIGH = lax.Precision.HIGHEST
F32 = jnp.float32
BF = jnp.bfloat16
AXES = ("gx", "gy")
MIB = 1024 * 1024


def split(x):
    hi = x.astype(BF)
    return hi, (x - hi.astype(F32)).astype(BF)


def dot(a, b):
    return jnp.dot(a, b, preferred_element_type=F32)


def thrice(a, b):
    (ah, al), (bh, bl) = a, b
    return dot(jnp.concatenate([ah, ah, al], axis=1), jnp.concatenate([bh, bl, bh], axis=0))


def shift_perm(axis_of, d):
    if axis_of == "gx":
        return [(i * 8 + j, (i + d) * 8 + j) for i in range(16) for j in range(8) if 0 <= i + d < 16]
    return [(i * 8 + j, i * 8 + j + d) for i in range(16) for j in range(8) if 0 <= j + d < 8]


def position(x, y, z, c):
    return ((x % 4) * 4 + y % 4) * 8 + (z % 4) * 2 + c % 2


def core_swap():
    return [(d, d ^ 1) for d in range(128)]


def target_of(x, y, z, c, k):
    k1, k2 = k // 2, k % 2
    side, half = y >> 1, y & 1
    return (x + z + 2 * c + 2 * side + k1) & 3, 2 * (half ^ k2) + c


def source_of(x, y, z, c, k):
    k1, k2 = k // 2, k % 2
    core = y & 1
    return (x - z - 2 * core - 2 * c - k1) & 3, core, (y >> 1) ^ k2


def piece_perm(k):
    pairs = []
    for x in range(4):
        for y in range(4):
            for z in range(4):
                for c in range(2):
                    tx, ty = target_of(x, y, z, c, k)
                    pairs.append((position(x, y, z, c), position(tx, ty, x, y // 2)))
    return pairs


def params(mib, us):
    return dict(
        compiler_params=pltpu.CompilerParams(vmem_limit_bytes=mib * MIB),
        cost_estimate=pl.CostEstimate(flops=0, transcendentals=0, bytes_accessed=us * 3_000_000),
    )


def table_kernel(pz_ref, pr_ref, pu_ref, zi_ref, main_ref, upper_ref, *outs):
    ro_ref, rb_ref, re_ref, uo_ref, uoe_ref, ub_ref, ube_ref, zo_ref, zb_ref = outs

    def grid_of(rows, cols):
        return (
            lax.broadcasted_iota(jnp.int32, (rows, cols), 0),
            lax.broadcasted_iota(jnp.int32, (rows, cols), 1),
        )

    def taps(ref, distance):
        total = jnp.zeros(distance.shape, F32)
        for k in range(32):
            total = jnp.where(distance == k, ref[k], total)
        return total

    def left_table(value):
        h, l = split(value)
        return jnp.concatenate([h, h, l], axis=1)

    def right_table(value):
        h, l = split(value)
        return jnp.concatenate([h, l, h], axis=0)

    rows = rb_ref.shape[0]
    i, j = grid_of(rows, 128)
    main, upper = main_ref[...], upper_ref[...]
    out = taps(pr_ref, j - i) * main + taps(pr_ref, j - 1 - i) * upper
    ro_ref[...] = left_table(out[:, : rows + 32])
    i, j = grid_of(128, 128)
    back = (taps(pr_ref, j - i + 16) * main + taps(pr_ref, j - i + 15) * upper).T[16 : 16 + rows]
    rb_ref[...] = left_table(back[:, 16 : 16 + rows])
    re_ref[0] = left_table(back[:16, :16])
    re_ref[1] = left_table(back[rows - 16 :, rows + 16 : rows + 32])

    width = uo_ref.shape[1]
    i, j = grid_of(width, width)
    uo_ref[...] = right_table(taps(pu_ref, i + 16 - j))
    ub_ref[...] = right_table(taps(pu_ref, j - i + 16))
    a, b = i % 16, j % 16
    same = i // 16 == j // 16
    left = i < 128
    uoe_ref[...] = right_table(jnp.where(same, taps(pu_ref, jnp.where(left, a - b, a - b + 32)), 0.0))
    ube_ref[...] = right_table(jnp.where(same, taps(pu_ref, jnp.where(left, b - a + 32, b - a)), 0.0))

    depth = zi_ref.shape[0]
    i, j = grid_of(depth, depth)
    mix = jnp.dot(taps(pz_ref, j - i + 16), zi_ref[...], precision=HIGH, preferred_element_type=F32)
    zo_ref[...] = left_table(mix)
    zb_ref[...] = left_table(mix.T)


def make_tables(psf_z, psf_r, psf_u, z_interp, main, upper, rows, width):
    depth = z_interp.shape[0]
    shapes = [(rows, 3 * (rows + 32)), (rows, 3 * rows), (2, 16, 48)] + [(3 * width, width)] * 4
    shapes += [(depth, 3 * depth)] * 2
    smem = pl.BlockSpec(memory_space=pltpu.SMEM)
    vmem = pl.BlockSpec(memory_space=pltpu.VMEM)
    return pl.pallas_call(
        table_kernel,
        in_specs=[smem] * 3 + [vmem] * 3,
        out_specs=[vmem] * len(shapes),
        out_shape=[jax.ShapeDtypeStruct(s, BF) for s in shapes],
        **params(8, 3),
    )(psf_z, psf_r, psf_u, z_interp, main[None], upper[None])


def packed(planes):
    lane = lax.broadcasted_iota(jnp.int32, planes[0][:, :128].shape, 1) // 16
    left = right = None
    for q, x in enumerate(planes):
        a, b = x[:, :128], x[:, x.shape[1] - 128 :]
        a = pltpu.roll(a, 16 * q, 1) if q else a
        b = pltpu.roll(b, (16 * q + 16) % 128, 1) if q != 7 else b
        left = a if q == 0 else jnp.where(lane == q, a, left)
        right = b if q == 0 else jnp.where(lane == q, b, right)
    return left, right


def edge_sums(both, table):
    total = across(both, table)
    return total[:, :128], total[:, 128:]


def unpacked(left, right, q):
    lane = lax.broadcasted_iota(jnp.int32, left.shape, 1)
    a = pltpu.roll(left, (128 - 16 * q) % 128, 1) if q else left
    b = pltpu.roll(right, 112 - 16 * q, 1) if q != 7 else right
    return jnp.concatenate([jnp.where(lane < 16, a, 0.0), jnp.where(lane >= 112, b, 0.0)], axis=1)


def across(x, table):
    h, l = split(x)
    return dot(jnp.concatenate([h, h, l], axis=1), table)


def along(table, x):
    h, l = split(x)
    return dot(table, jnp.concatenate([h, l, h], axis=0))


def whole(t):
    return pl.BlockSpec(t.shape, lambda i: (0,) * t.ndim)


def row_kernel(table_ref, own_ref, left_ref, right_ref, *refs):
    up_ref, down_ref, up_edge_ref, down_edge_ref = refs[:4]
    out_ref, edge_ref = refs[-2:]
    table = table_ref[...]
    for z in range(8):
        out_ref[z] = along(table, jnp.concatenate([up_ref[z], own_ref[z], down_ref[z]], axis=0))
    both = jnp.concatenate([left_ref[0], right_ref[0]], axis=1)
    edge_ref[0] = along(table, jnp.concatenate([up_edge_ref[0], both, down_edge_ref[0]], axis=0))


def row_mix(table, up, own, down, left, right, above, below, after):
    depth, rows, cols = own.shape
    groups = depth // 8
    block = lambda d, r: pl.BlockSpec((d, r, cols), lambda i: (i, 0, 0))
    packs = pl.BlockSpec((1, rows, 128), lambda i: (i, 0, 0))
    return pl.pallas_call(
        row_kernel,
        grid=(groups,),
        in_specs=[whole(table), block(8, rows), packs, packs, block(8, 16), block(8, 16), block(1, 16), block(1, 16)]
        + [ANY] * len(after),
        out_specs=[block(8, rows), block(1, rows)],
        out_shape=[jax.ShapeDtypeStruct(own.shape, F32), jax.ShapeDtypeStruct((groups, rows, cols), F32)],
        **params(10, 4),
    )(table, own, left, right, up, down, above, below, *after)


def blur_kernel(u_ref, e_ref, m_ref, edge_ref, x_ref, out_ref):
    depth, rows, cols = x_ref.shape
    total = across(x_ref[...].reshape(depth * rows, cols), u_ref[...]).reshape(depth, rows, cols)
    groups = depth // 8
    left, right = edge_sums(edge_ref[...].reshape(groups * rows, cols), e_ref[...])
    left, right = left.reshape(groups, rows, 128), right.reshape(groups, rows, 128)
    extra = [unpacked(left[g], right[g], q) for g in range(groups) for q in range(8)]
    total = jnp.transpose(total + jnp.stack(extra), (1, 0, 2))
    table = m_ref[...]
    for r in range(rows):
        out_ref[r] = along(table, total[r])


def blur(u, e, m, edge, x):
    depth, rows, cols = x.shape
    block = lambda d, c: pl.BlockSpec((d, 8, c), lambda i: (0, i, 0))
    return pl.pallas_call(
        blur_kernel,
        grid=(rows // 8,),
        in_specs=[whole(u), whole(e), whole(m), block(depth // 8, cols), block(depth, cols)],
        out_specs=pl.BlockSpec((8, depth, cols), lambda i: (i, 0, 0)),
        out_shape=jax.ShapeDtypeStruct((rows, depth, cols), F32),
        **params(14, 8),
    )(u, e, m, edge, x)


def ratio_kernel(blur_ref, *refs):
    pieces, (out_ref, left_ref, right_ref) = refs[:-3], refs[-3:]
    for k, piece in enumerate(pieces):
        pair, core, half = source_of(*place(), k)
        cols = pl.ds(pl.multiple_of(half * 128, 128), 128)
        for part in range(2):
            planes = pl.ds(pl.multiple_of((pair * 2 + (core ^ part)) * 8, 8), 8)
            seen = jnp.transpose(piece[part], (1, 0, 2))
            out_ref[:, planes, cols] = seen / (blur_ref[:, planes, cols] + background)
    for g in range(left_ref.shape[0]):
        left_ref[g], right_ref[g] = packed([out_ref[8 * g + q] for q in range(8)])


def ratio_of(blurred, pieces):
    rows, depth, cols = blurred.shape
    vmem = pl.BlockSpec(memory_space=pltpu.VMEM)
    shapes = [blurred.shape] + [(rows // 8, depth, 128)] * 2
    return pl.pallas_call(
        ratio_kernel,
        in_specs=[vmem] * (1 + len(pieces)),
        out_specs=[vmem] * 3,
        out_shape=[jax.ShapeDtypeStruct(s, F32) for s in shapes],
        **params(20, 7),
    )(blurred, *pieces)


def spread_tile(ratio, left, right, u, e, m):
    rows, depth, cols = ratio.shape
    total = across(ratio.reshape(rows * depth, cols), u).reshape(rows, depth, cols)
    left, right = edge_sums(jnp.concatenate([left, right], axis=1), e)
    planes = [along(m, total[q] + unpacked(left, right, q)) for q in range(rows)]
    return jnp.transpose(jnp.stack(planes), (1, 0, 2))


def ends_kernel(u_ref, e_ref, m_ref, left_ref, right_ref, x_ref, top_ref, bottom_ref):
    step = pl.program_id(0)
    tile = spread_tile(x_ref[...], left_ref[0], right_ref[0], u_ref[...], e_ref[...], m_ref[...])
    for s, ref in ((0, top_ref), (2, bottom_ref)):
        for t in range(2):

            @pl.when(step == s + t)
            def _(ref=ref, t=t):
                ref[:, 8 * t : 8 * t + 8, :] = tile


def spread_ends(u, e, m, left, right, ratio):
    rows, depth, cols = ratio.shape
    at = lambda i: (jnp.where(i < 2, i, rows // 8 - 4 + i), 0, 0)
    end = pl.BlockSpec((depth, 16, cols), lambda i: (0, 0, 0))
    return pl.pallas_call(
        ends_kernel,
        grid=(4,),
        in_specs=[whole(u), whole(e), whole(m)]
        + [pl.BlockSpec((1, depth, 128), at)] * 2
        + [pl.BlockSpec((8, depth, cols), at)],
        out_specs=[end, end],
        out_shape=[jax.ShapeDtypeStruct((depth, 16, cols), F32)] * 2,
        **params(14, 4),
    )(u, e, m, left, right, ratio)


def own_kernel(u_ref, e_ref, m_ref, a_ref, left_ref, right_ref, x_ref, top_ref, bottom_ref, est_ref, out_ref, kept):
    step = pl.program_id(0)
    inner = kept.shape[1] // 8

    @pl.when(step < inner)
    def _():
        rows = pl.ds(pl.multiple_of(step * 8, 8), 8)
        kept[:, rows, :] = spread_tile(x_ref[...], left_ref[0], right_ref[0], u_ref[...], e_ref[...], m_ref[...])

    @pl.when(step >= inner)
    def _():
        first = pl.multiple_of((step - inner) * 8, 8)
        table = a_ref[...]
        for z in range(8):
            x = jnp.concatenate([top_ref[z], kept[first + z], bottom_ref[z]], axis=0)
            out_ref[z] = est_ref[z] * along(table, x)


def own_update(u, e, m, a, left, right, ratio, top, bottom, est):
    rows, depth, cols = ratio.shape
    inner = rows // 8 - 4
    early = lambda i: (jnp.minimum(i, inner - 1) + 2, 0, 0)
    late = lambda i: (jnp.maximum(i - inner, 0), 0, 0)
    return pl.pallas_call(
        own_kernel,
        grid=(inner + depth // 8,),
        in_specs=[whole(u), whole(e), whole(m), whole(a)]
        + [pl.BlockSpec((1, depth, 128), early)] * 2
        + [pl.BlockSpec((8, depth, cols), early)]
        + [pl.BlockSpec((8, 16, cols), late)] * 2
        + [pl.BlockSpec((8, rows, cols), late)],
        out_specs=pl.BlockSpec((8, rows, cols), late),
        out_shape=jax.ShapeDtypeStruct(est.shape, F32),
        scratch_shapes=[pltpu.VMEM((depth, rows - 32, cols), F32)],
        **params(16, 8),
    )(u, e, m, a, left, right, ratio, top, bottom, est)


def edge_kernel(a_ref, up_ref, down_ref, est_ref, part_ref, out_ref):
    side = pl.program_id(0)
    for s, x_ref in ((0, up_ref), (1, down_ref)):

        @pl.when(side == s)
        def _(x_ref=x_ref):
            table = a_ref[0]
            for z in range(est_ref.shape[0]):
                out_ref[z] = part_ref[z] + est_ref[z] * along(table, x_ref[z])


def edge_update(a, up, down, est, part):
    depth, rows, cols = est.shape
    step, chunk = rows // 16 - 1, depth
    last = depth // chunk - 1
    tile = pl.BlockSpec((chunk, 16, cols), lambda s, i: (i, s * step, 0))
    return pl.pallas_call(
        edge_kernel,
        grid=(2, depth // chunk),
        in_specs=[pl.BlockSpec((1, 16, 48), lambda s, i: (s, 0, 0))]
        + [pl.BlockSpec((chunk, 16, cols), lambda s, i: (i + (last - i) * s, 0, 0))]
        + [pl.BlockSpec((chunk, 16, cols), lambda s, i: (i * s, 0, 0))]
        + [tile, tile],
        out_specs=tile,
        out_shape=jax.ShapeDtypeStruct(est.shape, F32),
        input_output_aliases={4: 0},
        **params(20, 3),
    )(a, up, down, est, part)


def send(x, axis, d):
    return lax.ppermute(x, AXES, shift_perm(axis, d))


def column_edges(left, right):
    return send(right, "gy", 1), send(left, "gy", -1)


def place():
    gx, gy = lax.axis_index("gx"), lax.axis_index("gy")
    return gx >> 2, gx & 3, gy >> 1, gy & 1


HBM = pl.BlockSpec(memory_space=pltpu.HBM)
ANY = pl.BlockSpec(memory_space=pl.ANY)


def run_copies(pairs, sems):
    copies = [pltpu.make_async_copy(src, dst, sems.at[n]) for n, (src, dst) in enumerate(pairs)]
    for copy in copies:
        copy.start()
    for copy in copies:
        copy.wait()


def copy_call(body, count, shapes, inputs, us):
    return pl.pallas_call(
        body,
        in_specs=[HBM] * len(inputs),
        out_specs=[pl.BlockSpec(memory_space=pltpu.VMEM)] * len(shapes),
        out_shape=[jax.ShapeDtypeStruct(s, F32) for s in shapes],
        scratch_shapes=[pltpu.SemaphoreType.DMA((count,))],
        **params(16, us),
    )(*inputs)


def column_ends(est, after):
    def body(*refs):
        est_ref, left_ref, right_ref = refs[-3:]
        for g in range(left_ref.shape[0]):
            left_ref[g], right_ref[g] = packed([est_ref[8 * g + q] for q in range(8)])

    depth, rows, _ = est.shape
    vmem = pl.BlockSpec(memory_space=pltpu.VMEM)
    return pl.pallas_call(
        body,
        in_specs=[ANY] * len(after) + [vmem],
        out_specs=[vmem] * 2,
        out_shape=[jax.ShapeDtypeStruct((depth // 8, rows, 128), F32)] * 2,
        **params(14, 2),
    )(*after, est)


def row_ends(est):
    def body(est_ref, top_ref, bottom_ref, sems):
        depth, rows, _ = est_ref.shape
        pairs = []
        for out, r in ((top_ref, 0), (bottom_ref, rows - 16)):
            for d in range(0, depth, 16):
                pairs.append((est_ref.at[pl.ds(d, 16), pl.ds(r, 16)], out.at[pl.ds(d, 16)]))
        run_copies(pairs, sems)

    depth, _, cols = est.shape
    return copy_call(body, depth // 8, [(depth, 16, cols)] * 2, (est,), 2)


def halves_of(measured, rows, after):
    def body(*refs):
        measured_ref, near_ref, far_ref, sems = refs[-4:]
        x, y, z, c = place()
        pairs = []
        for out, core in ((near_ref, c), (far_ref, 1 - c)):
            for k in range(8):
                tx, ty = target_of(x, y, z, core, k)
                pairs.append((measured_ref.at[:, tx * 4 + ty], out.at[k]))
        run_copies(pairs, sems)

    return copy_call(body, 16, [(8, 8, rows, 128)] * 2, (*after, measured.reshape(8, 16, rows, 128)), 2)


def pieces_of(near, far, steps, after):
    def body(*refs):
        near_ref, far_ref, *outs = refs[len(after) : -1]
        sems = refs[-1]
        pairs = []
        for k, out in zip(steps, outs):
            pairs.append((near_ref.at[k], out.at[0]))
            pairs.append((far_ref.at[k], out.at[1]))
        run_copies(pairs, sems)

    shapes = [(2, *near.shape[1:])] * len(steps)
    return copy_call(body, 2 * len(steps), shapes, (*after, near, far), 2)


def diagonal_windows(r_interp, gx, rows):
    total = r_interp.shape[0]
    first = jnp.clip(gx * rows - 64, 0, total - 192)
    band = lax.dynamic_slice(r_interp, (first, 0), (192, total))
    i = lax.broadcasted_iota(jnp.int32, (192, total), 0) + first
    j = lax.broadcasted_iota(jnp.int32, (192, total), 1)
    main = jnp.sum(jnp.where(i == j, band, 0.0), axis=0)
    upper = jnp.sum(jnp.where(i + 1 == j, band, 0.0), axis=0)
    window = lambda v: lax.dynamic_slice(jnp.pad(v, (16, 48)), (gx * rows,), (128,))
    return window(main), window(upper)


def forward(tables, up, estimate, down, left, right, above, below, after):
    mixed, edge = row_mix(tables[0], up, estimate, down, left, right, above, below, after)
    return blur(tables[3], tables[4], tables[7], edge, mixed)


def backward(tables, ratio, left, right, estimate, column_edges, row_edges):
    rb, re, ub, ube, zb = tables[1], tables[2], tables[5], tables[6], tables[8]
    left, right = column_edges(left, right)
    top, bottom = spread_ends(ub, ube, zb, left, right, ratio)
    up, down = row_edges(top, bottom)
    part = own_update(ub, ube, zb, rb, left, right, ratio, top, bottom, estimate)
    return edge_update(re, up, down, estimate, part)


def shards(estimate, measured, z_interp, r_interp, psf_z, psf_r, psf_u):
    depth, rows, width = estimate.shape
    gx = lax.axis_index("gx")
    row_edges = lambda top, bottom: (send(bottom, "gx", 1), send(top, "gx", -1))
    top, bottom = row_ends(estimate)
    up, down = row_edges(top, bottom)
    ends = column_ends(estimate, (top,))
    left, right = column_edges(*ends)
    near, far = halves_of(measured, rows, ends[:1])
    far = lax.ppermute(far, AXES, core_swap())
    both = jnp.concatenate([left, right], axis=2)
    above, below = row_edges(both[:, :16], both[:, rows - 16 :])
    main, upper = diagonal_windows(r_interp, gx, rows)
    tables = make_tables(psf_z, psf_r, psf_u, z_interp, main, upper, rows, width)
    first, second = range(3), range(3, 8)
    ship = lambda parts, steps: [lax.ppermute(p, AXES, piece_perm(k)) for p, k in zip(parts, steps)]
    pieces = ship(pieces_of(near, far, first, (above, below, tables[0], up, down)), first)
    pieces += ship(pieces_of(near, far, second, (tables[0],)), second)
    blurred = forward(tables, up, estimate, down, left, right, above, below, pieces[:3])
    ratio, left, right = ratio_of(blurred, pieces)
    return backward(tables, ratio, left, right, estimate, column_edges, row_edges)


def solution(mesh):
    in_specs = (P(None, "gx", "gy"), P("gy", None, "gx"), P(), P(), P(), P(), P())
    out_specs = P(None, "gx", "gy")
    return jax.shard_map(shards, mesh=mesh, in_specs=in_specs, out_specs=out_specs, check_vma=False)
```

```python
import functools

import jax
import jax.numpy as jnp
from jax import lax
from jax.experimental import pallas as pl
from jax.experimental.pallas import tpu as pltpu
from jax.sharding import PartitionSpec as P

background = 0.25
HIGH = lax.Precision.HIGHEST
F32 = jnp.float32
BF = jnp.bfloat16
AXES = ("gx", "gy")
MIB = 1024 * 1024


def split(x):
    hi = x.astype(BF)
    return hi, (x - hi.astype(F32)).astype(BF)


def dot(a, b):
    return jnp.dot(a, b, preferred_element_type=F32)


def thrice(a, b):
    (ah, al), (bh, bl) = a, b
    return dot(jnp.concatenate([ah, ah, al], axis=1), jnp.concatenate([bh, bl, bh], axis=0))


def shift_perm(axis_of, d):
    if axis_of == "gx":
        return [(i * 8 + j, (i + d) * 8 + j) for i in range(16) for j in range(8) if 0 <= i + d < 16]
    return [(i * 8 + j, i * 8 + j + d) for i in range(16) for j in range(8) if 0 <= j + d < 8]


def position(x, y, z, c):
    return ((x % 4) * 4 + y % 4) * 8 + (z % 4) * 2 + c % 2


def core_swap():
    return [(d, d ^ 1) for d in range(128)]


def target_of(x, y, z, c, k):
    k1, k2 = k // 2, k % 2
    side, half = y >> 1, y & 1
    return (x + z + 2 * c + 2 * side + k1) & 3, 2 * (half ^ k2) + c


def source_of(x, y, z, c, k):
    k1, k2 = k // 2, k % 2
    core = y & 1
    return (x - z - 2 * core - 2 * c - k1) & 3, core, (y >> 1) ^ k2


def piece_perm(k):
    pairs = []
    for x in range(4):
        for y in range(4):
            for z in range(4):
                for c in range(2):
                    tx, ty = target_of(x, y, z, c, k)
                    pairs.append((position(x, y, z, c), position(tx, ty, x, y // 2)))
    return pairs


def params(mib, us):
    return dict(
        compiler_params=pltpu.CompilerParams(vmem_limit_bytes=mib * MIB),
        cost_estimate=pl.CostEstimate(flops=0, transcendentals=0, bytes_accessed=us * 3_000_000),
    )


def table_kernel(pz_ref, pr_ref, pu_ref, zi_ref, main_ref, upper_ref, *outs):
    ro_ref, rb_ref, re_ref, uo_ref, uoe_ref, ub_ref, ube_ref, zo_ref, zb_ref = outs

    def grid_of(rows, cols):
        return (
            lax.broadcasted_iota(jnp.int32, (rows, cols), 0),
            lax.broadcasted_iota(jnp.int32, (rows, cols), 1),
        )

    def taps(ref, distance):
        total = jnp.zeros(distance.shape, F32)
        for k in range(32):
            total = jnp.where(distance == k, ref[k], total)
        return total

    def left_table(value):
        h, l = split(value)
        return jnp.concatenate([h, h, l], axis=1)

    def right_table(value):
        h, l = split(value)
        return jnp.concatenate([h, l, h], axis=0)

    rows = rb_ref.shape[0]
    i, j = grid_of(rows, 128)
    main, upper = main_ref[...], upper_ref[...]
    out = taps(pr_ref, j - i) * main + taps(pr_ref, j - 1 - i) * upper
    ro_ref[...] = left_table(out[:, : rows + 32])
    i, j = grid_of(128, 128)
    back = (taps(pr_ref, j - i + 16) * main + taps(pr_ref, j - i + 15) * upper).T[16 : 16 + rows]
    rb_ref[...] = left_table(back[:, 16 : 16 + rows])
    re_ref[0] = left_table(back[:16, :16])
    re_ref[1] = left_table(back[rows - 16 :, rows + 16 : rows + 32])

    width = uo_ref.shape[1]
    i, j = grid_of(width, width)
    uo_ref[...] = right_table(taps(pu_ref, i + 16 - j))
    ub_ref[...] = right_table(taps(pu_ref, j - i + 16))
    a, b = i % 16, j % 16
    same = i // 16 == j // 16
    left = i < 128
    uoe_ref[...] = right_table(jnp.where(same, taps(pu_ref, jnp.where(left, a - b, a - b + 32)), 0.0))
    ube_ref[...] = right_table(jnp.where(same, taps(pu_ref, jnp.where(left, b - a + 32, b - a)), 0.0))

    depth = zi_ref.shape[0]
    i, j = grid_of(depth, depth)
    mix = jnp.dot(taps(pz_ref, j - i + 16), zi_ref[...], precision=HIGH, preferred_element_type=F32)
    zo_ref[...] = left_table(mix)
    zb_ref[...] = left_table(mix.T)


def make_tables(psf_z, psf_r, psf_u, z_interp, main, upper, rows, width):
    depth = z_interp.shape[0]
    shapes = [(rows, 3 * (rows + 32)), (rows, 3 * rows), (2, 16, 48)] + [(3 * width, width)] * 4
    shapes += [(depth, 3 * depth)] * 2
    smem = pl.BlockSpec(memory_space=pltpu.SMEM)
    vmem = pl.BlockSpec(memory_space=pltpu.VMEM)
    return pl.pallas_call(
        table_kernel,
        in_specs=[smem] * 3 + [vmem] * 3,
        out_specs=[vmem] * len(shapes),
        out_shape=[jax.ShapeDtypeStruct(s, BF) for s in shapes],
        **params(8, 3),
    )(psf_z, psf_r, psf_u, z_interp, main[None], upper[None])


def packed(planes):
    lane = lax.broadcasted_iota(jnp.int32, planes[0][:, :128].shape, 1) // 16
    left = right = None
    for q, x in enumerate(planes):
        a, b = x[:, :128], x[:, x.shape[1] - 128 :]
        a = pltpu.roll(a, 16 * q, 1) if q else a
        b = pltpu.roll(b, (16 * q + 16) % 128, 1) if q != 7 else b
        left = a if q == 0 else jnp.where(lane == q, a, left)
        right = b if q == 0 else jnp.where(lane == q, b, right)
    return left, right


def edge_sums(both, table):
    total = across(both, table)
    return total[:, :128], total[:, 128:]


def unpacked(left, right, q):
    lane = lax.broadcasted_iota(jnp.int32, left.shape, 1)
    a = pltpu.roll(left, (128 - 16 * q) % 128, 1) if q else left
    b = pltpu.roll(right, 112 - 16 * q, 1) if q != 7 else right
    return jnp.concatenate([jnp.where(lane < 16, a, 0.0), jnp.where(lane >= 112, b, 0.0)], axis=1)


def across(x, table):
    h, l = split(x)
    return dot(jnp.concatenate([h, h, l], axis=1), table)


def along(table, x):
    h, l = split(x)
    return dot(table, jnp.concatenate([h, l, h], axis=0))


def whole(t):
    return pl.BlockSpec(t.shape, lambda i: (0,) * t.ndim)


def row_kernel(table_ref, own_ref, left_ref, right_ref, *refs):
    up_ref, down_ref, up_edge_ref, down_edge_ref = refs[:4]
    out_ref, edge_ref = refs[-2:]
    table = table_ref[...]
    for z in range(8):
        out_ref[z] = along(table, jnp.concatenate([up_ref[z], own_ref[z], down_ref[z]], axis=0))
    both = jnp.concatenate([left_ref[0], right_ref[0]], axis=1)
    edge_ref[0] = along(table, jnp.concatenate([up_edge_ref[0], both, down_edge_ref[0]], axis=0))


def row_mix(table, up, own, down, left, right, above, below, after):
    depth, rows, cols = own.shape
    groups = depth // 8
    block = lambda d, r: pl.BlockSpec((d, r, cols), lambda i: (i, 0, 0))
    packs = pl.BlockSpec((1, rows, 128), lambda i: (i, 0, 0))
    return pl.pallas_call(
        row_kernel,
        grid=(groups,),
        in_specs=[whole(table), block(8, rows), packs, packs, block(8, 16), block(8, 16), block(1, 16), block(1, 16)]
        + [ANY] * len(after),
        out_specs=[block(8, rows), block(1, rows)],
        out_shape=[jax.ShapeDtypeStruct(own.shape, F32), jax.ShapeDtypeStruct((groups, rows, cols), F32)],
        **params(10, 4),
    )(table, own, left, right, up, down, above, below, *after)


def blur_kernel(u_ref, e_ref, m_ref, edge_ref, x_ref, out_ref):
    depth, rows, cols = x_ref.shape
    total = across(x_ref[...].reshape(depth * rows, cols), u_ref[...]).reshape(depth, rows, cols)
    groups = depth // 8
    left, right = edge_sums(edge_ref[...].reshape(groups * rows, cols), e_ref[...])
    left, right = left.reshape(groups, rows, 128), right.reshape(groups, rows, 128)
    extra = [unpacked(left[g], right[g], q) for g in range(groups) for q in range(8)]
    total = jnp.transpose(total + jnp.stack(extra), (1, 0, 2))
    table = m_ref[...]
    for r in range(rows):
        out_ref[r] = along(table, total[r])


def blur(u, e, m, edge, x):
    depth, rows, cols = x.shape
    block = lambda d, c: pl.BlockSpec((d, 8, c), lambda i: (0, i, 0))
    return pl.pallas_call(
        blur_kernel,
        grid=(rows // 8,),
        in_specs=[whole(u), whole(e), whole(m), block(depth // 8, cols), block(depth, cols)],
        out_specs=pl.BlockSpec((8, depth, cols), lambda i: (i, 0, 0)),
        out_shape=jax.ShapeDtypeStruct((rows, depth, cols), F32),
        **params(14, 8),
    )(u, e, m, edge, x)


def ratio_kernel(blur_ref, *refs):
    pieces, (out_ref, top_ref, bottom_ref, left_ref, right_ref) = refs[:-5], refs[-5:]
    for k, piece in enumerate(pieces):
        pair, core, half = source_of(*place(), k)
        cols = pl.ds(pl.multiple_of(half * 128, 128), 128)
        for part in range(2):
            planes = pl.ds(pl.multiple_of((pair * 2 + (core ^ part)) * 8, 8), 8)
            seen = jnp.transpose(piece[part], (1, 0, 2))
            out_ref[:, planes, cols] = seen / (blur_ref[:, planes, cols] + background)
    top_ref[...] = out_ref[:16]
    bottom_ref[...] = out_ref[out_ref.shape[0] - 16 :]
    for g in range(left_ref.shape[0]):
        left_ref[g], right_ref[g] = packed([out_ref[8 * g + q] for q in range(8)])


def ratio_of(blurred, pieces):
    rows, depth, cols = blurred.shape
    vmem = pl.BlockSpec(memory_space=pltpu.VMEM)
    shapes = [blurred.shape] + [(16, depth, cols)] * 2 + [(rows // 8, depth, 128)] * 2
    return pl.pallas_call(
        ratio_kernel,
        in_specs=[vmem] * (1 + len(pieces)),
        out_specs=[vmem] * 5,
        out_shape=[jax.ShapeDtypeStruct(s, F32) for s in shapes],
        **params(20, 7),
    )(blurred, *pieces)


def spread_tile(ratio, both, u, e, m):
    rows, depth, cols = ratio.shape
    total = across(ratio.reshape(rows * depth, cols), u).reshape(rows, depth, cols)
    left, right = edge_sums(both, e)
    planes = [along(m, total[q] + unpacked(left, right, q)) for q in range(rows)]
    return jnp.transpose(jnp.stack(planes), (1, 0, 2))


def own_kernel(u_ref, e_ref, m_ref, a_ref, both_ref, x_ref, est_ref, out_ref, kept):
    step = pl.program_id(0)
    half = kept.shape[1] // 8

    @pl.when(step < half)
    def _():
        rows = pl.ds(pl.multiple_of(step * 8, 8), 8)
        kept[:, rows, :] = spread_tile(x_ref[...], both_ref[0], u_ref[...], e_ref[...], m_ref[...])

    @pl.when(step >= half)
    def _():
        first = pl.multiple_of((step - half) * 16, 16)
        table = a_ref[...]
        for z in range(16):
            out_ref[z] = est_ref[z] * along(table, kept[first + z])


def own_update(u, e, m, a, both, ratio, est):
    rows, depth, cols = ratio.shape
    half = rows // 8
    early = lambda i: (jnp.minimum(i, half - 1), 0, 0)
    late = lambda i: (jnp.maximum(i - half, 0), 0, 0)
    return pl.pallas_call(
        own_kernel,
        grid=(half + depth // 16,),
        in_specs=[whole(u), whole(e), whole(m), whole(a)]
        + [pl.BlockSpec((1, depth, cols), early), pl.BlockSpec((8, depth, cols), early)]
        + [pl.BlockSpec((16, rows, cols), late)],
        out_specs=pl.BlockSpec((16, rows, cols), late),
        out_shape=jax.ShapeDtypeStruct(est.shape, F32),
        scratch_shapes=[pltpu.VMEM(est.shape, F32)],
        **params(18, 10),
    )(u, e, m, a, both, ratio, est)


def edge_kernel(u_ref, e_ref, m_ref, a_ref, above_ref, below_ref, up_ref, down_ref, est_ref, part_ref, out_ref, kept):
    side, step = pl.program_id(0), pl.program_id(1)
    rows = pl.ds(pl.multiple_of(step * 8, 8), 8)
    for s, x_ref, c_ref in ((0, up_ref, above_ref), (1, down_ref, below_ref)):

        @pl.when(side == s)
        def _(x_ref=x_ref, c_ref=c_ref):
            kept[:, rows, :] = spread_tile(x_ref[...], c_ref[0], u_ref[...], e_ref[...], m_ref[...])

    @pl.when(step == 1)
    def _():
        table = a_ref[0]
        for z in range(est_ref.shape[0]):
            out_ref[z] = part_ref[z] + est_ref[z] * along(table, kept[z])


def edge_update(u, e, m, a, above, below, up, down, est, part):
    depth, rows, cols = est.shape
    far = rows // 16 - 1
    tile = pl.BlockSpec((depth, 16, cols), lambda s, i: (0, s * far, 0))
    fixed = lambda t: pl.BlockSpec(t.shape, lambda s, i: (0,) * t.ndim)
    order = (lambda s, i: (jnp.maximum(i, s), 0, 0), lambda s, i: (i * s, 0, 0))
    return pl.pallas_call(
        edge_kernel,
        grid=(2, 2),
        in_specs=[fixed(u), fixed(e), fixed(m), pl.BlockSpec((1, 16, 48), lambda s, i: (s, 0, 0))]
        + [pl.BlockSpec((1, depth, cols), at) for at in order]
        + [pl.BlockSpec((8, depth, cols), at) for at in order]
        + [tile, tile],
        out_specs=tile,
        out_shape=jax.ShapeDtypeStruct(est.shape, F32),
        scratch_shapes=[pltpu.VMEM((depth, 16, cols), F32)],
        input_output_aliases={9: 0},
        **params(20, 6),
    )(u, e, m, a, above, below, up, down, est, part)


def send(x, axis, d):
    return lax.ppermute(x, AXES, shift_perm(axis, d))


def column_edges(left, right):
    return send(right, "gy", 1), send(left, "gy", -1)


def place():
    gx, gy = lax.axis_index("gx"), lax.axis_index("gy")
    return gx >> 2, gx & 3, gy >> 1, gy & 1


HBM = pl.BlockSpec(memory_space=pltpu.HBM)
ANY = pl.BlockSpec(memory_space=pl.ANY)


def run_copies(pairs, sems):
    copies = [pltpu.make_async_copy(src, dst, sems.at[n]) for n, (src, dst) in enumerate(pairs)]
    for copy in copies:
        copy.start()
    for copy in copies:
        copy.wait()


def copy_call(body, count, shapes, inputs, us):
    return pl.pallas_call(
        body,
        in_specs=[HBM] * len(inputs),
        out_specs=[pl.BlockSpec(memory_space=pltpu.VMEM)] * len(shapes),
        out_shape=[jax.ShapeDtypeStruct(s, F32) for s in shapes],
        scratch_shapes=[pltpu.SemaphoreType.DMA((count,))],
        **params(16, us),
    )(*inputs)


def column_ends(est, after):
    def body(*refs):
        est_ref, left_ref, right_ref = refs[-3:]
        for g in range(left_ref.shape[0]):
            left_ref[g], right_ref[g] = packed([est_ref[8 * g + q] for q in range(8)])

    depth, rows, _ = est.shape
    vmem = pl.BlockSpec(memory_space=pltpu.VMEM)
    return pl.pallas_call(
        body,
        in_specs=[ANY] * len(after) + [vmem],
        out_specs=[vmem] * 2,
        out_shape=[jax.ShapeDtypeStruct((depth // 8, rows, 128), F32)] * 2,
        **params(14, 2),
    )(*after, est)


def row_ends(est):
    def body(est_ref, top_ref, bottom_ref, sems):
        depth, rows, _ = est_ref.shape
        pairs = []
        for out, r in ((top_ref, 0), (bottom_ref, rows - 16)):
            for d in range(0, depth, 16):
                pairs.append((est_ref.at[pl.ds(d, 16), pl.ds(r, 16)], out.at[pl.ds(d, 16)]))
        run_copies(pairs, sems)

    depth, _, cols = est.shape
    return copy_call(body, depth // 8, [(depth, 16, cols)] * 2, (est,), 2)


def halves_of(measured, rows, after):
    def body(*refs):
        measured_ref, near_ref, far_ref, sems = refs[-4:]
        x, y, z, c = place()
        pairs = []
        for out, core in ((near_ref, c), (far_ref, 1 - c)):
            for k in range(8):
                tx, ty = target_of(x, y, z, core, k)
                pairs.append((measured_ref.at[:, tx * 4 + ty], out.at[k]))
        run_copies(pairs, sems)

    return copy_call(body, 16, [(8, 8, rows, 128)] * 2, (*after, measured.reshape(8, 16, rows, 128)), 2)


def pieces_of(near, far, steps, after):
    def body(*refs):
        near_ref, far_ref, *outs = refs[len(after) : -1]
        sems = refs[-1]
        pairs = []
        for k, out in zip(steps, outs):
            pairs.append((near_ref.at[k], out.at[0]))
            pairs.append((far_ref.at[k], out.at[1]))
        run_copies(pairs, sems)

    shapes = [(2, *near.shape[1:])] * len(steps)
    return copy_call(body, 2 * len(steps), shapes, (*after, near, far), 2)


def diagonal_windows(r_interp, gx, rows):
    total = r_interp.shape[0]
    first = jnp.clip(gx * rows - 64, 0, total - 192)
    band = lax.dynamic_slice(r_interp, (first, 0), (192, total))
    i = lax.broadcasted_iota(jnp.int32, (192, total), 0) + first
    j = lax.broadcasted_iota(jnp.int32, (192, total), 1)
    main = jnp.sum(jnp.where(i == j, band, 0.0), axis=0)
    upper = jnp.sum(jnp.where(i + 1 == j, band, 0.0), axis=0)
    window = lambda v: lax.dynamic_slice(jnp.pad(v, (16, 48)), (gx * rows,), (128,))
    return window(main), window(upper)


def forward(tables, up, estimate, down, left, right, above, below, after):
    mixed, edge = row_mix(tables[0], up, estimate, down, left, right, above, below, after)
    return blur(tables[3], tables[4], tables[7], edge, mixed)


def backward(tables, ratio, top, bottom, left, right, estimate, column_edges, row_edges):
    rb, re, ub, ube, zb = tables[1], tables[2], tables[5], tables[6], tables[8]
    up, down = row_edges(top, bottom)
    both = jnp.concatenate(column_edges(left, right), axis=2)
    above, below = row_edges(both[:2], both[both.shape[0] - 2 :])
    part = own_update(ub, ube, zb, rb, both, ratio, estimate)
    return edge_update(ub, ube, zb, re, above, below, up, down, estimate, part)


def shards(estimate, measured, z_interp, r_interp, psf_z, psf_r, psf_u):
    depth, rows, width = estimate.shape
    gx = lax.axis_index("gx")
    row_edges = lambda top, bottom: (send(bottom, "gx", 1), send(top, "gx", -1))
    top, bottom = row_ends(estimate)
    up, down = row_edges(top, bottom)
    ends = column_ends(estimate, (top,))
    left, right = column_edges(*ends)
    near, far = halves_of(measured, rows, ends[:1])
    far = lax.ppermute(far, AXES, core_swap())
    both = jnp.concatenate([left, right], axis=2)
    above, below = row_edges(both[:, :16], both[:, rows - 16 :])
    main, upper = diagonal_windows(r_interp, gx, rows)
    tables = make_tables(psf_z, psf_r, psf_u, z_interp, main, upper, rows, width)
    first, second = range(3), range(3, 8)
    ship = lambda parts, steps: [lax.ppermute(p, AXES, piece_perm(k)) for p, k in zip(parts, steps)]
    pieces = ship(pieces_of(near, far, first, (above, below, tables[0], up, down)), first)
    pieces += ship(pieces_of(near, far, second, (tables[0],)), second)
    blurred = forward(tables, up, estimate, down, left, right, above, below, pieces[:3])
    return backward(tables, *ratio_of(blurred, pieces), estimate, column_edges, row_edges)


def solution(mesh):
    in_specs = (P(None, "gx", "gy"), P("gy", None, "gx"), P(), P(), P(), P(), P())
    out_specs = P(None, "gx", "gy")
    return jax.shard_map(shards, mesh=mesh, in_specs=in_specs, out_specs=out_specs, check_vma=False)
```

```python
import functools

import jax
import jax.numpy as jnp
from jax import lax
from jax.experimental import pallas as pl
from jax.experimental.pallas import tpu as pltpu
from jax.sharding import PartitionSpec as P

background = 0.25
HIGH = lax.Precision.HIGHEST
F32 = jnp.float32
BF = jnp.bfloat16
AXES = ("gx", "gy")
MIB = 1024 * 1024


def split(x):
    hi = x.astype(BF)
    return hi, (x - hi.astype(F32)).astype(BF)


def dot(a, b):
    return jnp.dot(a, b, preferred_element_type=F32)


def thrice(a, b):
    (ah, al), (bh, bl) = a, b
    return dot(jnp.concatenate([ah, ah, al], axis=1), jnp.concatenate([bh, bl, bh], axis=0))


def shift_perm(axis_of, d):
    if axis_of == "gx":
        return [(i * 8 + j, (i + d) * 8 + j) for i in range(16) for j in range(8) if 0 <= i + d < 16]
    return [(i * 8 + j, i * 8 + j + d) for i in range(16) for j in range(8) if 0 <= j + d < 8]


def position(x, y, z, c):
    return ((x % 4) * 4 + y % 4) * 8 + (z % 4) * 2 + c % 2


def core_swap():
    return [(d, d ^ 1) for d in range(128)]


def target_of(x, y, z, c, k):
    k1, k2 = k // 2, k % 2
    side, half = y >> 1, y & 1
    return (x + z + 2 * c + 2 * side + k1) & 3, 2 * (half ^ k2) + c


def source_of(x, y, z, c, k):
    k1, k2 = k // 2, k % 2
    core = y & 1
    return (x - z - 2 * core - 2 * c - k1) & 3, core, (y >> 1) ^ k2


def piece_perm(k):
    pairs = []
    for x in range(4):
        for y in range(4):
            for z in range(4):
                for c in range(2):
                    tx, ty = target_of(x, y, z, c, k)
                    pairs.append((position(x, y, z, c), position(tx, ty, x, y // 2)))
    return pairs


def params(mib, us):
    return dict(
        compiler_params=pltpu.CompilerParams(vmem_limit_bytes=mib * MIB),
        cost_estimate=pl.CostEstimate(flops=0, transcendentals=0, bytes_accessed=us * 3_000_000),
    )


def table_kernel(pz_ref, pr_ref, pu_ref, zi_ref, main_ref, upper_ref, *outs):
    ro_ref, rb_ref, re_ref, uo_ref, uoe_ref, ub_ref, ube_ref, zo_ref, zb_ref = outs

    def grid_of(rows, cols):
        return (
            lax.broadcasted_iota(jnp.int32, (rows, cols), 0),
            lax.broadcasted_iota(jnp.int32, (rows, cols), 1),
        )

    def taps(ref, distance):
        total = jnp.zeros(distance.shape, F32)
        for k in range(32):
            total = jnp.where(distance == k, ref[k], total)
        return total

    def left_table(value):
        h, l = split(value)
        return jnp.concatenate([h, h, l], axis=1)

    def right_table(value):
        h, l = split(value)
        return jnp.concatenate([h, l, h], axis=0)

    rows = rb_ref.shape[0]
    i, j = grid_of(rows, 128)
    main, upper = main_ref[...], upper_ref[...]
    out = taps(pr_ref, j - i) * main + taps(pr_ref, j - 1 - i) * upper
    ro_ref[...] = left_table(out[:, : rows + 32])
    i, j = grid_of(128, 128)
    back = (taps(pr_ref, j - i + 16) * main + taps(pr_ref, j - i + 15) * upper).T[16 : 16 + rows]
    rb_ref[...] = left_table(back[:, 16 : 16 + rows])
    re_ref[0] = left_table(back[:16, :16])
    re_ref[1] = left_table(back[rows - 16 :, rows + 16 : rows + 32])

    width = uo_ref.shape[1]
    i, j = grid_of(width, width)
    uo_ref[...] = right_table(taps(pu_ref, i + 16 - j))
    ub_ref[...] = right_table(taps(pu_ref, j - i + 16))
    a, b = i % 16, j % 16
    same = i // 16 == j // 16
    left = i < 128
    uoe_ref[...] = right_table(jnp.where(same, taps(pu_ref, jnp.where(left, a - b, a - b + 32)), 0.0))
    ube_ref[...] = right_table(jnp.where(same, taps(pu_ref, jnp.where(left, b - a + 32, b - a)), 0.0))

    depth = zi_ref.shape[0]
    i, j = grid_of(depth, depth)
    mix = jnp.dot(taps(pz_ref, j - i + 16), zi_ref[...], precision=HIGH, preferred_element_type=F32)
    zo_ref[...] = left_table(mix)
    zb_ref[...] = left_table(mix.T)


def make_tables(psf_z, psf_r, psf_u, z_interp, main, upper, rows, width):
    depth = z_interp.shape[0]
    shapes = [(rows, 3 * (rows + 32)), (rows, 3 * rows), (2, 16, 48)] + [(3 * width, width)] * 4
    shapes += [(depth, 3 * depth)] * 2
    smem = pl.BlockSpec(memory_space=pltpu.SMEM)
    vmem = pl.BlockSpec(memory_space=pltpu.VMEM)
    return pl.pallas_call(
        table_kernel,
        in_specs=[smem] * 3 + [vmem] * 3,
        out_specs=[vmem] * len(shapes),
        out_shape=[jax.ShapeDtypeStruct(s, BF) for s in shapes],
        **params(8, 3),
    )(psf_z, psf_r, psf_u, z_interp, main[None], upper[None])


def packed(planes):
    lane = lax.broadcasted_iota(jnp.int32, planes[0][:, :128].shape, 1) // 16
    left = right = None
    for q, x in enumerate(planes):
        a, b = x[:, :128], x[:, x.shape[1] - 128 :]
        a = pltpu.roll(a, 16 * q, 1) if q else a
        b = pltpu.roll(b, (16 * q + 16) % 128, 1) if q != 7 else b
        left = a if q == 0 else jnp.where(lane == q, a, left)
        right = b if q == 0 else jnp.where(lane == q, b, right)
    return left, right


def edge_sums(both, table):
    total = across(both, table)
    return total[:, :128], total[:, 128:]


def unpacked(left, right, q):
    lane = lax.broadcasted_iota(jnp.int32, left.shape, 1)
    a = pltpu.roll(left, (128 - 16 * q) % 128, 1) if q else left
    b = pltpu.roll(right, 112 - 16 * q, 1) if q != 7 else right
    return jnp.concatenate([jnp.where(lane < 16, a, 0.0), jnp.where(lane >= 112, b, 0.0)], axis=1)


def across(x, table):
    h, l = split(x)
    return dot(jnp.concatenate([h, h, l], axis=1), table)


def along(table, x):
    h, l = split(x)
    return dot(table, jnp.concatenate([h, l, h], axis=0))


def whole(t):
    return pl.BlockSpec(t.shape, lambda i: (0,) * t.ndim)


def row_kernel(table_ref, own_ref, both_ref, *refs):
    up_ref, down_ref, up_edge_ref, down_edge_ref = refs[:4]
    out_ref, edge_ref = refs[-2:]
    table = table_ref[...]
    for z in range(8):
        out_ref[z] = along(table, jnp.concatenate([up_ref[z], own_ref[z], down_ref[z]], axis=0))
    edge_ref[0] = along(table, jnp.concatenate([up_edge_ref[0], both_ref[0], down_edge_ref[0]], axis=0))


def row_mix(table, up, own, down, both, above, below, after):
    depth, rows, cols = own.shape
    groups = depth // 8
    block = lambda d, r: pl.BlockSpec((d, r, cols), lambda i: (i, 0, 0))
    return pl.pallas_call(
        row_kernel,
        grid=(groups,),
        in_specs=[whole(table), block(8, rows), block(1, rows), block(8, 16), block(8, 16), block(1, 16), block(1, 16)]
        + [ANY] * len(after),
        out_specs=[block(8, rows), block(1, rows)],
        out_shape=[jax.ShapeDtypeStruct(own.shape, F32), jax.ShapeDtypeStruct((groups, rows, cols), F32)],
        **params(10, 4),
    )(table, own, both, up, down, above, below, *after)


def blur_kernel(u_ref, e_ref, m_ref, edge_ref, x_ref, out_ref):
    depth, rows, cols = x_ref.shape
    total = across(x_ref[...].reshape(depth * rows, cols), u_ref[...]).reshape(depth, rows, cols)
    groups = depth // 8
    left, right = edge_sums(edge_ref[...].reshape(groups * rows, cols), e_ref[...])
    left, right = left.reshape(groups, rows, 128), right.reshape(groups, rows, 128)
    extra = [unpacked(left[g], right[g], q) for g in range(groups) for q in range(8)]
    total = jnp.transpose(total + jnp.stack(extra), (1, 0, 2))
    table = m_ref[...]
    for r in range(rows):
        out_ref[r] = along(table, total[r])


def blur(u, e, m, edge, x):
    depth, rows, cols = x.shape
    block = lambda d, c: pl.BlockSpec((d, 8, c), lambda i: (0, i, 0))
    return pl.pallas_call(
        blur_kernel,
        grid=(rows // 8,),
        in_specs=[whole(u), whole(e), whole(m), block(depth // 8, cols), block(depth, cols)],
        out_specs=pl.BlockSpec((8, depth, cols), lambda i: (i, 0, 0)),
        out_shape=jax.ShapeDtypeStruct((rows, depth, cols), F32),
        **params(14, 8),
    )(u, e, m, edge, x)


def ratio_kernel(blur_ref, *refs):
    pieces, (out_ref, top_ref, bottom_ref, left_ref, right_ref) = refs[:-5], refs[-5:]
    for k, piece in enumerate(pieces):
        pair, core, half = source_of(*place(), k)
        cols = pl.ds(pl.multiple_of(half * 128, 128), 128)
        for part in range(2):
            planes = pl.ds(pl.multiple_of((pair * 2 + (core ^ part)) * 8, 8), 8)
            seen = jnp.transpose(piece[part], (1, 0, 2))
            out_ref[:, planes, cols] = seen / (blur_ref[:, planes, cols] + background)
    top_ref[...] = out_ref[:16]
    bottom_ref[...] = out_ref[out_ref.shape[0] - 16 :]
    for g in range(left_ref.shape[0]):
        left_ref[g], right_ref[g] = packed([out_ref[8 * g + q] for q in range(8)])


def ratio_of(blurred, pieces):
    rows, depth, cols = blurred.shape
    vmem = pl.BlockSpec(memory_space=pltpu.VMEM)
    shapes = [blurred.shape] + [(16, depth, cols)] * 2 + [(rows // 8, depth, 128)] * 2
    return pl.pallas_call(
        ratio_kernel,
        in_specs=[vmem] * (1 + len(pieces)),
        out_specs=[vmem] * 5,
        out_shape=[jax.ShapeDtypeStruct(s, F32) for s in shapes],
        **params(20, 7),
    )(blurred, *pieces)


def spread_tile(ratio, both, u, e, m):
    rows, depth, cols = ratio.shape
    total = across(ratio.reshape(rows * depth, cols), u).reshape(rows, depth, cols)
    left, right = edge_sums(both, e)
    planes = [along(m, total[q] + unpacked(left, right, q)) for q in range(rows)]
    return jnp.transpose(jnp.stack(planes), (1, 0, 2))


def own_kernel(u_ref, e_ref, m_ref, a_ref, both_ref, x_ref, est_ref, out_ref, kept):
    step = pl.program_id(0)
    half = kept.shape[1] // 8

    @pl.when(step < half)
    def _():
        rows = pl.ds(pl.multiple_of(step * 8, 8), 8)
        kept[:, rows, :] = spread_tile(x_ref[...], both_ref[0], u_ref[...], e_ref[...], m_ref[...])

    @pl.when(step >= half)
    def _():
        first = pl.multiple_of((step - half) * 16, 16)
        table = a_ref[...]
        for z in range(16):
            out_ref[z] = est_ref[z] * along(table, kept[first + z])


def own_update(u, e, m, a, both, ratio, est):
    rows, depth, cols = ratio.shape
    half = rows // 8
    early = lambda i: (jnp.minimum(i, half - 1), 0, 0)
    late = lambda i: (jnp.maximum(i - half, 0), 0, 0)
    return pl.pallas_call(
        own_kernel,
        grid=(half + depth // 16,),
        in_specs=[whole(u), whole(e), whole(m), whole(a)]
        + [pl.BlockSpec((1, depth, cols), early), pl.BlockSpec((8, depth, cols), early)]
        + [pl.BlockSpec((16, rows, cols), late)],
        out_specs=pl.BlockSpec((16, rows, cols), late),
        out_shape=jax.ShapeDtypeStruct(est.shape, F32),
        scratch_shapes=[pltpu.VMEM(est.shape, F32)],
        **params(18, 10),
    )(u, e, m, a, both, ratio, est)


def edge_kernel(u_ref, e_ref, m_ref, a_ref, above_ref, below_ref, up_ref, down_ref, est_ref, part_ref, out_ref, kept):
    side, step = pl.program_id(0), pl.program_id(1)
    rows = pl.ds(pl.multiple_of(step * 8, 8), 8)
    for s, x_ref, c_ref in ((0, up_ref, above_ref), (1, down_ref, below_ref)):

        @pl.when(side == s)
        def _(x_ref=x_ref, c_ref=c_ref):
            kept[:, rows, :] = spread_tile(x_ref[...], c_ref[0], u_ref[...], e_ref[...], m_ref[...])

    @pl.when(step == 1)
    def _():
        table = a_ref[0]
        for z in range(est_ref.shape[0]):
            out_ref[z] = part_ref[z] + est_ref[z] * along(table, kept[z])


def edge_update(u, e, m, a, above, below, up, down, est, part):
    depth, rows, cols = est.shape
    far = rows // 16 - 1
    tile = pl.BlockSpec((depth, 16, cols), lambda s, i: (0, s * far, 0))
    fixed = lambda t: pl.BlockSpec(t.shape, lambda s, i: (0,) * t.ndim)
    order = (lambda s, i: (jnp.maximum(i, s), 0, 0), lambda s, i: (i * s, 0, 0))
    return pl.pallas_call(
        edge_kernel,
        grid=(2, 2),
        in_specs=[fixed(u), fixed(e), fixed(m), pl.BlockSpec((1, 16, 48), lambda s, i: (s, 0, 0))]
        + [pl.BlockSpec((1, depth, cols), at) for at in order]
        + [pl.BlockSpec((8, depth, cols), at) for at in order]
        + [tile, tile],
        out_specs=tile,
        out_shape=jax.ShapeDtypeStruct(est.shape, F32),
        scratch_shapes=[pltpu.VMEM((depth, 16, cols), F32)],
        input_output_aliases={9: 0},
        **params(20, 6),
    )(u, e, m, a, above, below, up, down, est, part)


def send(x, axis, d):
    return lax.ppermute(x, AXES, shift_perm(axis, d))


def column_edges(left, right):
    return send(right, "gy", 1), send(left, "gy", -1)


def place():
    gx, gy = lax.axis_index("gx"), lax.axis_index("gy")
    return gx >> 2, gx & 3, gy >> 1, gy & 1


HBM = pl.BlockSpec(memory_space=pltpu.HBM)
ANY = pl.BlockSpec(memory_space=pl.ANY)


def run_copies(pairs, sems):
    copies = [pltpu.make_async_copy(src, dst, sems.at[n]) for n, (src, dst) in enumerate(pairs)]
    for copy in copies:
        copy.start()
    for copy in copies:
        copy.wait()


def copy_call(body, count, shapes, inputs, us, mib=16):
    return pl.pallas_call(
        body,
        in_specs=[HBM] * len(inputs),
        out_specs=[pl.BlockSpec(memory_space=pltpu.VMEM)] * len(shapes),
        out_shape=[jax.ShapeDtypeStruct(s, F32) for s in shapes],
        scratch_shapes=[pltpu.SemaphoreType.DMA((count,))],
        **params(mib, us),
    )(*inputs)


def column_ends(est, after):
    def body(*refs):
        est_ref, left_ref, right_ref = refs[-3:]
        for g in range(left_ref.shape[0]):
            left_ref[g], right_ref[g] = packed([est_ref[8 * g + q] for q in range(8)])

    depth, rows, _ = est.shape
    vmem = pl.BlockSpec(memory_space=pltpu.VMEM)
    return pl.pallas_call(
        body,
        in_specs=[ANY] * len(after) + [vmem],
        out_specs=[vmem] * 2,
        out_shape=[jax.ShapeDtypeStruct((depth // 8, rows, 128), F32)] * 2,
        **params(14, 2),
    )(*after, est)


def row_ends(est):
    def body(est_ref, top_ref, bottom_ref, sems):
        depth, rows, _ = est_ref.shape
        pairs = []
        for out, r in ((top_ref, 0), (bottom_ref, rows - 16)):
            for d in range(0, depth, 16):
                pairs.append((est_ref.at[pl.ds(d, 16), pl.ds(r, 16)], out.at[pl.ds(d, 16)]))
        run_copies(pairs, sems)

    depth, _, cols = est.shape
    return copy_call(body, depth // 8, [(depth, 16, cols)] * 2, (est,), 2, 50)


def join_edges(left, right, dim, n):
    def body(left_ref, right_ref, both_ref, first_ref, last_ref):
        both_ref[:, :, :128] = left_ref[...]
        both_ref[:, :, 128:] = right_ref[...]
        size = both_ref.shape[dim]
        for ref, start in ((first_ref, 0), (last_ref, size - n)):
            at = tuple(pl.ds(start, n) if d == dim else slice(None) for d in range(3))
            ref[...] = both_ref[at]

    shape = (*left.shape[:2], 256)
    part = tuple(n if d == dim else size for d, size in enumerate(shape))
    vmem = pl.BlockSpec(memory_space=pltpu.VMEM)
    return pl.pallas_call(
        body,
        in_specs=[vmem] * 2,
        out_specs=[vmem] * 3,
        out_shape=[jax.ShapeDtypeStruct(t, F32) for t in (shape, part, part)],
        **params(8, 1),
    )(left, right)


def halves_of(measured, rows, after):
    def body(*refs):
        measured_ref, near_ref, far_ref, sems = refs[-4:]
        x, y, z, c = place()
        pairs = []
        for out, core in ((near_ref, c), (far_ref, 1 - c)):
            for k in range(8):
                tx, ty = target_of(x, y, z, core, k)
                pairs.append((measured_ref.at[:, tx * 4 + ty], out.at[k]))
        run_copies(pairs, sems)

    return copy_call(body, 16, [(8, 8, rows, 128)] * 2, (*after, measured.reshape(8, 16, rows, 128)), 2)


def pieces_of(near, far, steps, after):
    def body(*refs):
        near_ref, far_ref, *outs = refs[len(after) : -1]
        sems = refs[-1]
        pairs = []
        for k, out in zip(steps, outs):
            pairs.append((near_ref.at[k], out.at[0]))
            pairs.append((far_ref.at[k], out.at[1]))
        run_copies(pairs, sems)

    shapes = [(2, *near.shape[1:])] * len(steps)
    return copy_call(body, 2 * len(steps), shapes, (*after, near, far), 2)


def diagonal_windows(r_interp, gx, rows):
    total = r_interp.shape[0]
    first = jnp.clip(gx * rows - 64, 0, total - 192)
    band = lax.dynamic_slice(r_interp, (first, 0), (192, total))
    i = lax.broadcasted_iota(jnp.int32, (192, total), 0) + first
    j = lax.broadcasted_iota(jnp.int32, (192, total), 1)
    main = jnp.sum(jnp.where(i == j, band, 0.0), axis=0)
    upper = jnp.sum(jnp.where(i + 1 == j, band, 0.0), axis=0)
    window = lambda v: lax.dynamic_slice(jnp.pad(v, (16, 48)), (gx * rows,), (128,))
    return window(main), window(upper)


def forward(tables, up, estimate, down, both, above, below, after):
    mixed, edge = row_mix(tables[0], up, estimate, down, both, above, below, after)
    return blur(tables[3], tables[4], tables[7], edge, mixed)


def backward(tables, ratio, top, bottom, left, right, estimate, column_edges, row_edges):
    rb, re, ub, ube, zb = tables[1], tables[2], tables[5], tables[6], tables[8]
    up, down = row_edges(top, bottom)
    both, first, last = join_edges(*column_edges(left, right), 0, 2)
    above, below = row_edges(first, last)
    part = own_update(ub, ube, zb, rb, both, ratio, estimate)
    return edge_update(ub, ube, zb, re, above, below, up, down, estimate, part)


def shards(estimate, measured, z_interp, r_interp, psf_z, psf_r, psf_u):
    depth, rows, width = estimate.shape
    gx = lax.axis_index("gx")
    row_edges = lambda top, bottom: (send(bottom, "gx", 1), send(top, "gx", -1))
    top, bottom = row_ends(estimate)
    up, down = row_edges(top, bottom)
    ends = column_ends(estimate, (top,))
    left, right = column_edges(*ends)
    near, far = halves_of(measured, rows, ends[:1])
    far = lax.ppermute(far, AXES, core_swap())
    both, first, last = join_edges(left, right, 1, 16)
    above, below = row_edges(first, last)
    main, upper = diagonal_windows(r_interp, gx, rows)
    tables = make_tables(psf_z, psf_r, psf_u, z_interp, main, upper, rows, width)
    first, second = range(3), range(3, 8)
    ship = lambda parts, steps: [lax.ppermute(p, AXES, piece_perm(k)) for p, k in zip(parts, steps)]
    pieces = ship(pieces_of(near, far, first, (above, below, tables[0], up, down)), first)
    pieces += ship(pieces_of(near, far, second, (tables[0],)), second)
    blurred = forward(tables, up, estimate, down, both, above, below, pieces[:3])
    return backward(tables, *ratio_of(blurred, pieces), estimate, column_edges, row_edges)


def solution(mesh):
    in_specs = (P(None, "gx", "gy"), P("gy", None, "gx"), P(), P(), P(), P(), P())
    out_specs = P(None, "gx", "gy")
    return jax.shard_map(shards, mesh=mesh, in_specs=in_specs, out_specs=out_specs, check_vma=False)
```

```python
import functools

import jax
import jax.numpy as jnp
from jax import lax
from jax.experimental import pallas as pl
from jax.experimental.pallas import tpu as pltpu
from jax.sharding import PartitionSpec as P

background = 0.25
HIGH = lax.Precision.HIGHEST
F32 = jnp.float32
BF = jnp.bfloat16
AXES = ("gx", "gy")
MIB = 1024 * 1024


def split(x):
    hi = x.astype(BF)
    return hi, (x - hi.astype(F32)).astype(BF)


def dot(a, b):
    return jnp.dot(a, b, preferred_element_type=F32)


def thrice(a, b):
    (ah, al), (bh, bl) = a, b
    return dot(jnp.concatenate([ah, ah, al], axis=1), jnp.concatenate([bh, bl, bh], axis=0))


def shift_perm(axis_of, d):
    if axis_of == "gx":
        return [(i * 8 + j, (i + d) * 8 + j) for i in range(16) for j in range(8) if 0 <= i + d < 16]
    return [(i * 8 + j, i * 8 + j + d) for i in range(16) for j in range(8) if 0 <= j + d < 8]


def position(x, y, z, c):
    return ((x % 4) * 4 + y % 4) * 8 + (z % 4) * 2 + c % 2


def core_swap():
    return [(d, d ^ 1) for d in range(128)]


def target_of(x, y, z, c, k):
    k1, k2 = k // 2, k % 2
    side, half = y >> 1, y & 1
    return (x + z + 2 * c + 2 * side + k1) & 3, 2 * (half ^ k2) + c


def source_of(x, y, z, c, k):
    k1, k2 = k // 2, k % 2
    core = y & 1
    return (x - z - 2 * core - 2 * c - k1) & 3, core, (y >> 1) ^ k2


def piece_perm(k):
    pairs = []
    for x in range(4):
        for y in range(4):
            for z in range(4):
                for c in range(2):
                    tx, ty = target_of(x, y, z, c, k)
                    pairs.append((position(x, y, z, c), position(tx, ty, x, y // 2)))
    return pairs


def params(mib, us):
    return dict(
        compiler_params=pltpu.CompilerParams(vmem_limit_bytes=mib * MIB),
        cost_estimate=pl.CostEstimate(flops=0, transcendentals=0, bytes_accessed=us * 3_000_000),
    )


def table_kernel(pz_ref, pr_ref, pu_ref, zi_ref, main_ref, upper_ref, *outs):
    ro_ref, rb_ref, re_ref, uo_ref, uoe_ref, ub_ref, ube_ref, zo_ref, zb_ref = outs

    def grid_of(rows, cols):
        return (
            lax.broadcasted_iota(jnp.int32, (rows, cols), 0),
            lax.broadcasted_iota(jnp.int32, (rows, cols), 1),
        )

    def taps(ref, distance):
        total = jnp.zeros(distance.shape, F32)
        for k in range(32):
            total = jnp.where(distance == k, ref[k], total)
        return total

    def left_table(value):
        h, l = split(value)
        return jnp.concatenate([h, h, l], axis=1)

    def right_table(value):
        h, l = split(value)
        return jnp.concatenate([h, l, h], axis=0)

    rows = rb_ref.shape[0]
    i, j = grid_of(rows, 128)
    main, upper = main_ref[...], upper_ref[...]
    out = taps(pr_ref, j - i) * main + taps(pr_ref, j - 1 - i) * upper
    ro_ref[...] = left_table(out[:, : rows + 32])
    i, j = grid_of(128, 128)
    back = (taps(pr_ref, j - i + 16) * main + taps(pr_ref, j - i + 15) * upper).T[16 : 16 + rows]
    rb_ref[...] = left_table(back[:, 16 : 16 + rows])
    re_ref[0] = left_table(back[:16, :16])
    re_ref[1] = left_table(back[rows - 16 :, rows + 16 : rows + 32])

    width = uo_ref.shape[1]
    i, j = grid_of(width, width)
    uo_ref[...] = right_table(taps(pu_ref, i + 16 - j))
    ub_ref[...] = right_table(taps(pu_ref, j - i + 16))
    a, b = i % 16, j % 16
    same = i // 16 == j // 16
    left = i < 128
    uoe_ref[...] = right_table(jnp.where(same, taps(pu_ref, jnp.where(left, a - b, a - b + 32)), 0.0))
    ube_ref[...] = right_table(jnp.where(same, taps(pu_ref, jnp.where(left, b - a + 32, b - a)), 0.0))

    depth = zi_ref.shape[0]
    i, j = grid_of(depth, depth)
    mix = jnp.dot(taps(pz_ref, j - i + 16), zi_ref[...], precision=HIGH, preferred_element_type=F32)
    zo_ref[...] = left_table(mix)
    zb_ref[...] = left_table(mix.T)


def make_tables(psf_z, psf_r, psf_u, z_interp, main, upper, rows, width):
    depth = z_interp.shape[0]
    shapes = [(rows, 3 * (rows + 32)), (rows, 3 * rows), (2, 16, 48)] + [(3 * width, width)] * 4
    shapes += [(depth, 3 * depth)] * 2
    smem = pl.BlockSpec(memory_space=pltpu.SMEM)
    vmem = pl.BlockSpec(memory_space=pltpu.VMEM)
    return pl.pallas_call(
        table_kernel,
        in_specs=[smem] * 3 + [vmem] * 3,
        out_specs=[vmem] * len(shapes),
        out_shape=[jax.ShapeDtypeStruct(s, BF) for s in shapes],
        **params(8, 3),
    )(psf_z, psf_r, psf_u, z_interp, main[None], upper[None])


def packed(planes):
    lane = lax.broadcasted_iota(jnp.int32, planes[0][:, :128].shape, 1) // 16
    left = right = None
    for q, x in enumerate(planes):
        a, b = x[:, :128], x[:, x.shape[1] - 128 :]
        a = pltpu.roll(a, 16 * q, 1) if q else a
        b = pltpu.roll(b, (16 * q + 16) % 128, 1) if q != 7 else b
        left = a if q == 0 else jnp.where(lane == q, a, left)
        right = b if q == 0 else jnp.where(lane == q, b, right)
    return left, right


def edge_sums(both, table):
    total = across(both, table)
    return total[:, :128], total[:, 128:]


def unpacked(left, right, q):
    lane = lax.broadcasted_iota(jnp.int32, left.shape, 1)
    a = pltpu.roll(left, (128 - 16 * q) % 128, 1) if q else left
    b = pltpu.roll(right, 112 - 16 * q, 1) if q != 7 else right
    return jnp.concatenate([jnp.where(lane < 16, a, 0.0), jnp.where(lane >= 112, b, 0.0)], axis=1)


def across(x, table):
    h, l = split(x)
    return dot(jnp.concatenate([h, h, l], axis=1), table)


def along(table, x):
    h, l = split(x)
    return dot(table, jnp.concatenate([h, l, h], axis=0))


def whole(t):
    return pl.BlockSpec(t.shape, lambda i: (0,) * t.ndim)


def row_kernel(table_ref, own_ref, both_ref, *refs):
    up_ref, down_ref, up_edge_ref, down_edge_ref = refs[:4]
    out_ref, edge_ref = refs[-2:]
    table = table_ref[...]
    for z in range(8):
        out_ref[z] = along(table, jnp.concatenate([up_ref[z], own_ref[z], down_ref[z]], axis=0))
    edge_ref[0] = along(table, jnp.concatenate([up_edge_ref[0], both_ref[0], down_edge_ref[0]], axis=0))


def row_mix(table, up, own, down, both, above, below, after):
    depth, rows, cols = own.shape
    groups = depth // 8
    block = lambda d, r: pl.BlockSpec((d, r, cols), lambda i: (i, 0, 0))
    return pl.pallas_call(
        row_kernel,
        grid=(groups,),
        in_specs=[whole(table), block(8, rows), block(1, rows), block(8, 16), block(8, 16), block(1, 16), block(1, 16)]
        + [ANY] * len(after),
        out_specs=[block(8, rows), block(1, rows)],
        out_shape=[jax.ShapeDtypeStruct(own.shape, F32), jax.ShapeDtypeStruct((groups, rows, cols), F32)],
        **params(10, 4),
    )(table, own, both, up, down, above, below, *after)


def blur_kernel(u_ref, e_ref, m_ref, edge_ref, x_ref, out_ref):
    depth, rows, cols = x_ref.shape
    total = across(x_ref[...].reshape(depth * rows, cols), u_ref[...]).reshape(depth, rows, cols)
    groups = depth // 8
    left, right = edge_sums(edge_ref[...].reshape(groups * rows, cols), e_ref[...])
    left, right = left.reshape(groups, rows, 128), right.reshape(groups, rows, 128)
    extra = [unpacked(left[g], right[g], q) for g in range(groups) for q in range(8)]
    total = jnp.transpose(total + jnp.stack(extra), (1, 0, 2))
    table = m_ref[...]
    for r in range(rows):
        out_ref[r] = along(table, total[r])


def blur(u, e, m, edge, x):
    depth, rows, cols = x.shape
    block = lambda d, c: pl.BlockSpec((d, 8, c), lambda i: (0, i, 0))
    return pl.pallas_call(
        blur_kernel,
        grid=(rows // 8,),
        in_specs=[whole(u), whole(e), whole(m), block(depth // 8, cols), block(depth, cols)],
        out_specs=pl.BlockSpec((8, depth, cols), lambda i: (i, 0, 0)),
        out_shape=jax.ShapeDtypeStruct((rows, depth, cols), F32),
        **params(14, 8),
    )(u, e, m, edge, x)


def ratio_kernel(blur_ref, *refs):
    pieces, (out_ref, top_ref, bottom_ref, left_ref, right_ref) = refs[:-5], refs[-5:]
    for k, piece in enumerate(pieces):
        pair, core, half = source_of(*place(), k)
        cols = pl.ds(pl.multiple_of(half * 128, 128), 128)
        for part in range(2):
            planes = pl.ds(pl.multiple_of((pair * 2 + (core ^ part)) * 8, 8), 8)
            seen = jnp.transpose(piece[part], (1, 0, 2))
            out_ref[:, planes, cols] = seen / (blur_ref[:, planes, cols] + background)
    top_ref[...] = out_ref[:16]
    bottom_ref[...] = out_ref[out_ref.shape[0] - 16 :]
    for g in range(left_ref.shape[0]):
        left_ref[g], right_ref[g] = packed([out_ref[8 * g + q] for q in range(8)])


def ratio_of(blurred, pieces):
    rows, depth, cols = blurred.shape
    vmem = pl.BlockSpec(memory_space=pltpu.VMEM)
    shapes = [blurred.shape] + [(16, depth, cols)] * 2 + [(rows // 8, depth, 128)] * 2
    return pl.pallas_call(
        ratio_kernel,
        in_specs=[vmem] * (1 + len(pieces)),
        out_specs=[vmem] * 5,
        out_shape=[jax.ShapeDtypeStruct(s, F32) for s in shapes],
        **params(20, 7),
    )(blurred, *pieces)


def spread_tile(ratio, both, u, e, m):
    rows, depth, cols = ratio.shape
    total = across(ratio.reshape(rows * depth, cols), u).reshape(rows, depth, cols)
    left, right = edge_sums(both, e)
    planes = [along(m, total[q] + unpacked(left, right, q)) for q in range(rows)]
    return jnp.transpose(jnp.stack(planes), (1, 0, 2))


def own_kernel(u_ref, e_ref, m_ref, a_ref, both_ref, x_ref, est_ref, out_ref, kept):
    step = pl.program_id(0)
    half = kept.shape[1] // 8

    @pl.when(step < half)
    def _():
        rows = pl.ds(pl.multiple_of(step * 8, 8), 8)
        kept[:, rows, :] = spread_tile(x_ref[...], both_ref[0], u_ref[...], e_ref[...], m_ref[...])

    @pl.when(step >= half)
    def _():
        first = pl.multiple_of((step - half) * 16, 16)
        table = a_ref[...]
        for z in range(16):
            out_ref[z] = est_ref[z] * along(table, kept[first + z])


def own_update(u, e, m, a, both, ratio, est):
    rows, depth, cols = ratio.shape
    half = rows // 8
    early = lambda i: (jnp.minimum(i, half - 1), 0, 0)
    late = lambda i: (jnp.maximum(i - half, 0), 0, 0)
    return pl.pallas_call(
        own_kernel,
        grid=(half + depth // 16,),
        in_specs=[whole(u), whole(e), whole(m), whole(a)]
        + [pl.BlockSpec((1, depth, cols), early), pl.BlockSpec((8, depth, cols), early)]
        + [pl.BlockSpec((16, rows, cols), late)],
        out_specs=pl.BlockSpec((16, rows, cols), late),
        out_shape=jax.ShapeDtypeStruct(est.shape, F32),
        scratch_shapes=[pltpu.VMEM(est.shape, F32)],
        **params(18, 10),
    )(u, e, m, a, both, ratio, est)


def edge_kernel(u_ref, e_ref, m_ref, a_ref, above_ref, below_ref, up_ref, down_ref, est_ref, part_ref, out_ref, kept):
    side, step = pl.program_id(0), pl.program_id(1)
    rows = pl.ds(pl.multiple_of(step * 8, 8), 8)
    for s, x_ref, c_ref in ((0, up_ref, above_ref), (1, down_ref, below_ref)):

        @pl.when(side == s)
        def _(x_ref=x_ref, c_ref=c_ref):
            kept[:, rows, :] = spread_tile(x_ref[...], c_ref[0], u_ref[...], e_ref[...], m_ref[...])

    @pl.when(step == 1)
    def _():
        table = a_ref[0]
        for z in range(est_ref.shape[0]):
            out_ref[z] = part_ref[z] + est_ref[z] * along(table, kept[z])


def edge_update(u, e, m, a, above, below, up, down, est, part):
    depth, rows, cols = est.shape
    far = rows // 16 - 1
    tile = pl.BlockSpec((depth, 16, cols), lambda s, i: (0, s * far, 0))
    fixed = lambda t: pl.BlockSpec(t.shape, lambda s, i: (0,) * t.ndim)
    order = (lambda s, i: (jnp.maximum(i, s), 0, 0), lambda s, i: (i * s, 0, 0))
    return pl.pallas_call(
        edge_kernel,
        grid=(2, 2),
        in_specs=[fixed(u), fixed(e), fixed(m), pl.BlockSpec((1, 16, 48), lambda s, i: (s, 0, 0))]
        + [pl.BlockSpec((1, depth, cols), at) for at in order]
        + [pl.BlockSpec((8, depth, cols), at) for at in order]
        + [tile, tile],
        out_specs=tile,
        out_shape=jax.ShapeDtypeStruct(est.shape, F32),
        scratch_shapes=[pltpu.VMEM((depth, 16, cols), F32)],
        input_output_aliases={9: 0},
        **params(20, 6),
    )(u, e, m, a, above, below, up, down, est, part)


def send(x, axis, d):
    return lax.ppermute(x, AXES, shift_perm(axis, d))


def column_edges(left, right):
    return send(right, "gy", 1), send(left, "gy", -1)


def place():
    gx, gy = lax.axis_index("gx"), lax.axis_index("gy")
    return gx >> 2, gx & 3, gy >> 1, gy & 1


HBM = pl.BlockSpec(memory_space=pltpu.HBM)
ANY = pl.BlockSpec(memory_space=pl.ANY)


def run_copies(pairs, sems):
    copies = [pltpu.make_async_copy(src, dst, sems.at[n]) for n, (src, dst) in enumerate(pairs)]
    for copy in copies:
        copy.start()
    for copy in copies:
        copy.wait()


def copy_call(body, count, shapes, inputs, us, mib=16):
    return pl.pallas_call(
        body,
        in_specs=[HBM] * len(inputs),
        out_specs=[pl.BlockSpec(memory_space=pltpu.VMEM)] * len(shapes),
        out_shape=[jax.ShapeDtypeStruct(s, F32) for s in shapes],
        scratch_shapes=[pltpu.SemaphoreType.DMA((count,))],
        **params(mib, us),
    )(*inputs)


def column_ends(est, after):
    def body(*refs):
        est_ref, left_ref, right_ref = refs[-3:]
        for g in range(left_ref.shape[0]):
            left_ref[g], right_ref[g] = packed([est_ref[8 * g + q] for q in range(8)])

    depth, rows, _ = est.shape
    vmem = pl.BlockSpec(memory_space=pltpu.VMEM)
    return pl.pallas_call(
        body,
        in_specs=[ANY] * len(after) + [vmem],
        out_specs=[vmem] * 2,
        out_shape=[jax.ShapeDtypeStruct((depth // 8, rows, 128), F32)] * 2,
        **params(14, 2),
    )(*after, est)


def row_ends(est):
    def body(est_ref, top_ref, bottom_ref, sems):
        depth, rows, _ = est_ref.shape
        pairs = []
        for out, r in ((top_ref, 0), (bottom_ref, rows - 16)):
            for d in range(0, depth, 16):
                pairs.append((est_ref.at[pl.ds(d, 16), pl.ds(r, 16)], out.at[pl.ds(d, 16)]))
        run_copies(pairs, sems)

    depth, _, cols = est.shape
    return copy_call(body, depth // 8, [(depth, 16, cols)] * 2, (est,), 2, 50)


def join_edges(left, right, dim, n):
    def body(left_ref, right_ref, both_ref, first_ref, last_ref):
        both_ref[:, :, :128] = left_ref[...]
        both_ref[:, :, 128:] = right_ref[...]
        size = both_ref.shape[dim]
        for ref, start in ((first_ref, 0), (last_ref, size - n)):
            at = tuple(pl.ds(start, n) if d == dim else slice(None) for d in range(3))
            ref[...] = both_ref[at]

    shape = (*left.shape[:2], 256)
    part = tuple(n if d == dim else size for d, size in enumerate(shape))
    vmem = pl.BlockSpec(memory_space=pltpu.VMEM)
    return pl.pallas_call(
        body,
        in_specs=[vmem] * 2,
        out_specs=[vmem] * 3,
        out_shape=[jax.ShapeDtypeStruct(t, F32) for t in (shape, part, part)],
        **params(8, 1),
    )(left, right)


def halves_of(measured, rows, after):
    def body(*refs):
        measured_ref, near_ref, far_ref, sems = refs[-4:]
        x, y, z, c = place()
        pairs = []
        for out, core in ((near_ref, c), (far_ref, 1 - c)):
            for k in range(8):
                tx, ty = target_of(x, y, z, core, k)
                pairs.append((measured_ref.at[:, tx * 4 + ty], out.at[k]))
        run_copies(pairs, sems)

    return copy_call(body, 16, [(8, 8, rows, 128)] * 2, (*after, measured.reshape(8, 16, rows, 128)), 2)


def pieces_of(near, far, steps, after):
    def body(*refs):
        near_ref, far_ref, *outs = refs[len(after) : -1]
        sems = refs[-1]
        pairs = []
        for k, out in zip(steps, outs):
            pairs.append((near_ref.at[k], out.at[0]))
            pairs.append((far_ref.at[k], out.at[1]))
        run_copies(pairs, sems)

    shapes = [(2, *near.shape[1:])] * len(steps)
    return copy_call(body, 2 * len(steps), shapes, (*after, near, far), 2)


def diagonal_windows(r_interp, gx, rows):
    total = r_interp.shape[0]
    first = jnp.clip(gx * rows - 64, 0, total - 192)
    band = lax.dynamic_slice(r_interp, (first, 0), (192, total))
    i = lax.broadcasted_iota(jnp.int32, (192, total), 0) + first
    j = lax.broadcasted_iota(jnp.int32, (192, total), 1)
    main = jnp.sum(jnp.where(i == j, band, 0.0), axis=0)
    upper = jnp.sum(jnp.where(i + 1 == j, band, 0.0), axis=0)
    window = lambda v: lax.dynamic_slice(jnp.pad(v, (16, 48)), (gx * rows,), (128,))
    return window(main), window(upper)


def forward(tables, up, estimate, down, both, above, below, after):
    mixed, edge = row_mix(tables[0], up, estimate, down, both, above, below, after)
    return blur(tables[3], tables[4], tables[7], edge, mixed)


def backward(tables, ratio, top, bottom, left, right, estimate, column_edges, row_edges):
    rb, re, ub, ube, zb = tables[1], tables[2], tables[5], tables[6], tables[8]
    up, down = row_edges(top, bottom)
    both, first, last = join_edges(*column_edges(left, right), 0, 2)
    above, below = row_edges(first, last)
    part = own_update(ub, ube, zb, rb, both, ratio, estimate)
    return edge_update(ub, ube, zb, re, above, below, up, down, estimate, part)


def shards(estimate, measured, z_interp, r_interp, psf_z, psf_r, psf_u):
    depth, rows, width = estimate.shape
    gx = lax.axis_index("gx")
    row_edges = lambda top, bottom: (send(bottom, "gx", 1), send(top, "gx", -1))
    top, bottom = row_ends(estimate)
    up, down = row_edges(top, bottom)
    ends = column_ends(estimate, (top,))
    left, right = column_edges(*ends)
    near, far = halves_of(measured, rows, ends[:1])
    far = lax.ppermute(far, AXES, core_swap())
    both, first, last = join_edges(left, right, 1, 16)
    above, below = row_edges(first, last)
    main, upper = diagonal_windows(r_interp, gx, rows)
    tables = make_tables(psf_z, psf_r, psf_u, z_interp, main, upper, rows, width)
    first, second = range(5), range(5, 8)
    ship = lambda parts, steps: [lax.ppermute(p, AXES, piece_perm(k)) for p, k in zip(parts, steps)]
    pieces = ship(pieces_of(near, far, first, (above, below, tables[0], up, down)), first)
    blurred = forward(tables, up, estimate, down, both, above, below, pieces[:1])
    pieces += ship(pieces_of(near, far, second, (blurred,)), second)
    return backward(tables, *ratio_of(blurred, pieces), estimate, column_edges, row_edges)


def solution(mesh):
    in_specs = (P(None, "gx", "gy"), P("gy", None, "gx"), P(), P(), P(), P(), P())
    out_specs = P(None, "gx", "gy")
    return jax.shard_map(shards, mesh=mesh, in_specs=in_specs, out_specs=out_specs, check_vma=False)
```

```python
import functools

import jax
import jax.numpy as jnp
from jax import lax
from jax.experimental import pallas as pl
from jax.experimental.pallas import tpu as pltpu
from jax.sharding import PartitionSpec as P

background = 0.25
HIGH = lax.Precision.HIGHEST
F32 = jnp.float32
BF = jnp.bfloat16
AXES = ("gx", "gy")
MIB = 1024 * 1024


def split(x):
    hi = x.astype(BF)
    return hi, (x - hi.astype(F32)).astype(BF)


def dot(a, b):
    return jnp.dot(a, b, preferred_element_type=F32)


def thrice(a, b):
    (ah, al), (bh, bl) = a, b
    return dot(jnp.concatenate([ah, ah, al], axis=1), jnp.concatenate([bh, bl, bh], axis=0))


def shift_perm(axis_of, d):
    if axis_of == "gx":
        return [(i * 8 + j, (i + d) * 8 + j) for i in range(16) for j in range(8) if 0 <= i + d < 16]
    return [(i * 8 + j, i * 8 + j + d) for i in range(16) for j in range(8) if 0 <= j + d < 8]


def position(x, y, z, c):
    return ((x % 4) * 4 + y % 4) * 8 + (z % 4) * 2 + c % 2


def core_swap():
    return [(d, d ^ 1) for d in range(128)]


def target_of(x, y, z, c, k):
    k1, k2 = k // 2, k % 2
    side, half = y >> 1, y & 1
    return (x + z + 2 * c + 2 * side + k1) & 3, 2 * (half ^ k2 ^ (z & 1)) + c


def source_of(x, y, z, c, k):
    k1, k2 = k // 2, k % 2
    core = y & 1
    pair = (x - z - 2 * core - 2 * c - k1) & 3
    return pair, core, (y >> 1) ^ k2 ^ (pair & 1)


def piece_perm(k):
    pairs = []
    for x in range(4):
        for y in range(4):
            for z in range(4):
                for c in range(2):
                    tx, ty = target_of(x, y, z, c, k)
                    pairs.append((position(x, y, z, c), position(tx, ty, x, y // 2)))
    return pairs


def params(mib, us):
    return dict(
        compiler_params=pltpu.CompilerParams(vmem_limit_bytes=mib * MIB),
        cost_estimate=pl.CostEstimate(flops=0, transcendentals=0, bytes_accessed=us * 3_000_000),
    )


def table_kernel(pz_ref, pr_ref, pu_ref, zi_ref, main_ref, upper_ref, *outs):
    ro_ref, rb_ref, re_ref, uo_ref, uoe_ref, ub_ref, ube_ref, zo_ref, zb_ref = outs

    def grid_of(rows, cols):
        return (
            lax.broadcasted_iota(jnp.int32, (rows, cols), 0),
            lax.broadcasted_iota(jnp.int32, (rows, cols), 1),
        )

    def taps(ref, distance):
        total = jnp.zeros(distance.shape, F32)
        for k in range(32):
            total = jnp.where(distance == k, ref[k], total)
        return total

    def left_table(value):
        h, l = split(value)
        return jnp.concatenate([h, h, l], axis=1)

    def right_table(value):
        h, l = split(value)
        return jnp.concatenate([h, l, h], axis=0)

    rows = rb_ref.shape[0]
    i, j = grid_of(rows, 128)
    main, upper = main_ref[...], upper_ref[...]
    out = taps(pr_ref, j - i) * main + taps(pr_ref, j - 1 - i) * upper
    ro_ref[...] = left_table(out[:, : rows + 32])
    i, j = grid_of(128, 128)
    back = (taps(pr_ref, j - i + 16) * main + taps(pr_ref, j - i + 15) * upper).T[16 : 16 + rows]
    rb_ref[...] = left_table(back[:, 16 : 16 + rows])
    re_ref[0] = left_table(back[:16, :16])
    re_ref[1] = left_table(back[rows - 16 :, rows + 16 : rows + 32])

    width = uo_ref.shape[1]
    i, j = grid_of(width, width)
    uo_ref[...] = right_table(taps(pu_ref, i + 16 - j))
    ub_ref[...] = right_table(taps(pu_ref, j - i + 16))
    a, b = i % 16, j % 16
    same = i // 16 == j // 16
    left = i < 128
    uoe_ref[...] = right_table(jnp.where(same, taps(pu_ref, jnp.where(left, a - b, a - b + 32)), 0.0))
    ube_ref[...] = right_table(jnp.where(same, taps(pu_ref, jnp.where(left, b - a + 32, b - a)), 0.0))

    depth = zi_ref.shape[0]
    i, j = grid_of(depth, depth)
    mix = jnp.dot(taps(pz_ref, j - i + 16), zi_ref[...], precision=HIGH, preferred_element_type=F32)
    zo_ref[...] = left_table(mix)
    zb_ref[...] = left_table(mix.T)


def make_tables(psf_z, psf_r, psf_u, z_interp, main, upper, rows, width):
    depth = z_interp.shape[0]
    shapes = [(rows, 3 * (rows + 32)), (rows, 3 * rows), (2, 16, 48)] + [(3 * width, width)] * 4
    shapes += [(depth, 3 * depth)] * 2
    smem = pl.BlockSpec(memory_space=pltpu.SMEM)
    vmem = pl.BlockSpec(memory_space=pltpu.VMEM)
    return pl.pallas_call(
        table_kernel,
        in_specs=[smem] * 3 + [vmem] * 3,
        out_specs=[vmem] * len(shapes),
        out_shape=[jax.ShapeDtypeStruct(s, BF) for s in shapes],
        **params(8, 3),
    )(psf_z, psf_r, psf_u, z_interp, main[None], upper[None])


def packed(planes):
    lane = lax.broadcasted_iota(jnp.int32, planes[0][:, :128].shape, 1) // 16
    left = right = None
    for q, x in enumerate(planes):
        a, b = x[:, :128], x[:, x.shape[1] - 128 :]
        a = pltpu.roll(a, 16 * q, 1) if q else a
        b = pltpu.roll(b, (16 * q + 16) % 128, 1) if q != 7 else b
        left = a if q == 0 else jnp.where(lane == q, a, left)
        right = b if q == 0 else jnp.where(lane == q, b, right)
    return left, right


def edge_sums(both, table):
    total = across(both, table)
    return total[:, :128], total[:, 128:]


def unpacked(left, right, q):
    lane = lax.broadcasted_iota(jnp.int32, left.shape, 1)
    a = pltpu.roll(left, (128 - 16 * q) % 128, 1) if q else left
    b = pltpu.roll(right, 112 - 16 * q, 1) if q != 7 else right
    return jnp.concatenate([jnp.where(lane < 16, a, 0.0), jnp.where(lane >= 112, b, 0.0)], axis=1)


def across(x, table):
    h, l = split(x)
    return dot(jnp.concatenate([h, h, l], axis=1), table)


def along(table, x):
    h, l = split(x)
    return dot(table, jnp.concatenate([h, l, h], axis=0))


def whole(t):
    return pl.BlockSpec(t.shape, lambda i: (0,) * t.ndim)


def row_kernel(table_ref, own_ref, both_ref, *refs):
    up_ref, down_ref, up_edge_ref, down_edge_ref = refs[:4]
    out_ref, edge_ref = refs[-2:]
    table = table_ref[...]
    for z in range(8):
        out_ref[z] = along(table, jnp.concatenate([up_ref[z], own_ref[z], down_ref[z]], axis=0))
    edge_ref[0] = along(table, jnp.concatenate([up_edge_ref[0], both_ref[0], down_edge_ref[0]], axis=0))


def row_mix(table, up, own, down, both, above, below, after):
    depth, rows, cols = own.shape
    groups = depth // 8
    block = lambda d, r: pl.BlockSpec((d, r, cols), lambda i: (i, 0, 0))
    return pl.pallas_call(
        row_kernel,
        grid=(groups,),
        in_specs=[whole(table), block(8, rows), block(1, rows), block(8, 16), block(8, 16), block(1, 16), block(1, 16)]
        + [ANY] * len(after),
        out_specs=[block(8, rows), block(1, rows)],
        out_shape=[jax.ShapeDtypeStruct(own.shape, F32), jax.ShapeDtypeStruct((groups, rows, cols), F32)],
        **params(10, 4),
    )(table, own, both, up, down, above, below, *after)


def blur_kernel(u_ref, e_ref, m_ref, edge_ref, x_ref, out_ref):
    depth, rows, cols = x_ref.shape
    total = across(x_ref[...].reshape(depth * rows, cols), u_ref[...]).reshape(depth, rows, cols)
    groups = depth // 8
    left, right = edge_sums(edge_ref[...].reshape(groups * rows, cols), e_ref[...])
    left, right = left.reshape(groups, rows, 128), right.reshape(groups, rows, 128)
    extra = [unpacked(left[g], right[g], q) for g in range(groups) for q in range(8)]
    total = jnp.transpose(total + jnp.stack(extra), (1, 0, 2))
    table = m_ref[...]
    for r in range(rows):
        out_ref[r] = along(table, total[r])


def blur(u, e, m, edge, x):
    depth, rows, cols = x.shape
    block = lambda d, c: pl.BlockSpec((d, 8, c), lambda i: (0, i, 0))
    return pl.pallas_call(
        blur_kernel,
        grid=(rows // 8,),
        in_specs=[whole(u), whole(e), whole(m), block(depth // 8, cols), block(depth, cols)],
        out_specs=pl.BlockSpec((8, depth, cols), lambda i: (i, 0, 0)),
        out_shape=jax.ShapeDtypeStruct((rows, depth, cols), F32),
        **params(14, 8),
    )(u, e, m, edge, x)


def ratio_kernel(blur_ref, *refs):
    pieces, (out_ref, top_ref, bottom_ref, left_ref, right_ref) = refs[:-5], refs[-5:]
    for k, piece in enumerate(pieces):
        pair, core, half = source_of(*place(), k)
        cols = pl.ds(pl.multiple_of(half * 128, 128), 128)
        for part in range(2):
            planes = pl.ds(pl.multiple_of((pair * 2 + (core ^ part)) * 8, 8), 8)
            seen = jnp.transpose(piece[part], (1, 0, 2))
            out_ref[:, planes, cols] = seen / (blur_ref[:, planes, cols] + background)
    top_ref[...] = out_ref[:16]
    bottom_ref[...] = out_ref[out_ref.shape[0] - 16 :]
    for g in range(left_ref.shape[0]):
        left_ref[g], right_ref[g] = packed([out_ref[8 * g + q] for q in range(8)])


def ratio_of(blurred, pieces):
    rows, depth, cols = blurred.shape
    vmem = pl.BlockSpec(memory_space=pltpu.VMEM)
    shapes = [blurred.shape] + [(16, depth, cols)] * 2 + [(rows // 8, depth, 128)] * 2
    return pl.pallas_call(
        ratio_kernel,
        in_specs=[vmem] * (1 + len(pieces)),
        out_specs=[vmem] * 5,
        out_shape=[jax.ShapeDtypeStruct(s, F32) for s in shapes],
        **params(20, 7),
    )(blurred, *pieces)


def spread_tile(ratio, both, u, e, m):
    rows, depth, cols = ratio.shape
    total = across(ratio.reshape(rows * depth, cols), u).reshape(rows, depth, cols)
    left, right = edge_sums(both, e)
    planes = [along(m, total[q] + unpacked(left, right, q)) for q in range(rows)]
    return jnp.transpose(jnp.stack(planes), (1, 0, 2))


def own_kernel(u_ref, e_ref, m_ref, a_ref, both_ref, x_ref, est_ref, out_ref, kept):
    step = pl.program_id(0)
    half = kept.shape[1] // 8

    @pl.when(step < half)
    def _():
        rows = pl.ds(pl.multiple_of(step * 8, 8), 8)
        kept[:, rows, :] = spread_tile(x_ref[...], both_ref[0], u_ref[...], e_ref[...], m_ref[...])

    @pl.when(step >= half)
    def _():
        first = pl.multiple_of((step - half) * 16, 16)
        table = a_ref[...]
        for z in range(16):
            out_ref[z] = est_ref[z] * along(table, kept[first + z])


def own_update(u, e, m, a, both, ratio, est):
    rows, depth, cols = ratio.shape
    half = rows // 8
    early = lambda i: (jnp.minimum(i, half - 1), 0, 0)
    late = lambda i: (jnp.maximum(i - half, 0), 0, 0)
    return pl.pallas_call(
        own_kernel,
        grid=(half + depth // 16,),
        in_specs=[whole(u), whole(e), whole(m), whole(a)]
        + [pl.BlockSpec((1, depth, cols), early), pl.BlockSpec((8, depth, cols), early)]
        + [pl.BlockSpec((16, rows, cols), late)],
        out_specs=pl.BlockSpec((16, rows, cols), late),
        out_shape=jax.ShapeDtypeStruct(est.shape, F32),
        scratch_shapes=[pltpu.VMEM(est.shape, F32)],
        **params(18, 10),
    )(u, e, m, a, both, ratio, est)


def edge_kernel(u_ref, e_ref, m_ref, a_ref, above_ref, below_ref, up_ref, down_ref, est_ref, part_ref, out_ref, kept):
    side, step = pl.program_id(0), pl.program_id(1)
    rows = pl.ds(pl.multiple_of(step * 8, 8), 8)
    for s, x_ref, c_ref in ((0, up_ref, above_ref), (1, down_ref, below_ref)):

        @pl.when(side == s)
        def _(x_ref=x_ref, c_ref=c_ref):
            kept[:, rows, :] = spread_tile(x_ref[...], c_ref[0], u_ref[...], e_ref[...], m_ref[...])

    @pl.when(step == 1)
    def _():
        table = a_ref[0]
        for z in range(est_ref.shape[0]):
            out_ref[z] = part_ref[z] + est_ref[z] * along(table, kept[z])


def edge_update(u, e, m, a, above, below, up, down, est, part):
    depth, rows, cols = est.shape
    far = rows // 16 - 1
    tile = pl.BlockSpec((depth, 16, cols), lambda s, i: (0, s * far, 0))
    fixed = lambda t: pl.BlockSpec(t.shape, lambda s, i: (0,) * t.ndim)
    order = (lambda s, i: (jnp.maximum(i, s), 0, 0), lambda s, i: (i * s, 0, 0))
    return pl.pallas_call(
        edge_kernel,
        grid=(2, 2),
        in_specs=[fixed(u), fixed(e), fixed(m), pl.BlockSpec((1, 16, 48), lambda s, i: (s, 0, 0))]
        + [pl.BlockSpec((1, depth, cols), at) for at in order]
        + [pl.BlockSpec((8, depth, cols), at) for at in order]
        + [tile, tile],
        out_specs=tile,
        out_shape=jax.ShapeDtypeStruct(est.shape, F32),
        scratch_shapes=[pltpu.VMEM((depth, 16, cols), F32)],
        input_output_aliases={9: 0},
        **params(20, 6),
    )(u, e, m, a, above, below, up, down, est, part)


def send(x, axis, d):
    return lax.ppermute(x, AXES, shift_perm(axis, d))


def column_edges(left, right):
    return send(right, "gy", 1), send(left, "gy", -1)


def place():
    gx, gy = lax.axis_index("gx"), lax.axis_index("gy")
    return gx >> 2, gx & 3, gy >> 1, gy & 1


HBM = pl.BlockSpec(memory_space=pltpu.HBM)
ANY = pl.BlockSpec(memory_space=pl.ANY)


def run_copies(pairs, sems):
    copies = [pltpu.make_async_copy(src, dst, sems.at[n]) for n, (src, dst) in enumerate(pairs)]
    for copy in copies:
        copy.start()
    for copy in copies:
        copy.wait()


def copy_call(body, count, shapes, inputs, us, mib=16):
    return pl.pallas_call(
        body,
        in_specs=[HBM] * len(inputs),
        out_specs=[pl.BlockSpec(memory_space=pltpu.VMEM)] * len(shapes),
        out_shape=[jax.ShapeDtypeStruct(s, F32) for s in shapes],
        scratch_shapes=[pltpu.SemaphoreType.DMA((count,))],
        **params(mib, us),
    )(*inputs)


def column_ends(est, after):
    def body(*refs):
        est_ref, left_ref, right_ref = refs[-3:]
        for g in range(left_ref.shape[0]):
            left_ref[g], right_ref[g] = packed([est_ref[8 * g + q] for q in range(8)])

    depth, rows, _ = est.shape
    vmem = pl.BlockSpec(memory_space=pltpu.VMEM)
    return pl.pallas_call(
        body,
        in_specs=[ANY] * len(after) + [vmem],
        out_specs=[vmem] * 2,
        out_shape=[jax.ShapeDtypeStruct((depth // 8, rows, 128), F32)] * 2,
        **params(14, 2),
    )(*after, est)


def row_ends(est):
    def body(est_ref, top_ref, bottom_ref, sems):
        depth, rows, _ = est_ref.shape
        pairs = []
        for out, r in ((top_ref, 0), (bottom_ref, rows - 16)):
            for d in range(0, depth, 16):
                pairs.append((est_ref.at[pl.ds(d, 16), pl.ds(r, 16)], out.at[pl.ds(d, 16)]))
        run_copies(pairs, sems)

    depth, _, cols = est.shape
    return copy_call(body, depth // 8, [(depth, 16, cols)] * 2, (est,), 2, 50)


def join_edges(left, right, dim, n):
    def body(left_ref, right_ref, both_ref, first_ref, last_ref):
        both_ref[:, :, :128] = left_ref[...]
        both_ref[:, :, 128:] = right_ref[...]
        size = both_ref.shape[dim]
        for ref, start in ((first_ref, 0), (last_ref, size - n)):
            at = tuple(pl.ds(start, n) if d == dim else slice(None) for d in range(3))
            ref[...] = both_ref[at]

    shape = (*left.shape[:2], 256)
    part = tuple(n if d == dim else size for d, size in enumerate(shape))
    vmem = pl.BlockSpec(memory_space=pltpu.VMEM)
    return pl.pallas_call(
        body,
        in_specs=[vmem] * 2,
        out_specs=[vmem] * 3,
        out_shape=[jax.ShapeDtypeStruct(t, F32) for t in (shape, part, part)],
        **params(8, 1),
    )(left, right)


def halves_of(measured, rows, after):
    def body(*refs):
        measured_ref, near_ref, far_ref, sems = refs[-4:]
        x, y, z, c = place()
        pairs = []
        for out, core in ((near_ref, c), (far_ref, 1 - c)):
            for k in range(8):
                tx, ty = target_of(x, y, z, core, k)
                pairs.append((measured_ref.at[:, tx * 4 + ty], out.at[k]))
        run_copies(pairs, sems)

    return copy_call(body, 16, [(8, 8, rows, 128)] * 2, (*after, measured.reshape(8, 16, rows, 128)), 2)


def pieces_of(near, far, steps, after):
    def body(*refs):
        near_ref, far_ref, *outs = refs[len(after) : -1]
        sems = refs[-1]
        pairs = []
        for k, out in zip(steps, outs):
            pairs.append((near_ref.at[k], out.at[0]))
            pairs.append((far_ref.at[k], out.at[1]))
        run_copies(pairs, sems)

    shapes = [(2, *near.shape[1:])] * len(steps)
    return copy_call(body, 2 * len(steps), shapes, (*after, near, far), 2)


def diagonal_windows(r_interp, gx, rows):
    total = r_interp.shape[0]
    first = jnp.clip(gx * rows - 64, 0, total - 192)
    band = lax.dynamic_slice(r_interp, (first, 0), (192, total))
    i = lax.broadcasted_iota(jnp.int32, (192, total), 0) + first
    j = lax.broadcasted_iota(jnp.int32, (192, total), 1)
    main = jnp.sum(jnp.where(i == j, band, 0.0), axis=0)
    upper = jnp.sum(jnp.where(i + 1 == j, band, 0.0), axis=0)
    window = lambda v: lax.dynamic_slice(jnp.pad(v, (16, 48)), (gx * rows,), (128,))
    return window(main), window(upper)


def forward(tables, up, estimate, down, both, above, below, after):
    mixed, edge = row_mix(tables[0], up, estimate, down, both, above, below, after)
    return blur(tables[3], tables[4], tables[7], edge, mixed)


def backward(tables, ratio, top, bottom, left, right, estimate, column_edges, row_edges):
    rb, re, ub, ube, zb = tables[1], tables[2], tables[5], tables[6], tables[8]
    up, down = row_edges(top, bottom)
    both, first, last = join_edges(*column_edges(left, right), 0, 2)
    above, below = row_edges(first, last)
    part = own_update(ub, ube, zb, rb, both, ratio, estimate)
    return edge_update(ub, ube, zb, re, above, below, up, down, estimate, part)


def shards(estimate, measured, z_interp, r_interp, psf_z, psf_r, psf_u):
    depth, rows, width = estimate.shape
    gx = lax.axis_index("gx")
    row_edges = lambda top, bottom: (send(bottom, "gx", 1), send(top, "gx", -1))
    top, bottom = row_ends(estimate)
    up, down = row_edges(top, bottom)
    ends = column_ends(estimate, (top,))
    left, right = column_edges(*ends)
    near, far = halves_of(measured, rows, ends[:1])
    far = lax.ppermute(far, AXES, core_swap())
    both, first, last = join_edges(left, right, 1, 16)
    above, below = row_edges(first, last)
    main, upper = diagonal_windows(r_interp, gx, rows)
    tables = make_tables(psf_z, psf_r, psf_u, z_interp, main, upper, rows, width)
    first, second = range(3), range(3, 8)
    ship = lambda parts, steps: [lax.ppermute(p, AXES, piece_perm(k)) for p, k in zip(parts, steps)]
    pieces = ship(pieces_of(near, far, first, (above, below, tables[0], up, down)), first)
    pieces += ship(pieces_of(near, far, second, (tables[0],)), second)
    blurred = forward(tables, up, estimate, down, both, above, below, pieces[:3])
    return backward(tables, *ratio_of(blurred, pieces), estimate, column_edges, row_edges)


def solution(mesh):
    in_specs = (P(None, "gx", "gy"), P("gy", None, "gx"), P(), P(), P(), P(), P())
    out_specs = P(None, "gx", "gy")
    return jax.shard_map(shards, mesh=mesh, in_specs=in_specs, out_specs=out_specs, check_vma=False)
```

```python
import functools

import jax
import jax.numpy as jnp
from jax import lax
from jax.experimental import pallas as pl
from jax.experimental.pallas import tpu as pltpu
from jax.sharding import PartitionSpec as P

background = 0.25
HIGH = lax.Precision.HIGHEST
F32 = jnp.float32
BF = jnp.bfloat16
AXES = ("gx", "gy")
MIB = 1024 * 1024


def split(x):
    hi = x.astype(BF)
    return hi, (x - hi.astype(F32)).astype(BF)


def dot(a, b):
    return jnp.dot(a, b, preferred_element_type=F32)


def thrice(a, b):
    (ah, al), (bh, bl) = a, b
    return dot(jnp.concatenate([ah, ah, al], axis=1), jnp.concatenate([bh, bl, bh], axis=0))


def shift_perm(axis_of, d):
    if axis_of == "gx":
        return [(i * 8 + j, (i + d) * 8 + j) for i in range(16) for j in range(8) if 0 <= i + d < 16]
    return [(i * 8 + j, i * 8 + j + d) for i in range(16) for j in range(8) if 0 <= j + d < 8]


def position(x, y, z, c):
    return ((x % 4) * 4 + y % 4) * 8 + (z % 4) * 2 + c % 2


def core_swap():
    return [(d, d ^ 1) for d in range(128)]


def target_of(x, y, z, c, k):
    k1, k2 = k // 2, k % 2
    side, half = y >> 1, y & 1
    return (x + z + 2 * c + 2 * side + k1) & 3, 2 * (half ^ k2) + c


def source_of(x, y, z, c, k):
    k1, k2 = k // 2, k % 2
    core = y & 1
    return (x - z - 2 * core - 2 * c - k1) & 3, core, (y >> 1) ^ k2


def piece_perm(k):
    pairs = []
    for x in range(4):
        for y in range(4):
            for z in range(4):
                for c in range(2):
                    tx, ty = target_of(x, y, z, c, k)
                    pairs.append((position(x, y, z, c), position(tx, ty, x, y // 2)))
    return pairs


def params(mib, us):
    return dict(
        compiler_params=pltpu.CompilerParams(vmem_limit_bytes=mib * MIB),
        cost_estimate=pl.CostEstimate(flops=0, transcendentals=0, bytes_accessed=us * 3_000_000),
    )


def table_kernel(pz_ref, pr_ref, pu_ref, zi_ref, main_ref, upper_ref, *outs):
    ro_ref, rb_ref, re_ref, uo_ref, uoe_ref, ub_ref, ube_ref, zo_ref, zb_ref = outs

    def grid_of(rows, cols):
        return (
            lax.broadcasted_iota(jnp.int32, (rows, cols), 0),
            lax.broadcasted_iota(jnp.int32, (rows, cols), 1),
        )

    def taps(ref, distance):
        total = jnp.zeros(distance.shape, F32)
        for k in range(32):
            total = jnp.where(distance == k, ref[k], total)
        return total

    def left_table(value):
        h, l = split(value)
        return jnp.concatenate([h, h, l], axis=1)

    def right_table(value):
        h, l = split(value)
        return jnp.concatenate([h, l, h], axis=0)

    rows = rb_ref.shape[0]
    i, j = grid_of(rows, 128)
    main, upper = main_ref[...], upper_ref[...]
    out = taps(pr_ref, j - i) * main + taps(pr_ref, j - 1 - i) * upper
    ro_ref[...] = left_table(out[:, : rows + 32])
    i, j = grid_of(128, 128)
    back = (taps(pr_ref, j - i + 16) * main + taps(pr_ref, j - i + 15) * upper).T[16 : 16 + rows]
    rb_ref[...] = left_table(back[:, 16 : 16 + rows])
    re_ref[0] = left_table(back[:16, :16])
    re_ref[1] = left_table(back[rows - 16 :, rows + 16 : rows + 32])

    width = uo_ref.shape[1]
    i, j = grid_of(width, width)
    uo_ref[...] = right_table(taps(pu_ref, i + 16 - j))
    ub_ref[...] = right_table(taps(pu_ref, j - i + 16))
    a, b = i % 16, j % 16
    same = i // 16 == j // 16
    left = i < 128
    uoe_ref[...] = right_table(jnp.where(same, taps(pu_ref, jnp.where(left, a - b, a - b + 32)), 0.0))
    ube_ref[...] = right_table(jnp.where(same, taps(pu_ref, jnp.where(left, b - a + 32, b - a)), 0.0))

    depth = zi_ref.shape[0]
    i, j = grid_of(depth, depth)
    mix = jnp.dot(taps(pz_ref, j - i + 16), zi_ref[...], precision=HIGH, preferred_element_type=F32)
    zo_ref[...] = left_table(mix)
    zb_ref[...] = left_table(mix.T)


def make_tables(psf_z, psf_r, psf_u, z_interp, main, upper, rows, width):
    depth = z_interp.shape[0]
    shapes = [(rows, 3 * (rows + 32)), (rows, 3 * rows), (2, 16, 48)] + [(3 * width, width)] * 4
    shapes += [(depth, 3 * depth)] * 2
    smem = pl.BlockSpec(memory_space=pltpu.SMEM)
    vmem = pl.BlockSpec(memory_space=pltpu.VMEM)
    return pl.pallas_call(
        table_kernel,
        in_specs=[smem] * 3 + [vmem] * 3,
        out_specs=[vmem] * len(shapes),
        out_shape=[jax.ShapeDtypeStruct(s, BF) for s in shapes],
        **params(8, 3),
    )(psf_z, psf_r, psf_u, z_interp, main[None], upper[None])


def packed(planes):
    lane = lax.broadcasted_iota(jnp.int32, planes[0][:, :128].shape, 1) // 16
    left = right = None
    for q, x in enumerate(planes):
        a, b = x[:, :128], x[:, x.shape[1] - 128 :]
        a = pltpu.roll(a, 16 * q, 1) if q else a
        b = pltpu.roll(b, (16 * q + 16) % 128, 1) if q != 7 else b
        left = a if q == 0 else jnp.where(lane == q, a, left)
        right = b if q == 0 else jnp.where(lane == q, b, right)
    return left, right


def edge_sums(both, table):
    total = across(both, table)
    return total[:, :128], total[:, 128:]


def unpacked(left, right, q):
    lane = lax.broadcasted_iota(jnp.int32, left.shape, 1)
    a = pltpu.roll(left, (128 - 16 * q) % 128, 1) if q else left
    b = pltpu.roll(right, 112 - 16 * q, 1) if q != 7 else right
    return jnp.concatenate([jnp.where(lane < 16, a, 0.0), jnp.where(lane >= 112, b, 0.0)], axis=1)


def across(x, table):
    h, l = split(x)
    return dot(jnp.concatenate([h, h, l], axis=1), table)


def along(table, x):
    h, l = split(x)
    return dot(table, jnp.concatenate([h, l, h], axis=0))


def whole(t):
    return pl.BlockSpec(t.shape, lambda i: (0,) * t.ndim)


def row_kernel(table_ref, own_ref, left_ref, right_ref, *refs):
    up_ref, down_ref, up_edge_ref, down_edge_ref = refs[:4]
    out_ref, edge_ref = refs[-2:]
    table = table_ref[...]
    for z in range(8):
        out_ref[z] = along(table, jnp.concatenate([up_ref[z], own_ref[z], down_ref[z]], axis=0))
    both = jnp.concatenate([left_ref[0], right_ref[0]], axis=1)
    edge_ref[0] = along(table, jnp.concatenate([up_edge_ref[0], both, down_edge_ref[0]], axis=0))


def row_mix(table, up, own, down, left, right, above, below, after):
    depth, rows, cols = own.shape
    groups = depth // 8
    block = lambda d, r: pl.BlockSpec((d, r, cols), lambda i: (i, 0, 0))
    packs = pl.BlockSpec((1, rows, 128), lambda i: (i, 0, 0))
    return pl.pallas_call(
        row_kernel,
        grid=(groups,),
        in_specs=[whole(table), block(8, rows), packs, packs, block(8, 16), block(8, 16), block(1, 16), block(1, 16)]
        + [ANY] * len(after),
        out_specs=[block(8, rows), block(1, rows)],
        out_shape=[jax.ShapeDtypeStruct(own.shape, F32), jax.ShapeDtypeStruct((groups, rows, cols), F32)],
        **params(10, 4),
    )(table, own, left, right, up, down, above, below, *after)


def blur_kernel(u_ref, e_ref, m_ref, edge_ref, x_ref, out_ref):
    depth, rows, cols = x_ref.shape
    total = across(x_ref[...].reshape(depth * rows, cols), u_ref[...]).reshape(depth, rows, cols)
    groups = depth // 8
    left, right = edge_sums(edge_ref[...].reshape(groups * rows, cols), e_ref[...])
    left, right = left.reshape(groups, rows, 128), right.reshape(groups, rows, 128)
    extra = [unpacked(left[g], right[g], q) for g in range(groups) for q in range(8)]
    total = jnp.transpose(total + jnp.stack(extra), (1, 0, 2))
    table = m_ref[...]
    for r in range(rows):
        out_ref[r] = along(table, total[r])


def blur(u, e, m, edge, x):
    depth, rows, cols = x.shape
    block = lambda d, c: pl.BlockSpec((d, 8, c), lambda i: (0, i, 0))
    return pl.pallas_call(
        blur_kernel,
        grid=(rows // 8,),
        in_specs=[whole(u), whole(e), whole(m), block(depth // 8, cols), block(depth, cols)],
        out_specs=pl.BlockSpec((8, depth, cols), lambda i: (i, 0, 0)),
        out_shape=jax.ShapeDtypeStruct((rows, depth, cols), F32),
        **params(14, 8),
    )(u, e, m, edge, x)


def ratio_kernel(blur_ref, *refs):
    pieces, (out_ref, top_ref, bottom_ref, left_ref, right_ref) = refs[:-5], refs[-5:]
    for k, piece in enumerate(pieces):
        pair, core, half = source_of(*place(), k)
        cols = pl.ds(pl.multiple_of(half * 128, 128), 128)
        for part in range(2):
            planes = pl.ds(pl.multiple_of((pair * 2 + (core ^ part)) * 8, 8), 8)
            seen = jnp.transpose(piece[part], (1, 0, 2))
            out_ref[:, planes, cols] = seen / (blur_ref[:, planes, cols] + background)
    top_ref[...] = out_ref[:16]
    bottom_ref[...] = out_ref[out_ref.shape[0] - 16 :]
    for g in range(left_ref.shape[0]):
        left_ref[g], right_ref[g] = packed([out_ref[8 * g + q] for q in range(8)])


def ratio_of(blurred, pieces):
    rows, depth, cols = blurred.shape
    vmem = pl.BlockSpec(memory_space=pltpu.VMEM)
    shapes = [blurred.shape] + [(16, depth, cols)] * 2 + [(rows // 8, depth, 128)] * 2
    return pl.pallas_call(
        ratio_kernel,
        in_specs=[vmem] * (1 + len(pieces)),
        out_specs=[vmem] * 5,
        out_shape=[jax.ShapeDtypeStruct(s, F32) for s in shapes],
        **params(20, 7),
    )(blurred, *pieces)


def spread_tile(ratio, both, u, e, m):
    rows, depth, cols = ratio.shape
    total = across(ratio.reshape(rows * depth, cols), u).reshape(rows, depth, cols)
    left, right = edge_sums(both, e)
    planes = [along(m, total[q] + unpacked(left, right, q)) for q in range(rows)]
    return jnp.transpose(jnp.stack(planes), (1, 0, 2))


def own_kernel(u_ref, e_ref, m_ref, a_ref, both_ref, x_ref, est_ref, out_ref, kept):
    step = pl.program_id(0)
    half = kept.shape[1] // 16

    @pl.when(step < half)
    def _():
        for t in range(2):
            rows = pl.ds(pl.multiple_of(step * 16 + t * 8, 8), 8)
            x = x_ref[8 * t : 8 * t + 8]
            kept[:, rows, :] = spread_tile(x, both_ref[t], u_ref[...], e_ref[...], m_ref[...])

    @pl.when(step >= half)
    def _():
        first = pl.multiple_of((step - half) * 16, 16)
        table = a_ref[...]
        for z in range(16):
            out_ref[z] = est_ref[z] * along(table, kept[first + z])


def own_update(u, e, m, a, both, ratio, est):
    rows, depth, cols = ratio.shape
    half = rows // 16
    early = lambda i: (jnp.minimum(i, half - 1), 0, 0)
    late = lambda i: (jnp.maximum(i - half, 0), 0, 0)
    return pl.pallas_call(
        own_kernel,
        grid=(half + depth // 16,),
        in_specs=[whole(u), whole(e), whole(m), whole(a)]
        + [pl.BlockSpec((2, depth, cols), early), pl.BlockSpec((16, depth, cols), early)]
        + [pl.BlockSpec((16, rows, cols), late)],
        out_specs=pl.BlockSpec((16, rows, cols), late),
        out_shape=jax.ShapeDtypeStruct(est.shape, F32),
        scratch_shapes=[pltpu.VMEM(est.shape, F32)],
        **params(18, 10),
    )(u, e, m, a, both, ratio, est)


def edge_kernel(u_ref, e_ref, m_ref, a_ref, above_ref, below_ref, up_ref, down_ref, est_ref, part_ref, out_ref, kept):
    side = pl.program_id(0)
    for s, x_ref, c_ref in ((0, up_ref, above_ref), (1, down_ref, below_ref)):

        @pl.when(side == s)
        def _(x_ref=x_ref, c_ref=c_ref):
            for t in range(2):
                x = x_ref[8 * t : 8 * t + 8]
                tile = spread_tile(x, c_ref[t], u_ref[...], e_ref[...], m_ref[...])
                kept[:, 8 * t : 8 * t + 8, :] = tile

    table = a_ref[0]
    for z in range(est_ref.shape[0]):
        out_ref[z] = part_ref[z] + est_ref[z] * along(table, kept[z])


def edge_update(u, e, m, a, above, below, up, down, est, part):
    depth, rows, cols = est.shape
    far = rows // 16 - 1
    tile = pl.BlockSpec((depth, 16, cols), lambda s: (0, s * far, 0))
    return pl.pallas_call(
        edge_kernel,
        grid=(2,),
        in_specs=[whole(u), whole(e), whole(m), pl.BlockSpec((1, 16, 48), lambda s: (s, 0, 0))]
        + [whole(t) for t in (above, below, up, down)]
        + [tile, tile],
        out_specs=tile,
        out_shape=jax.ShapeDtypeStruct(est.shape, F32),
        scratch_shapes=[pltpu.VMEM((depth, 16, cols), F32)],
        input_output_aliases={9: 0},
        **params(20, 6),
    )(u, e, m, a, above, below, up, down, est, part)


def send(x, axis, d):
    return lax.ppermute(x, AXES, shift_perm(axis, d))


def column_edges(left, right):
    return send(right, "gy", 1), send(left, "gy", -1)


def place():
    gx, gy = lax.axis_index("gx"), lax.axis_index("gy")
    return gx >> 2, gx & 3, gy >> 1, gy & 1


HBM = pl.BlockSpec(memory_space=pltpu.HBM)
ANY = pl.BlockSpec(memory_space=pl.ANY)


def run_copies(pairs, sems):
    copies = [pltpu.make_async_copy(src, dst, sems.at[n]) for n, (src, dst) in enumerate(pairs)]
    for copy in copies:
        copy.start()
    for copy in copies:
        copy.wait()


def copy_call(body, count, shapes, inputs, us):
    return pl.pallas_call(
        body,
        in_specs=[HBM] * len(inputs),
        out_specs=[pl.BlockSpec(memory_space=pltpu.VMEM)] * len(shapes),
        out_shape=[jax.ShapeDtypeStruct(s, F32) for s in shapes],
        scratch_shapes=[pltpu.SemaphoreType.DMA((count,))],
        **params(16, us),
    )(*inputs)


def column_ends(est, after):
    def body(*refs):
        est_ref, left_ref, right_ref = refs[-3:]
        for g in range(left_ref.shape[0]):
            left_ref[g], right_ref[g] = packed([est_ref[8 * g + q] for q in range(8)])

    depth, rows, _ = est.shape
    vmem = pl.BlockSpec(memory_space=pltpu.VMEM)
    return pl.pallas_call(
        body,
        in_specs=[ANY] * len(after) + [vmem],
        out_specs=[vmem] * 2,
        out_shape=[jax.ShapeDtypeStruct((depth // 8, rows, 128), F32)] * 2,
        **params(14, 2),
    )(*after, est)


def row_ends(est):
    def body(est_ref, top_ref, bottom_ref, sems):
        depth, rows, _ = est_ref.shape
        pairs = []
        for out, r in ((top_ref, 0), (bottom_ref, rows - 16)):
            for d in range(0, depth, 16):
                pairs.append((est_ref.at[pl.ds(d, 16), pl.ds(r, 16)], out.at[pl.ds(d, 16)]))
        run_copies(pairs, sems)

    depth, _, cols = est.shape
    return copy_call(body, depth // 8, [(depth, 16, cols)] * 2, (est,), 2)


def halves_of(measured, rows, after):
    def body(*refs):
        measured_ref, near_ref, far_ref, sems = refs[-4:]
        x, y, z, c = place()
        pairs = []
        for out, core in ((near_ref, c), (far_ref, 1 - c)):
            for k in range(8):
                tx, ty = target_of(x, y, z, core, k)
                pairs.append((measured_ref.at[:, tx * 4 + ty], out.at[k]))
        run_copies(pairs, sems)

    return copy_call(body, 16, [(8, 8, rows, 128)] * 2, (*after, measured.reshape(8, 16, rows, 128)), 2)


def pieces_of(near, far, steps, after):
    def body(*refs):
        near_ref, far_ref, *outs = refs[len(after) : -1]
        sems = refs[-1]
        pairs = []
        for k, out in zip(steps, outs):
            pairs.append((near_ref.at[k], out.at[0]))
            pairs.append((far_ref.at[k], out.at[1]))
        run_copies(pairs, sems)

    shapes = [(2, *near.shape[1:])] * len(steps)
    return copy_call(body, 2 * len(steps), shapes, (*after, near, far), 2)


def diagonal_windows(r_interp, gx, rows):
    total = r_interp.shape[0]
    first = jnp.clip(gx * rows - 64, 0, total - 192)
    band = lax.dynamic_slice(r_interp, (first, 0), (192, total))
    i = lax.broadcasted_iota(jnp.int32, (192, total), 0) + first
    j = lax.broadcasted_iota(jnp.int32, (192, total), 1)
    main = jnp.sum(jnp.where(i == j, band, 0.0), axis=0)
    upper = jnp.sum(jnp.where(i + 1 == j, band, 0.0), axis=0)
    window = lambda v: lax.dynamic_slice(jnp.pad(v, (16, 48)), (gx * rows,), (128,))
    return window(main), window(upper)


def forward(tables, up, estimate, down, left, right, above, below, after):
    mixed, edge = row_mix(tables[0], up, estimate, down, left, right, above, below, after)
    return blur(tables[3], tables[4], tables[7], edge, mixed)


def backward(tables, ratio, top, bottom, left, right, estimate, column_edges, row_edges):
    rb, re, ub, ube, zb = tables[1], tables[2], tables[5], tables[6], tables[8]
    up, down = row_edges(top, bottom)
    both = jnp.concatenate(column_edges(left, right), axis=2)
    above, below = row_edges(both[:2], both[both.shape[0] - 2 :])
    part = own_update(ub, ube, zb, rb, both, ratio, estimate)
    return edge_update(ub, ube, zb, re, above, below, up, down, estimate, part)


def shards(estimate, measured, z_interp, r_interp, psf_z, psf_r, psf_u):
    depth, rows, width = estimate.shape
    gx = lax.axis_index("gx")
    row_edges = lambda top, bottom: (send(bottom, "gx", 1), send(top, "gx", -1))
    top, bottom = row_ends(estimate)
    up, down = row_edges(top, bottom)
    ends = column_ends(estimate, (top,))
    left, right = column_edges(*ends)
    near, far = halves_of(measured, rows, ends[:1])
    far = lax.ppermute(far, AXES, core_swap())
    both = jnp.concatenate([left, right], axis=2)
    above, below = row_edges(both[:, :16], both[:, rows - 16 :])
    main, upper = diagonal_windows(r_interp, gx, rows)
    tables = make_tables(psf_z, psf_r, psf_u, z_interp, main, upper, rows, width)
    first, second = range(3), range(3, 8)
    ship = lambda parts, steps: [lax.ppermute(p, AXES, piece_perm(k)) for p, k in zip(parts, steps)]
    pieces = ship(pieces_of(near, far, first, (above, below, tables[0], up, down)), first)
    pieces += ship(pieces_of(near, far, second, (tables[0],)), second)
    blurred = forward(tables, up, estimate, down, left, right, above, below, pieces[:3])
    return backward(tables, *ratio_of(blurred, pieces), estimate, column_edges, row_edges)


def solution(mesh):
    in_specs = (P(None, "gx", "gy"), P("gy", None, "gx"), P(), P(), P(), P(), P())
    out_specs = P(None, "gx", "gy")
    return jax.shard_map(shards, mesh=mesh, in_specs=in_specs, out_specs=out_specs, check_vma=False)
```
